128 devices in a mesh: tm: 32 (over y, z, core), stn: 4 (over x).
Axes of the slice: x: 4, y: 4, z: 4, core: 2. Of those that a mesh axis runs over, the one named last changes fastest.
Arguments:
- readings: float32 [512, 1536], P('tm', 'stn'), may hold values from -96 to 96
- gap_mask: int32 [512, 1536], P('tm', 'stn'), may hold values 0 or 1
- transfer: float32 [1536, 256], P('stn'), may hold values from -1 to 4
- channel_weight: float32 [1536], P('stn'), may hold values from 0.5 to 4
- pole_site: int32 [1536], P('stn'), may hold values from 0 to 255
- forget: float32 [512, 256], P('tm'), may hold values from 0 to 1, as said below
Outputs:
- filtered: float32 [512, 256], P(('tm', 'stn'))
- smoothed: float32 [512, 256], P(('tm', 'stn'))
The draws below stay inside these ranges and needn't reach their ends.
Inputs may be any that keep to these rules, and one draw needn't show every extreme that they name: `forget`: every factor lies strictly between 0 and 1.
All inputs are finite; a program needn't handle non-finite values. No bound on the sum of `gap_mask` on one device may be relied on, other than what follows from the above.
Results may differ from the reference program's by a relative error of at most 0.0003.
Values sent between devices are 32-bit elements; how exact they have to be, the bound alone decides.
No kernel may reach another device: no remote copies, remote signals or barrier semaphores. Data moves between devices by JAX's collectives and lax.ppermute only.
A program may use at most 192 MiB of HBM per device.

```python
import math
import jax
import jax.numpy as jnp
from jax import lax

P_SIZE = 256
C = 1536
T_DEV = 16
EPOCHS = 512
N_TM = 32


kernel_width = 3.0


def draw_transfer(key, part):
    key = jax.random.fold_in(key, 5)
    keys = jax.random.split(key, 3)
    centre = jax.random.uniform(keys[0], (C, 1), minval=-2.0, maxval=P_SIZE + 2.0)
    pole_axis = jnp.arange(P_SIZE).astype(jnp.float32)[None, :]
    amplitude = 2.0 * jax.random.uniform(keys[1], (C, 1), minval=0.8, maxval=1.2)
    noise = jnp.clip(jax.random.normal(keys[2], (C, P_SIZE)), -4.0, 4.0)
    offset = (pole_axis - centre) / kernel_width
    kernel = jnp.exp(-0.5 * offset * offset)
    scale = 1.0 / jnp.sqrt(jnp.float32(C))
    return (amplitude * kernel + noise * scale).astype(jnp.float32)


def draw_forget(key, part):
    key = jax.random.fold_in(key, 11)
    keys = jax.random.split(key, 9)
    slow_share = 0.5
    slow = jax.random.uniform(keys[0], (P_SIZE,)) < slow_share
    slow_rate = jnp.exp(jax.random.uniform(keys[1], (P_SIZE,), minval=jnp.log(0.08), maxval=jnp.log(0.3))) / EPOCHS
    fast_rate = jnp.exp(jax.random.uniform(keys[2], (P_SIZE,), minval=jnp.log(1.0 / 60.0), maxval=jnp.log(1.0 / 25.0)))
    attenuation_speed = jnp.where(slow, slow_rate, fast_rate)
    segment_multiplier = 2.0 ** (jax.random.uniform(keys[3], (EPOCHS // T_DEV, 1, 1)) - 0.5)
    segment_multiplier = jnp.broadcast_to(segment_multiplier, (EPOCHS // T_DEV, T_DEV, 1)).reshape(EPOCHS, 1)
    prior_stiffness = jax.random.uniform(keys[4], (EPOCHS, P_SIZE), minval=0.6, maxval=1.4)
    positions = jax.random.randint(keys[5], (3,), 0, EPOCHS)
    missing_sample_cases = jax.random.uniform(keys[6], (3,), minval=0.8, maxval=0.9)
    epoch_index = jnp.arange(EPOCHS)
    lightning_occurrences = epoch_index[:, None] == positions[None, :]
    spike_occurrences = jnp.prod(jnp.where(lightning_occurrences, missing_sample_cases[None, :], 1.0), axis=1)
    sharp_drop = jnp.logical_and(jnp.logical_not(slow)[None, :], jax.random.uniform(keys[7], (EPOCHS, P_SIZE)) < 0.25)
    drop_depth = jnp.exp(jax.random.uniform(keys[8], (EPOCHS, P_SIZE), minval=jnp.log(0.03), maxval=jnp.log(0.15)))
    drop_factor = jnp.where(sharp_drop, drop_depth, 1.0)
    multiplier_sequence = jnp.exp(-attenuation_speed[None, :] * segment_multiplier * prior_stiffness) * spike_occurrences[:, None] * drop_factor
    return multiplier_sequence.astype(jnp.float32)


def place_ends(result, rng, smallest, high):
    dims = result.shape
    place = [jax.random.randint(jax.random.fold_in(rng, axis), (), 0, dims[axis]) for axis in range(len(dims))]
    result = result.at[tuple(place)].set(smallest)
    longest = dims.index(max(dims))
    place[longest] = (place[longest] + 1) % dims[longest]
    return result.at[tuple(place)].set(high)


def shard_levels(key, shape, cuts, least, top_value):
    def one(axis_at, blocks):
        steps = jax.random.uniform(jax.random.fold_in(jax.random.fold_in(key, 6), axis_at), (blocks,), jnp.float32, least / len(cuts), top_value / len(cuts))
        return jnp.repeat(jnp.exp(steps), shape[axis_at] // blocks).reshape((-1,) + (1,) * (len(shape) - axis_at - 1))

    factor_of = one(*cuts[0])
    for cut in cuts[1:]:
        factor_of = factor_of * one(*cut)
    return factor_of


def centred(key, dims, spread, reach, cuts=(), kind=jnp.bfloat16):
    factor_of = shard_levels(key, dims, cuts, -0.22, 0.18) if cuts else 1.0
    entries = jax.random.normal(key, dims, jnp.float32) * spread * factor_of
    return jnp.minimum(jnp.maximum(entries, -reach), reach).astype(kind)


def setup_inputs(seed: int = 0) -> dict:
    arg_keys = jax.random.split(jax.random.key(seed), 7)
    readings = centred(arg_keys[0], (EPOCHS, C), 16.0, 96.0, ((0, 32), (1, 4)), jnp.float32)
    gap_mask = place_ends((jax.random.randint(arg_keys[1], (EPOCHS, C), 0, 8) < 7).astype(jnp.int32), jax.random.fold_in(arg_keys[1], 1), 0, 1)
    transfer = draw_transfer(jax.random.fold_in(arg_keys[6], 71), 0)
    channel_weight = jnp.clip(jnp.exp(math.log(4.0) - 2.0794415 * jax.random.uniform(arg_keys[3], (C,), jnp.float32) ** shard_levels(arg_keys[3], (C,), ((0, 4),), -0.2, 0.2)), 0.5, 4.0)
    pole_site = place_ends(jax.random.randint(arg_keys[4], (C,), 0, P_SIZE), jax.random.fold_in(arg_keys[4], 1), 0, P_SIZE - 1).astype(jnp.int32)
    forget = draw_forget(jax.random.fold_in(arg_keys[6], 71), 0)
    return dict(readings=readings, gap_mask=gap_mask, transfer=transfer, channel_weight=channel_weight, pole_site=pole_site, forget=forget)


near_gain = 0.5
ridge = 1.0

def design_matrix(transfer, pole_site):
    pole_index = lax.broadcasted_iota(jnp.int32, transfer.shape, 1)
    return transfer + near_gain * (pole_index == pole_site[:, None]).astype(jnp.float32)

def block_terms(design, readings, gap_mask, channel_weight):
    weighted = gap_mask.astype(jnp.float32) * channel_weight[None, :]
    scaled = weighted[:, :, None] * design[None, :, :]
    gram_stack = jnp.einsum('tcp,cq->tpq', scaled, design, precision=lax.Precision.HIGHEST)
    info_stack = jnp.dot(weighted * readings, design, precision=lax.Precision.HIGHEST)
    return (gram_stack, info_stack)

def solve_system(matrix, vector):
    factor = jnp.linalg.cholesky(matrix)
    return jax.scipy.linalg.cho_solve((factor, True), vector[:, None])[:, 0]

def reference(readings, gap_mask, transfer, channel_weight, pole_site, forget):
    design = design_matrix(transfer, pole_site)
    state_size = transfer.shape[1]
    channels = transfer.shape[0]
    identity_matrix = jnp.eye(state_size, dtype=jnp.float32)
    reading_blocks = readings.reshape(N_TM, T_DEV, channels)
    mask_blocks = gap_mask.reshape(N_TM, T_DEV, channels)
    forget_blocks = forget.reshape(N_TM, T_DEV, state_size)
    zero_gram = jnp.zeros((state_size, state_size), jnp.float32)
    zero_vec = jnp.zeros((state_size,), jnp.float32)

    def fold_back(state, element):
        back_gram, back_vec = state
        multiplier_sequence, gram_now, info_now = element
        new_gram = multiplier_sequence[:, None] * (back_gram + gram_now) * multiplier_sequence[None, :]
        new_vec = multiplier_sequence * (back_vec + info_now)
        return ((new_gram, new_vec), state)

    def later_pass(running, block):
        rows, masks, multiplier_sequence = block
        gram_stack, info_stack = block_terms(design, rows, masks, channel_weight)
        final, _ = lax.scan(fold_back, running, (multiplier_sequence, gram_stack, info_stack), reverse=True)
        return (final, running)
    _, entering = lax.scan(later_pass, (zero_gram, zero_vec), (reading_blocks, mask_blocks, forget_blocks), reverse=True)

    def ahead_step(state, element):
        ahead_gram, ahead_vec = state
        multiplier_sequence, gram_now, info_now, back_gram, back_vec = element
        ahead_gram = multiplier_sequence[:, None] * ahead_gram * multiplier_sequence[None, :] + gram_now
        ahead_vec = multiplier_sequence * ahead_vec + info_now
        filt_row = solve_system(ridge * identity_matrix + ahead_gram, ahead_vec)
        smooth_row = solve_system(ridge * identity_matrix + ahead_gram + back_gram, ahead_vec + back_vec)
        return ((ahead_gram, ahead_vec), (filt_row, smooth_row))

    def earlier_pass(running, block):
        rows, masks, multiplier_sequence, enter_gram, enter_vec = block
        gram_stack, info_stack = block_terms(design, rows, masks, channel_weight)
        _, (back_grams, back_vecs) = lax.scan(fold_back, (enter_gram, enter_vec), (multiplier_sequence, gram_stack, info_stack), reverse=True)
        final, outputs = lax.scan(ahead_step, running, (multiplier_sequence, gram_stack, info_stack, back_grams, back_vecs))
        return (final, outputs)
    _, (filt_rows, smooth_rows) = lax.scan(earlier_pass, (zero_gram, zero_vec), (reading_blocks, mask_blocks, forget_blocks, entering[0], entering[1]))
    return (filt_rows.reshape(N_TM * T_DEV, state_size), smooth_rows.reshape(N_TM * T_DEV, state_size))
```

```python
import jax
import jax.numpy as jnp
from jax import lax
from jax.experimental import pallas as pl
from jax.experimental.pallas import tpu as pltpu
from jax.sharding import PartitionSpec as P

near_gain = 0.5
ridge = 1.0
VMEM = 48 << 20
PANEL = 32
SUB = 8
f32 = jnp.float32
bf16 = jnp.bfloat16


def split3(x):
    high = x.astype(bf16)
    rest = x - high.astype(f32)
    mid = rest.astype(bf16)
    low = (rest - mid.astype(f32)).astype(bf16)
    return high, mid, low


def inverse(x):
    r = pl.reciprocal(x, approx=True)
    r = r * (2.0 - x * r)
    return r * (2.0 - x * r)


def spread(rows, lane):
    n = rows.shape[0]
    flat = rows.reshape(n * 8, 128)
    index = jnp.full((n * 8, 128), lane, jnp.int32)
    return jnp.take_along_axis(flat, index, axis=1).reshape(n, 8, 128)


def panel_solve(parts, lane0):
    parts = [[p[SUB * s : SUB * s + SUB] for s in range(PANEL // SUB)] for p in parts]
    for s in range(PANEL // SUB):
        lane = lane0 + SUB * s
        block = parts[0][s]
        e = {}
        for i in range(SUB):
            for j in range(i, SUB):
                e[i, j] = spread(block[i : i + 1], lane + j)[0]
        mult = {}
        for q in range(PANEL // SUB):
            if q != s:
                mult[q] = [spread(parts[0][q], lane + j) for j in range(SUB)]
        low = {}
        dinv = []
        for j in range(SUB):
            d = inverse(e[j, j])
            dinv.append(d)
            for i in range(j + 1, SUB):
                low[i, j] = e[j, i] * d
            for i in range(j + 1, SUB):
                for c in range(i, SUB):
                    e[i, c] = e[i, c] - low[i, j] * e[j, c]
        for p in parts:
            rows = [p[s][i] for i in range(SUB)]
            for j in range(SUB):
                for i in range(j + 1, SUB):
                    rows[i] = rows[i] - low[i, j] * rows[j]
            rows = [rows[j] * dinv[j] for j in range(SUB)]
            for j in range(SUB - 1, 0, -1):
                for i in range(j):
                    rows[i] = rows[i] - low[j, i] * rows[j]
            p[s] = jnp.stack(rows)
            for q in range(PANEL // SUB):
                if q != s:
                    new = p[q]
                    for j in range(SUB):
                        new = new - mult[q][j] * rows[j][None]
                    p[q] = new
    return [jnp.concatenate(p, axis=0) for p in parts]


def solve_in_place(t_ref, b_ref, pn_ref, px_ref, bx_ref):
    def step(k, half):
        row0 = k * PANEL
        lane0 = row0 - 128 * half
        halves = [half] if half else [0, 1]

        def load(h):
            return jnp.stack([t_ref[h, pl.ds(row0 + i, 8, stride=256), :] for i in range(PANEL)])

        original = [load(h) for h in halves]
        vec = b_ref[half]
        right = jnp.stack([spread(vec[None], lane0 + i)[0] for i in range(PANEL)])
        done = panel_solve(original + [right], lane0)
        for h, p in zip(halves, done):
            px_ref[h, pl.ds(row0, PANEL)] = p
            for i in range(PANEL):
                pn_ref[h, pl.ds(i, 8, stride=PANEL), :] = p[i]
        bx_ref[pl.ds(row0, PANEL)] = done[-1]
        for h in halves:
            acc = b_ref[h]
            for i in range(PANEL):
                acc = acc - t_ref[h, pl.ds(row0 + i, 8, stride=256), :] * done[-1][i]
            b_ref[h] = acc
        for m in range(8):
            def cat(get, pick):
                pieces = split3(get)
                return jnp.concatenate([pieces[c] for c in pick], axis=0)

            left = [cat(t_ref[h, pl.ds(m * 256 + row0, PANEL), :], (0, 0, 0, 1, 1, 2)) for h in halves]
            rgt = [cat(pn_ref[h, pl.ds(m * PANEL, PANEL), :], (0, 1, 2, 0, 1, 0)) for h in halves]

            def dot(a, b):
                return lax.dot_general(a, b, (((0,), (0,)), ((), ())), preferred_element_type=f32)

            top = pl.ds(m * 256, 128)
            bottom = pl.ds(m * 256 + 128, 128)
            if half:
                t_ref[1, bottom, :] = t_ref[1, bottom, :] - dot(left[0], rgt[0])
            else:
                t_ref[0, top, :] = t_ref[0, top, :] - dot(left[0], rgt[0])
                t_ref[1, top, :] = t_ref[1, top, :] - dot(left[0], rgt[1])
                t_ref[1, bottom, :] = t_ref[1, bottom, :] - dot(left[1], rgt[1])

    @pl.loop(0, 4)
    def _(k):
        step(k, 0)

    @pl.loop(4, 8)
    def _(k):
        step(k, 1)

    lanes = lax.broadcasted_iota(jnp.int32, (PANEL, 8, 128), 2)
    order = lax.broadcasted_iota(jnp.int32, (PANEL, 8, 128), 0)
    zero = jnp.zeros((8, 128), f32)

    def back(k, x_halves, half):
        row0 = k * PANEL
        total = sum(px_ref[h, pl.ds(row0, PANEL)] * x_halves[h][None] for h in range(half, 2))
        x_new = bx_ref[pl.ds(row0, PANEL)] - jnp.sum(total, axis=2, keepdims=True)
        keep = jnp.where(lanes == order + (row0 - 128 * half), x_new, 0.0)
        add = jnp.sum(keep, axis=0)
        return (x_halves[0] + add, x_halves[1]) if half == 0 else (x_halves[0], x_halves[1] + add)

    x = lax.fori_loop(0, 4, lambda n, x: back(7 - n, x, 1), (zero, zero))
    x = lax.fori_loop(0, 4, lambda n, x: back(3 - n, x, 0), x)
    return x


SOLVE_SCRATCH = [
    pltpu.VMEM((2, 8 * 256, 128), f32),
    pltpu.VMEM((2, 8, 128), f32),
    pltpu.VMEM((2, 8 * PANEL, 128), f32),
    pltpu.VMEM((2, 256, 8, 128), f32),
    pltpu.VMEM((256, 8, 128), f32),
]


def scalars():
    tm = lax.axis_index("tm")
    stn = lax.axis_index("stn")
    return jnp.stack([lax.rem(tm, 2), stn, tm * 4 + stn]).astype(jnp.int32)


def column(row):
    return jnp.broadcast_to(row, (128, 128)).T


def quarter_rows(rows, quarter):
    out = rows[0:4]
    for q in range(1, 4):
        out = jnp.where(quarter == q, rows[4 * q : 4 * q + 4], out)
    return out


def prepare_kernel(at, transfer, site, weight, mask, readings, design, own, msg1, msg2, msg3):
    core, stn = at[0], at[1]
    for c in range(3):
        rows = pl.ds(128 * c, 128)
        root = column(jnp.sqrt(weight[:, 128 * c : 128 * c + 128]))
        where_site = column(site[:, 128 * c : 128 * c + 128].astype(f32))
        for h in range(2):
            pole = lax.broadcasted_iota(jnp.int32, (128, 128), 1).astype(f32) + 128.0 * h
            near = jnp.where(pole == where_site, near_gain, 0.0)
            design[rows, 128 * h : 128 * h + 128] = (transfer[rows, 128 * h : 128 * h + 128] + near) * root
    half = design[pl.ds(192 * core, 192), :]
    masks = mask[...].astype(f32)
    scaled = masks * jnp.sqrt(weight[...]) * readings[...]

    def piece(quarter):
        return jnp.concatenate([quarter_rows(masks, quarter), quarter_rows(scaled, quarter)], axis=0)

    own[...] = piece(stn)
    for o, msg in enumerate((msg1, msg2, msg3)):
        rows = piece(lax.rem(stn + (o + 1), 4))
        msg[0:192, :] = half
        msg[192:200, :] = rows[:, 0:256]
        msg[200:208, 0:128] = rows[:, 256:384]
        msg[200:208, 128:256] = jnp.zeros((8, 128), f32)


def decay(forget, quarter):
    rows = quarter_rows(forget, quarter)
    row = [[rows[t : t + 1, 128 * h : 128 * h + 128] for h in range(2)] for t in range(4)]
    col = [[column(row[t][h]) for h in range(2)] for t in range(4)]
    return row, col


BLOCKS = ((0, 0), (0, 1), (1, 1))


def gram_kernel(at, design, own, got1, got2, got3, oth1, oth2, oth3, forget, gram, info, msg, block):
    core, stn = at[0], at[1]
    for n, (got, oth) in enumerate(((design, None), (got1, oth1), (got2, oth2), (got3, oth3))):
        if n == 0:
            x = design[...]
            rows = own[...]
        else:
            block[pl.ds(192 * core, 192), :] = got[0:192, :]
            block[pl.ds(192 * (1 - core), 192), :] = oth[0:192, :]
            x = block[...]
            rows = jnp.concatenate([got[192:200, :], got[200:208, 0:128]], axis=1)
        high, mid, low = split3(x)
        thigh, tmid, tlow = split3(x.T)
        part = jnp.dot(rows, x, precision=lax.Precision.HIGHEST, preferred_element_type=f32)
        if n == 0:
            info[...] = part
        else:
            info[...] += part
        for t in range(4):
            keep = rows[t : t + 1, :].astype(bf16)
            a, b, c = thigh * keep, tmid * keep, tlow * keep

            def dot(p, q):
                return jnp.dot(p, q, preferred_element_type=f32)

            total = dot(c, high) + dot(a, low) + dot(b, mid) + dot(b, high) + dot(a, mid) + dot(a, high)
            if n == 0:
                gram[t] = total
            else:
                gram[t] += total
    row, col = decay(forget[...], stn)
    ahead, behind = {}, {}
    for i, j in BLOCKS:
        rs, cs = slice(128 * i, 128 * i + 128), slice(128 * j, 128 * j + 128)
        g = [gram[t, rs, cs] for t in range(4)]
        f = [col[t][i] * row[t][j] for t in range(4)]
        acc = g[0]
        for t in range(1, 4):
            acc = f[t] * acc + g[t]
        ahead[i, j] = acc
        acc = f[3] * g[3]
        for t in (2, 1, 0):
            acc = f[t] * (acc + g[t])
        behind[i, j] = acc
    lanes = lax.broadcasted_iota(jnp.int32, (128, 128), 1)
    rows_at = lax.broadcasted_iota(jnp.int32, (128, 128), 0)
    eye = lanes == rows_at
    lower = lanes <= rows_at
    vec_f, vec_b, gains = [], [], []
    for h in range(2):
        v = [info[4 + t : 5 + t, 128 * h : 128 * h + 128] for t in range(4)]
        f = [row[t][h] for t in range(4)]
        acc = v[0]
        for t in range(1, 4):
            acc = f[t] * acc + v[t]
        vec_f.append(acc)
        acc = f[3] * v[3]
        for t in (2, 1, 0):
            acc = f[t] * (acc + v[t])
        vec_b.append(acc)
        gains.append(f[0] * f[1] * f[2] * f[3])

    def down(values):
        return jnp.sum(jnp.where(eye, values, 0.0), axis=1, keepdims=True)

    extras = [ahead[1, 1], behind[1, 1], vec_f[0], vec_f[1], vec_b[0], vec_b[1]]
    last = jnp.zeros((128, 128), f32)
    for n, e in enumerate(extras):
        last = jnp.where(lanes == n, down(e), last)
    msg[:, 0:128] = jnp.where(lower, ahead[0, 0], ahead[1, 1])
    msg[:, 128:256] = ahead[0, 1]
    msg[:, 256:384] = jnp.where(lower, behind[0, 0], behind[1, 1])
    msg[:, 384:512] = behind[0, 1]
    msg[:, 512:640] = jnp.broadcast_to(gains[0], (128, 128))
    msg[:, 640:768] = jnp.broadcast_to(gains[1], (128, 128))
    msg[:, 768:896] = last


def shifted(x, n, fill, up):
    edge = jnp.full((n, x.shape[1]), fill, f32)
    if up:
        return jnp.concatenate([x[n:], edge], axis=0)
    return jnp.concatenate([edge, x[:-n]], axis=0)


def running(gain, value, up):
    n = 1
    while n < 128:
        value = value + gain * shifted(value, n, 0.0, up)
        if n < 64:
            gain = gain * shifted(gain, n, 1.0, up)
        n *= 2
    return shifted(value, 1, 0.0, up)


def carry_kernel(at, got, out):
    place = at[2]
    lanes = lax.broadcasted_iota(jnp.int32, (128, 128), 1)
    low, high = got[:, 512:640], got[:, 640:768]
    here = lanes == place
    at_low = jnp.sum(jnp.where(here, low, 0.0), axis=1, keepdims=True)
    at_high = jnp.sum(jnp.where(here, high, 0.0), axis=1, keepdims=True)
    extra = jnp.where(lanes < 2, at_high * at_high, jnp.where((lanes == 2) | (lanes == 4), at_low, at_high))
    gain = [jnp.where(lanes <= place, at_low * low, at_high * high), at_low * high, extra]
    last = got[:, 768:896]
    enter = [running(g, v, False) for g, v in zip(gain, (got[:, 0:128], got[:, 128:256], last))]
    leave = [running(g, v, True) for g, v in zip(gain, (got[:, 256:384], got[:, 384:512], last))]
    out[:, 0:128] = enter[0]
    out[:, 128:256] = enter[1]
    out[:, 256:384] = leave[0]
    out[:, 384:512] = leave[1]
    ahead_lane = (lanes == 0) | (lanes == 2) | (lanes == 3)
    out[:, 512:640] = jnp.where(ahead_lane, enter[2], leave[2])


def final_kernel(at, got, gram, info, forget, filtered, smoothed, t_ref, b_ref, pn_ref, px_ref, bx_ref):
    stn = at[1]
    lanes = lax.broadcasted_iota(jnp.int32, (128, 128), 1)
    rows_at = lax.broadcasted_iota(jnp.int32, (128, 128), 0)
    eye = lanes == rows_at
    lower = lanes <= rows_at
    unit = jnp.where(eye, ridge, 0.0)
    last = got[:, 512:640]

    def lane_column(n):
        return jnp.sum(jnp.where(lanes == n, last, 0.0), axis=1, keepdims=True)

    def to_row(col):
        return jnp.sum(jnp.where(eye, col, 0.0), axis=0, keepdims=True)

    def unpack(base, diagonal):
        packed = got[:, base : base + 128]
        turned = packed.T
        first = jnp.where(lower, packed, turned)
        second = jnp.where(eye, diagonal, jnp.where(lower, turned, packed))
        return {(0, 0): first, (0, 1): got[:, base + 128 : base + 256], (1, 1): second}

    ahead = unpack(0, lane_column(0))
    behind = unpack(256, lane_column(1))
    row, col = decay(forget[...], stn)
    for i, j in BLOCKS:
        rs, cs = slice(128 * i, 128 * i + 128), slice(128 * j, 128 * j + 128)
        f = [col[t][i] * row[t][j] for t in range(4)]
        acc = ahead[i, j]
        held = []
        for t in range(4):
            acc = f[t] * acc + gram[t, rs, cs]
            full = acc + unit if i == j else acc
            held.append(full)
            t_ref[j, 256 * t + 128 * i : 256 * t + 128 * i + 128, :] = full
        acc = behind[i, j]
        for t in (3, 2, 1, 0):
            at_row = 256 * (4 + t) + 128 * i
            t_ref[j, at_row : at_row + 128, :] = held[t] + acc
            if t:
                acc = f[t] * (acc + gram[t, rs, cs])
    for h in range(2):
        vec = to_row(lane_column(2 + h))
        held = []
        for t in range(4):
            vec = row[t][h] * vec + info[4 + t : 5 + t, 128 * h : 128 * h + 128]
            held.append(vec)
        vec = to_row(lane_column(4 + h))
        both = [None] * 4
        for t in (3, 2, 1, 0):
            both[t] = held[t] + vec
            if t:
                vec = row[t][h] * (vec + info[4 + t : 5 + t, 128 * h : 128 * h + 128])
        b_ref[h] = jnp.concatenate(held + both, axis=0)
    x = solve_in_place(t_ref, b_ref, pn_ref, px_ref, bx_ref)
    for h in range(2):
        filtered[:, 128 * h : 128 * h + 128] = x[h][0:4]
        smoothed[:, 128 * h : 128 * h + 128] = x[h][4:8]


def call(kernel, outs, scratch, operands):
    return pl.pallas_call(
        kernel,
        out_shape=[jax.ShapeDtypeStruct(s, f32) for s in outs],
        in_specs=[pl.BlockSpec(memory_space=pltpu.SMEM)]
        + [pl.BlockSpec(memory_space=pltpu.VMEM)] * (len(operands) - 1),
        out_specs=[pl.BlockSpec(memory_space=pltpu.VMEM)] * len(outs),
        scratch_shapes=scratch,
        compiler_params=pltpu.CompilerParams(vmem_limit_bytes=VMEM),
    )(*operands)


def ring(count, shift):
    return [(i, (i + shift) % count) for i in range(count)]


def body(readings, gap_mask, transfer, channel_weight, pole_site, forget):
    at = scalars()
    with jax.named_scope("design"):
        design, own, *msgs = call(
            prepare_kernel,
            [(384, 256), (8, 384)] + [(208, 256)] * 3,
            [],
            (at, transfer, pole_site[None], channel_weight[None], gap_mask, readings),
        )
    with jax.named_scope("gather"):
        got = [lax.ppermute(m, "stn", ring(4, o + 1)) for o, m in enumerate(msgs)]
        swap = [(i, i ^ 1) for i in range(32)]
        other = [lax.ppermute(g, "tm", swap) for g in got]
    with jax.named_scope("gram"):
        gram, info, totals = call(
            gram_kernel,
            [(4, 256, 256), (8, 256), (128, 896)],
            [pltpu.VMEM((384, 256), f32)],
            (at, design, own, *got, *other, forget),
        )
    with jax.named_scope("carry"):
        mine = lax.all_to_all(totals, ("tm", "stn"), 0, 0, tiled=True)
        (entering,) = call(carry_kernel, [(128, 640)], [], (at, mine))
        entering = lax.all_to_all(entering, ("tm", "stn"), 0, 0, tiled=True)
    with jax.named_scope("solve"):
        filtered, smoothed = call(
            final_kernel, [(4, 256)] * 2, SOLVE_SCRATCH, (at, entering, gram, info, forget)
        )
    return (filtered, smoothed)


def solution(mesh):
    in_specs = (P("tm", "stn"), P("tm", "stn"), P("stn", None), P("stn"), P("stn"), P("tm", None))
    out_specs = (P(("tm", "stn"), None), P(("tm", "stn"), None))
    return jax.shard_map(body, mesh=mesh, in_specs=in_specs, out_specs=out_specs, check_vma=False)
```

```python
import jax
import jax.numpy as jnp
from jax import lax
from jax.experimental import pallas as pl
from jax.experimental.pallas import tpu as pltpu
from jax.sharding import PartitionSpec as P

near_gain = 0.5
ridge = 1.0
VMEM = 48 << 20
PANEL = 16
SUB = 16
PITCH = PANEL + 1
STEPS = 128 // PANEL
f32 = jnp.float32
bf16 = jnp.bfloat16


def split3(x):
    high = x.astype(bf16)
    rest = x - high.astype(f32)
    mid = rest.astype(bf16)
    low = (rest - mid.astype(f32)).astype(bf16)
    return high, mid, low


def inverse(x):
    return pl.reciprocal(x, approx=True)


def spread(rows, lane):
    n = rows.shape[0]
    flat = rows.reshape(n * 8, 128)
    index = jnp.full((n * 8, 128), lane, jnp.int32)
    return jnp.take_along_axis(flat, index, axis=1).reshape(n, 8, 128)


def panel_solve(parts, lane0):
    parts = [[p[SUB * s : SUB * s + SUB] for s in range(PANEL // SUB)] for p in parts]
    for s in range(PANEL // SUB):
        lane = lane0 + SUB * s
        block = parts[0][s]
        e = {}
        for i in range(SUB):
            for j in range(i, SUB):
                e[i, j] = spread(block[i : i + 1], lane + j)[0]
        mult = {}
        for q in range(PANEL // SUB):
            if q != s:
                mult[q] = [spread(parts[0][q], lane + j) for j in range(SUB)]
        low = {}
        dinv = []
        for j in range(SUB):
            d = inverse(e[j, j])
            dinv.append(d)
            for i in range(j + 1, SUB):
                low[i, j] = e[j, i] * d
            for i in range(j + 1, SUB):
                for c in range(i, SUB):
                    e[i, c] = e[i, c] - low[i, j] * e[j, c]
        for p in parts:
            rows = [p[s][i] for i in range(SUB)]
            for j in range(SUB):
                for i in range(j + 1, SUB):
                    rows[i] = rows[i] - low[i, j] * rows[j]
            rows = [rows[j] * dinv[j] for j in range(SUB)]
            for j in range(SUB - 1, 0, -1):
                for i in range(j):
                    rows[i] = rows[i] - low[j, i] * rows[j]
            p[s] = jnp.stack(rows)
            for q in range(PANEL // SUB):
                if q != s:
                    new = p[q]
                    for j in range(SUB):
                        new = new - mult[q][j] * rows[j][None]
                    p[q] = new
    return [jnp.concatenate(p, axis=0) for p in parts]


def solve_in_place(t_ref, b_ref, pan_ref, pn_ref, px_ref, bx_ref):
    def step(k, half):
        row0 = k * PANEL
        lane0 = row0 - 128 * half
        halves = [half] if half else [0, 1]

        for h in halves:
            for m in range(8):
                pan_ref[h, m * PITCH : m * PITCH + PANEL, :] = t_ref[h, pl.ds(m * 256 + row0, PANEL), :]

        def load(h):
            return jnp.stack([pan_ref[h, pl.ds(i, 8, stride=PITCH), :] for i in range(PANEL)])

        original = [load(h) for h in halves]
        vec = b_ref[half]
        right = jnp.stack([spread(vec[None], lane0 + i)[0] for i in range(PANEL)])
        done = panel_solve(original + [right], lane0)
        for h, p in zip(halves, done):
            px_ref[h, pl.ds(row0, PANEL)] = p
            for i in range(PANEL):
                pn_ref[h, pl.ds(i, 8, stride=PITCH), :] = p[i]
        bx_ref[pl.ds(row0, PANEL)] = done[-1]
        for n, h in enumerate(halves):
            b_ref[h] = b_ref[h] - jnp.sum(original[n] * done[-1], axis=0)
        def cat(x, pick):
            pieces = split3(x)
            return jnp.concatenate([pieces[c] for c in pick], axis=0)

        def dot(a, b):
            return lax.dot_general(a, b, (((0,), (0,)), ((), ())), preferred_element_type=f32)

        left = [[cat(t_ref[h, pl.ds(m * 256 + row0, PANEL), :], (0, 0, 0, 1, 1, 2)) for h in halves] for m in range(8)]
        rgt = [[cat(pn_ref[h, m * PITCH : m * PITCH + PANEL, :], (0, 1, 2, 0, 1, 0)) for h in halves] for m in range(8)]
        for m in range(8):
            top = pl.ds(m * 256, 128)
            bottom = pl.ds(m * 256 + 128, 128)
            if half:
                t_ref[1, bottom, :] = t_ref[1, bottom, :] - dot(left[m][0], rgt[m][0])
            else:
                t_ref[0, top, :] = t_ref[0, top, :] - dot(left[m][0], rgt[m][0])
                t_ref[1, top, :] = t_ref[1, top, :] - dot(left[m][0], rgt[m][1])
                t_ref[1, bottom, :] = t_ref[1, bottom, :] - dot(left[m][1], rgt[m][1])

    @pl.loop(0, STEPS)
    def _(k):
        step(k, 0)

    @pl.loop(STEPS, 2 * STEPS)
    def _(k):
        step(k, 1)

    lanes = lax.broadcasted_iota(jnp.int32, (PANEL, 8, 128), 2)
    order = lax.broadcasted_iota(jnp.int32, (PANEL, 8, 128), 0)
    zero = jnp.zeros((8, 128), f32)

    def back(k, x_halves, half):
        row0 = k * PANEL
        total = sum(px_ref[h, pl.ds(row0, PANEL)] * x_halves[h][None] for h in range(half, 2))
        x_new = bx_ref[pl.ds(row0, PANEL)] - jnp.sum(total, axis=2, keepdims=True)
        keep = jnp.where(lanes == order + (row0 - 128 * half), x_new, 0.0)
        add = jnp.sum(keep, axis=0)
        return (x_halves[0] + add, x_halves[1]) if half == 0 else (x_halves[0], x_halves[1] + add)

    x = lax.fori_loop(0, STEPS, lambda n, x: back(2 * STEPS - 1 - n, x, 1), (zero, zero))
    x = lax.fori_loop(0, STEPS, lambda n, x: back(STEPS - 1 - n, x, 0), x)
    return x


SOLVE_SCRATCH = [
    pltpu.VMEM((2, 8 * 256, 128), f32),
    pltpu.VMEM((2, 8, 128), f32),
    pltpu.VMEM((2, 8 * PITCH, 128), f32),
    pltpu.VMEM((2, 8 * PITCH, 128), f32),
    pltpu.VMEM((2, 256, 8, 128), f32),
    pltpu.VMEM((256, 8, 128), f32),
]


def scalars():
    tm = lax.axis_index("tm")
    stn = lax.axis_index("stn")
    return jnp.stack([lax.rem(tm, 2), stn, tm * 4 + stn]).astype(jnp.int32)


def column(row):
    return jnp.broadcast_to(row, (128, 128)).T


def quarter_rows(rows, quarter):
    out = rows[0:4]
    for q in range(1, 4):
        out = jnp.where(quarter == q, rows[4 * q : 4 * q + 4], out)
    return out


def prepare_kernel(at, transfer, site, weight, mask, readings, design, own, msg1, msg2, msg3):
    core, stn = at[0], at[1]
    for c in range(3):
        rows = pl.ds(128 * c, 128)
        root = column(jnp.sqrt(weight[:, 128 * c : 128 * c + 128]))
        where_site = column(site[:, 128 * c : 128 * c + 128].astype(f32))
        for h in range(2):
            pole = lax.broadcasted_iota(jnp.int32, (128, 128), 1).astype(f32) + 128.0 * h
            near = jnp.where(pole == where_site, near_gain, 0.0)
            design[rows, 128 * h : 128 * h + 128] = (transfer[rows, 128 * h : 128 * h + 128] + near) * root
    half = design[pl.ds(192 * core, 192), :]
    masks = mask[...].astype(f32)
    scaled = masks * jnp.sqrt(weight[...]) * readings[...]

    def piece(quarter):
        return jnp.concatenate([quarter_rows(masks, quarter), quarter_rows(scaled, quarter)], axis=0)

    own[...] = piece(stn)
    for o, msg in enumerate((msg1, msg2, msg3)):
        rows = piece(lax.rem(stn + (o + 1), 4))
        msg[0:192, :] = half
        msg[192:200, :] = rows[:, 0:256]
        msg[200:208, 0:128] = rows[:, 256:384]
        msg[200:208, 128:256] = jnp.zeros((8, 128), f32)


def decay(forget, quarter):
    rows = quarter_rows(forget, quarter)
    row = [[rows[t : t + 1, 128 * h : 128 * h + 128] for h in range(2)] for t in range(4)]
    col = [[column(row[t][h]) for h in range(2)] for t in range(4)]
    return row, col


BLOCKS = ((0, 0), (0, 1), (1, 1))


def add_block(x, rows, even, odd, info, first):
    high, mid, low = split3(x)
    turned = x.T
    thigh = turned.astype(bf16)
    tmid = (turned - thigh.astype(f32)).astype(bf16)

    def dot(p, q):
        return jnp.dot(p, q, preferred_element_type=f32)

    part = jnp.dot(rows, x, precision=lax.Precision.HIGHEST, preferred_element_type=f32)
    info[...] = part if first else info[...] + part
    for t in range(4):
        keep = rows[t : t + 1, :].astype(bf16)
        a, b = thigh * keep, tmid * keep
        same = dot(b, mid) + dot(a, high)
        cross = dot(a, low) + dot(a, mid)
        even[t] = same if first else even[t] + same
        odd[t] = cross if first else odd[t] + cross


def gram_block(even, odd, t, n):
    i, j = BLOCKS[n]
    rs, cs = slice(128 * i, 128 * i + 128), slice(128 * j, 128 * j + 128)
    return even[t, rs, cs] + (odd[t, rs, cs] + odd[t, cs, rs].T)


def own_gram_kernel(at, design, own, gram, info, even, odd):
    add_block(design[...], own[...], even, odd, info, True)
    for t in range(4):
        for n in range(3):
            gram[t, n] = gram_block(even, odd, t, n)


def gram_kernel(at, gram_in, info_in, got1, got2, got3, oth1, oth2, oth3, forget, gram, info, msg, block, even, odd):
    core, stn = at[0], at[1]
    for n, (got, oth) in enumerate(((got1, oth1), (got3, oth3), (got2, oth2))):
        block[n, pl.ds(192 * core, 192), :] = got[0:192, :]
        block[n, pl.ds(192 * (1 - core), 192), :] = oth[0:192, :]
        rows = jnp.concatenate([got[192:200, :], got[200:208, 0:128]], axis=1)
        add_block(block[n], rows, even, odd, info, n == 0)
    info[...] += info_in[...]
    for t in range(4):
        for n in range(3):
            gram[t, n] = gram_in[t, n] + gram_block(even, odd, t, n)
    row, col = decay(forget[...], stn)
    ahead, behind = {}, {}
    for n, (i, j) in enumerate(BLOCKS):
        g = [gram[t, n] for t in range(4)]
        f = [col[t][i] * row[t][j] for t in range(4)]
        acc = g[0]
        for t in range(1, 4):
            acc = f[t] * acc + g[t]
        ahead[i, j] = acc
        acc = f[3] * g[3]
        for t in (2, 1, 0):
            acc = f[t] * (acc + g[t])
        behind[i, j] = acc
    lanes = lax.broadcasted_iota(jnp.int32, (128, 128), 1)
    rows_at = lax.broadcasted_iota(jnp.int32, (128, 128), 0)
    eye = lanes == rows_at
    lower = lanes <= rows_at
    vec_f, vec_b, gains = [], [], []
    for h in range(2):
        v = [info[4 + t : 5 + t, 128 * h : 128 * h + 128] for t in range(4)]
        f = [row[t][h] for t in range(4)]
        acc = v[0]
        for t in range(1, 4):
            acc = f[t] * acc + v[t]
        vec_f.append(acc)
        acc = f[3] * v[3]
        for t in (2, 1, 0):
            acc = f[t] * (acc + v[t])
        vec_b.append(acc)
        gains.append(f[0] * f[1] * f[2] * f[3])

    def down(values):
        return jnp.sum(jnp.where(eye, values, 0.0), axis=1, keepdims=True)

    extras = [ahead[1, 1], behind[1, 1], vec_f[0], vec_f[1], vec_b[0], vec_b[1]]
    last = jnp.zeros((128, 128), f32)
    for n, e in enumerate(extras):
        last = jnp.where(lanes == n, down(e), last)
    msg[:, 0:128] = jnp.where(lower, ahead[0, 0], ahead[1, 1])
    msg[:, 128:256] = ahead[0, 1]
    msg[:, 256:384] = jnp.where(lower, behind[0, 0], behind[1, 1])
    msg[:, 384:512] = behind[0, 1]
    msg[:, 512:640] = jnp.broadcast_to(gains[0], (128, 128))
    msg[:, 640:768] = jnp.broadcast_to(gains[1], (128, 128))
    msg[:, 768:896] = last


def shifted(x, n, fill, up):
    edge = jnp.full((n, x.shape[1]), fill, f32)
    if up:
        return jnp.concatenate([x[n:], edge], axis=0)
    return jnp.concatenate([edge, x[:-n]], axis=0)


def running(gain, value, up):
    n = 1
    while n < 128:
        value = value + gain * shifted(value, n, 0.0, up)
        if n < 64:
            gain = gain * shifted(gain, n, 1.0, up)
        n *= 2
    return shifted(value, 1, 0.0, up)


def carry_kernel(at, got, out):
    place = at[2]
    lanes = lax.broadcasted_iota(jnp.int32, (128, 128), 1)
    low, high = got[:, 512:640], got[:, 640:768]
    here = lanes == place
    at_low = jnp.sum(jnp.where(here, low, 0.0), axis=1, keepdims=True)
    at_high = jnp.sum(jnp.where(here, high, 0.0), axis=1, keepdims=True)
    extra = jnp.where(lanes < 2, at_high * at_high, jnp.where((lanes == 2) | (lanes == 4), at_low, at_high))
    gain = [jnp.where(lanes <= place, at_low * low, at_high * high), at_low * high, extra]
    last = got[:, 768:896]
    enter = [running(g, v, False) for g, v in zip(gain, (got[:, 0:128], got[:, 128:256], last))]
    leave = [running(g, v, True) for g, v in zip(gain, (got[:, 256:384], got[:, 384:512], last))]
    out[:, 0:128] = enter[0]
    out[:, 128:256] = enter[1]
    out[:, 256:384] = leave[0]
    out[:, 384:512] = leave[1]
    ahead_lane = (lanes == 0) | (lanes == 2) | (lanes == 3)
    out[:, 512:640] = jnp.where(ahead_lane, enter[2], leave[2])


def final_kernel(at, got, gram, info, forget, filtered, smoothed, t_ref, b_ref, pan_ref, pn_ref, px_ref, bx_ref):
    stn = at[1]
    lanes = lax.broadcasted_iota(jnp.int32, (128, 128), 1)
    rows_at = lax.broadcasted_iota(jnp.int32, (128, 128), 0)
    eye = lanes == rows_at
    lower = lanes <= rows_at
    unit = jnp.where(eye, ridge, 0.0)
    last = got[:, 512:640]

    def lane_column(n):
        return jnp.sum(jnp.where(lanes == n, last, 0.0), axis=1, keepdims=True)

    def to_row(col):
        return jnp.sum(jnp.where(eye, col, 0.0), axis=0, keepdims=True)

    def unpack(base, diagonal):
        packed = got[:, base : base + 128]
        turned = packed.T
        first = jnp.where(lower, packed, turned)
        second = jnp.where(eye, diagonal, jnp.where(lower, turned, packed))
        return {(0, 0): first, (0, 1): got[:, base + 128 : base + 256], (1, 1): second}

    ahead = unpack(0, lane_column(0))
    behind = unpack(256, lane_column(1))
    row, col = decay(forget[...], stn)
    for n, (i, j) in enumerate(BLOCKS):
        f = [col[t][i] * row[t][j] for t in range(4)]
        acc = ahead[i, j]
        held = []
        for t in range(4):
            acc = f[t] * acc + gram[t, n]
            full = acc + unit if i == j else acc
            held.append(full)
            t_ref[j, 256 * t + 128 * i : 256 * t + 128 * i + 128, :] = full
        acc = behind[i, j]
        for t in (3, 2, 1, 0):
            at_row = 256 * (4 + t) + 128 * i
            t_ref[j, at_row : at_row + 128, :] = held[t] + acc
            if t:
                acc = f[t] * (acc + gram[t, n])
    for h in range(2):
        vec = to_row(lane_column(2 + h))
        held = []
        for t in range(4):
            vec = row[t][h] * vec + info[4 + t : 5 + t, 128 * h : 128 * h + 128]
            held.append(vec)
        vec = to_row(lane_column(4 + h))
        both = [None] * 4
        for t in (3, 2, 1, 0):
            both[t] = held[t] + vec
            if t:
                vec = row[t][h] * (vec + info[4 + t : 5 + t, 128 * h : 128 * h + 128])
        b_ref[h] = jnp.concatenate(held + both, axis=0)
    x = solve_in_place(t_ref, b_ref, pan_ref, pn_ref, px_ref, bx_ref)
    for h in range(2):
        filtered[:, 128 * h : 128 * h + 128] = x[h][0:4]
        smoothed[:, 128 * h : 128 * h + 128] = x[h][4:8]


def call(kernel, outs, scratch, operands, flops=1e6):
    return pl.pallas_call(
        kernel,
        out_shape=[jax.ShapeDtypeStruct(s, f32) for s in outs],
        in_specs=[pl.BlockSpec(memory_space=pltpu.SMEM)]
        + [pl.BlockSpec(memory_space=pltpu.VMEM)] * (len(operands) - 1),
        out_specs=[pl.BlockSpec(memory_space=pltpu.VMEM)] * len(outs),
        scratch_shapes=scratch,
        compiler_params=pltpu.CompilerParams(vmem_limit_bytes=VMEM),
        cost_estimate=pl.CostEstimate(flops=int(flops), bytes_accessed=1 << 20, transcendentals=0),
    )(*operands)


def ring(count, shift):
    return [(i, (i + shift) % count) for i in range(count)]


def body(readings, gap_mask, transfer, channel_weight, pole_site, forget):
    at = scalars()
    with jax.named_scope("design"):
        design, own, *msgs = call(
            prepare_kernel,
            [(384, 256), (8, 384)] + [(208, 256)] * 3,
            [],
            (at, transfer, pole_site[None], channel_weight[None], gap_mask, readings),
        )
    parts = [pltpu.VMEM((4, 256, 256), f32)] * 2
    with jax.named_scope("own_gram"):
        gram, info = call(own_gram_kernel, [(4, 3, 128, 128), (8, 256)], parts, (at, design, own), 6e8)
        msgs[2], gram, info = lax.optimization_barrier((msgs[2], gram, info))
    with jax.named_scope("gather"):
        got = [lax.ppermute(m, "stn", ring(4, o + 1)) for o, m in enumerate(msgs)]
        swap = [(i, i ^ 1) for i in range(32)]
        other = [lax.ppermute(g, "tm", swap) for g in got]
    with jax.named_scope("gram"):
        gram, info, totals = call(
            gram_kernel,
            [(4, 3, 128, 128), (8, 256), (128, 896)],
            [pltpu.VMEM((3, 384, 256), f32)] + parts,
            (at, gram, info, *got, *other, forget),
            2e9,
        )
    with jax.named_scope("carry"):
        mine = lax.all_to_all(totals, ("tm", "stn"), 0, 0, tiled=True)
        (entering,) = call(carry_kernel, [(128, 640)], [], (at, mine))
        entering = lax.all_to_all(entering, ("tm", "stn"), 0, 0, tiled=True)
    with jax.named_scope("solve"):
        filtered, smoothed = call(
            final_kernel, [(4, 256)] * 2, SOLVE_SCRATCH, (at, entering, gram, info, forget)
        )
    return (filtered, smoothed)


def solution(mesh):
    in_specs = (P("tm", "stn"), P("tm", "stn"), P("stn", None), P("stn"), P("stn"), P("tm", None))
    out_specs = (P(("tm", "stn"), None), P(("tm", "stn"), None))
    return jax.shard_map(body, mesh=mesh, in_specs=in_specs, out_specs=out_specs, check_vma=False)
```

```python
import jax
import jax.numpy as jnp
from jax import lax
from jax.experimental import pallas as pl
from jax.experimental.pallas import tpu as pltpu
from jax.sharding import PartitionSpec as P

near_gain = 0.5
ridge = 1.0
VMEM = 24 << 20
PANEL = 16
SUB = 16
PITCH = PANEL + 1
STEPS = 128 // PANEL
f32 = jnp.float32
bf16 = jnp.bfloat16


def split3(x):
    high = x.astype(bf16)
    rest = x - high.astype(f32)
    mid = rest.astype(bf16)
    low = (rest - mid.astype(f32)).astype(bf16)
    return high, mid, low


def inverse(x):
    return pl.reciprocal(x, approx=True)


def spread(rows, lane):
    n = rows.shape[0]
    flat = rows.reshape(n * 8, 128)
    index = jnp.full((n * 8, 128), lane, jnp.int32)
    return jnp.take_along_axis(flat, index, axis=1).reshape(n, 8, 128)


def panel_solve(parts, lane0):
    parts = [[p[SUB * s : SUB * s + SUB] for s in range(PANEL // SUB)] for p in parts]
    for s in range(PANEL // SUB):
        lane = lane0 + SUB * s
        block = parts[0][s]
        e = {}
        for i in range(SUB):
            for j in range(i, SUB):
                e[i, j] = spread(block[i : i + 1], lane + j)[0]
        mult = {}
        for q in range(PANEL // SUB):
            if q != s:
                mult[q] = [spread(parts[0][q], lane + j) for j in range(SUB)]
        low = {}
        dinv = []
        for j in range(SUB):
            d = inverse(e[j, j])
            dinv.append(d)
            for i in range(j + 1, SUB):
                low[i, j] = e[j, i] * d
            for i in range(j + 1, SUB):
                for c in range(i, SUB):
                    e[i, c] = e[i, c] - low[i, j] * e[j, c]
        for p in parts:
            rows = [p[s][i] for i in range(SUB)]
            for j in range(SUB):
                for i in range(j + 1, SUB):
                    rows[i] = rows[i] - low[i, j] * rows[j]
            rows = [rows[j] * dinv[j] for j in range(SUB)]
            for j in range(SUB - 1, 0, -1):
                for i in range(j):
                    rows[i] = rows[i] - low[j, i] * rows[j]
            p[s] = jnp.stack(rows)
            for q in range(PANEL // SUB):
                if q != s:
                    new = p[q]
                    for j in range(SUB):
                        new = new - mult[q][j] * rows[j][None]
                    p[q] = new
    return [jnp.concatenate(p, axis=0) for p in parts]


def solve_in_place(t_ref, b_ref, pan_ref, pn_ref, px_ref, bx_ref):
    def step(k, half):
        row0 = k * PANEL
        lane0 = row0 - 128 * half
        halves = [half] if half else [0, 1]

        for h in halves:
            for m in range(8):
                pan_ref[h, m * PITCH : m * PITCH + PANEL, :] = t_ref[h, pl.ds(m * 256 + row0, PANEL), :]

        def load(h):
            return jnp.stack([pan_ref[h, pl.ds(i, 8, stride=PITCH), :] for i in range(PANEL)])

        original = [load(h) for h in halves]
        vec = b_ref[half]
        right = jnp.stack([spread(vec[None], lane0 + i)[0] for i in range(PANEL)])
        done = panel_solve(original + [right], lane0)
        for h, p in zip(halves, done):
            px_ref[h, pl.ds(row0, PANEL)] = p
            for i in range(PANEL):
                pn_ref[h, pl.ds(i, 8, stride=PITCH), :] = p[i]
        bx_ref[pl.ds(row0, PANEL)] = done[-1]
        for n, h in enumerate(halves):
            b_ref[h] = b_ref[h] - jnp.sum(original[n] * done[-1], axis=0)
        def cat(x, pick):
            pieces = split3(x)
            return jnp.concatenate([pieces[c] for c in pick], axis=0)

        def dot(a, b):
            return lax.dot_general(a, b, (((0,), (0,)), ((), ())), preferred_element_type=f32)

        left = [[cat(t_ref[h, pl.ds(m * 256 + row0, PANEL), :], (0, 0, 0, 1, 1, 2)) for h in halves] for m in range(8)]
        rgt = [[cat(pn_ref[h, m * PITCH : m * PITCH + PANEL, :], (0, 1, 2, 0, 1, 0)) for h in halves] for m in range(8)]
        for m in range(8):
            top = pl.ds(m * 256, 128)
            bottom = pl.ds(m * 256 + 128, 128)
            if half:
                t_ref[1, bottom, :] = t_ref[1, bottom, :] - dot(left[m][0], rgt[m][0])
            else:
                t_ref[0, top, :] = t_ref[0, top, :] - dot(left[m][0], rgt[m][0])
                t_ref[1, top, :] = t_ref[1, top, :] - dot(left[m][0], rgt[m][1])
                t_ref[1, bottom, :] = t_ref[1, bottom, :] - dot(left[m][1], rgt[m][1])

    @pl.loop(0, STEPS)
    def _(k):
        step(k, 0)

    @pl.loop(STEPS, 2 * STEPS)
    def _(k):
        step(k, 1)

    lanes = lax.broadcasted_iota(jnp.int32, (PANEL, 8, 128), 2)
    order = lax.broadcasted_iota(jnp.int32, (PANEL, 8, 128), 0)
    zero = jnp.zeros((8, 128), f32)

    def back(k, x_halves, half):
        row0 = k * PANEL
        total = sum(px_ref[h, pl.ds(row0, PANEL)] * x_halves[h][None] for h in range(half, 2))
        x_new = bx_ref[pl.ds(row0, PANEL)] - jnp.sum(total, axis=2, keepdims=True)
        keep = jnp.where(lanes == order + (row0 - 128 * half), x_new, 0.0)
        add = jnp.sum(keep, axis=0)
        return (x_halves[0] + add, x_halves[1]) if half == 0 else (x_halves[0], x_halves[1] + add)

    x = lax.fori_loop(0, STEPS, lambda n, x: back(2 * STEPS - 1 - n, x, 1), (zero, zero))
    x = lax.fori_loop(0, STEPS, lambda n, x: back(STEPS - 1 - n, x, 0), x)
    return x


SOLVE_SCRATCH = [
    pltpu.VMEM((2, 8 * 256, 128), f32),
    pltpu.VMEM((2, 8, 128), f32),
    pltpu.VMEM((2, 8 * PITCH, 128), f32),
    pltpu.VMEM((2, 8 * PITCH, 128), f32),
    pltpu.VMEM((2, 256, 8, 128), f32),
    pltpu.VMEM((256, 8, 128), f32),
]


def scalars():
    tm = lax.axis_index("tm")
    stn = lax.axis_index("stn")
    return jnp.stack([lax.rem(tm, 2), stn, tm * 4 + stn]).astype(jnp.int32)


def column(row):
    return jnp.broadcast_to(row, (128, 128)).T


def quarter_rows(rows, quarter):
    out = rows[0:4]
    for q in range(1, 4):
        out = jnp.where(quarter == q, rows[4 * q : 4 * q + 4], out)
    return out


def prepare_kernel(at, transfer, site, weight, mask, readings, design, own, msg1, msg2, msg3):
    core, stn = at[0], at[1]
    for c in range(3):
        rows = pl.ds(128 * c, 128)
        root = column(jnp.sqrt(weight[:, 128 * c : 128 * c + 128]))
        where_site = column(site[:, 128 * c : 128 * c + 128].astype(f32))
        for h in range(2):
            pole = lax.broadcasted_iota(jnp.int32, (128, 128), 1).astype(f32) + 128.0 * h
            near = jnp.where(pole == where_site, near_gain, 0.0)
            design[rows, 128 * h : 128 * h + 128] = (transfer[rows, 128 * h : 128 * h + 128] + near) * root
    masks = mask[...].astype(f32)
    scaled = masks * jnp.sqrt(weight[...]) * readings[...]

    def piece(quarter):
        return jnp.concatenate([quarter_rows(masks, quarter), quarter_rows(scaled, quarter)], axis=0)

    own[0:16, :] = masks
    own[16:32, :] = scaled
    for o, msg in enumerate((msg1, msg2, msg3)):
        rows = piece(lax.rem(stn + (o + 1), 4))
        msg[0:384, :] = design[...]
        msg[384:392, :] = rows[:, 0:256]
        msg[392:400, 0:128] = rows[:, 256:384]
        msg[392:400, 128:256] = jnp.zeros((8, 128), f32)


def decay(forget, quarter):
    rows = quarter_rows(forget, quarter)
    row = [[rows[t : t + 1, 128 * h : 128 * h + 128] for h in range(2)] for t in range(4)]
    col = [[column(row[t][h]) for h in range(2)] for t in range(4)]
    return row, col


BLOCKS = ((0, 0), (0, 1), (1, 1))


def add_block(x, rows, even, odd, info, first):
    high, mid, low = split3(x)
    turned = x.T
    thigh = turned.astype(bf16)
    tmid = (turned - thigh.astype(f32)).astype(bf16)

    def dot(p, q):
        return jnp.dot(p, q, preferred_element_type=f32)

    part = jnp.dot(rows, x, precision=lax.Precision.HIGHEST, preferred_element_type=f32)
    info[...] = part if first else info[...] + part
    for t in range(4):
        keep = rows[t : t + 1, :].astype(bf16)
        a, b = thigh * keep, tmid * keep
        same = dot(b, mid) + dot(a, high)
        cross = dot(a, low) + dot(a, mid)
        even[t] = same if first else even[t] + same
        odd[t] = cross if first else odd[t] + cross


def gram_block(even, odd, t, n):
    i, j = BLOCKS[n]
    rs, cs = slice(128 * i, 128 * i + 128), slice(128 * j, 128 * j + 128)
    return even[t, rs, cs] + (odd[t, rs, cs] + odd[t, cs, rs].T)


def pack(ahead, behind, vec_f, vec_b):
    lanes = lax.broadcasted_iota(jnp.int32, (128, 128), 1)
    rows_at = lax.broadcasted_iota(jnp.int32, (128, 128), 0)
    eye = lanes == rows_at
    lower = lanes <= rows_at
    last = jnp.zeros((128, 128), f32)
    for n, e in enumerate([ahead[1, 1], behind[1, 1], vec_f[0], vec_f[1], vec_b[0], vec_b[1]]):
        last = jnp.where(lanes == n, jnp.sum(jnp.where(eye, e, 0.0), axis=1, keepdims=True), last)
    return (
        (jnp.where(lower, ahead[0, 0], ahead[1, 1]), ahead[0, 1]),
        (jnp.where(lower, behind[0, 0], behind[1, 1]), behind[0, 1]),
        last,
    )


def block_kernel(at, design, own, forget, gram, info, msg, grams, infos, ahead, behind):
    stn = at[1]
    x = design[...]
    high, mid, low = split3(x)
    turned = x.T
    thigh = turned.astype(bf16)
    tmid = (turned - thigh.astype(f32)).astype(bf16)

    def dot(p, q):
        return jnp.dot(p, q, preferred_element_type=f32)

    infos[...] = jnp.dot(own[16:32, :], x, precision=lax.Precision.HIGHEST, preferred_element_type=f32)
    keeps = own[0:16, :].astype(bf16)
    all_row, all_col = None, None
    vec_f, vec_b = [None, None], [None, None]
    for t in range(16):
        keep = keeps[t : t + 1, :]
        a, b = thigh * keep, tmid * keep
        same = dot(b, mid) + dot(a, high)
        cross = dot(a, low) + dot(a, mid)
        row = [forget[t : t + 1, 128 * h : 128 * h + 128] for h in range(2)]
        col = [column(r) for r in row]
        all_row = row if t == 0 else [p * q for p, q in zip(all_row, row)]
        all_col = col if t == 0 else [p * q for p, q in zip(all_col, col)]
        for n, (i, j) in enumerate(BLOCKS):
            rs, cs = slice(128 * i, 128 * i + 128), slice(128 * j, 128 * j + 128)
            g = same[rs, cs] + (cross[rs, cs] + cross[cs, rs].T)
            grams[t, n] = g
            past = (all_col[i] * all_row[j]) * g
            if t == 0:
                ahead[n] = g
                behind[n] = past
            else:
                ahead[n] = (col[i] * row[j]) * ahead[n] + g
                behind[n] += past
        for h in range(2):
            v = infos[t : t + 1, 128 * h : 128 * h + 128]
            vec_f[h] = v if t == 0 else row[h] * vec_f[h] + v
            vec_b[h] = all_row[h] * v if t == 0 else vec_b[h] + all_row[h] * v
    for t in range(4):
        for n in range(3):
            gram[t, n] = grams[4 * stn + t, n]
    info[0:4, :] = jnp.zeros((4, 256), f32)
    info[4:8, :] = quarter_rows(infos[...], stn)
    f, b, last = pack(
        {k: ahead[n] for n, k in enumerate(BLOCKS)}, {k: behind[n] for n, k in enumerate(BLOCKS)}, vec_f, vec_b
    )
    wide = [jnp.broadcast_to(r, (128, 128)) for r in all_row]
    share = jnp.where(stn == 1, wide[0], wide[1])
    turned_share = pltpu.roll(jnp.where(stn == 0, wide[0], wide[1]), 64, 1)
    share = jnp.where((stn == 0) | (stn == 2), turned_share, share)
    lanes = lax.broadcasted_iota(jnp.int32, (128, 128), 1)
    for n, part in enumerate((*f, *b, jnp.where(lanes < 64, last, share))):
        msg[:, 128 * n : 128 * n + 128] = part


def gram_kernel(
    at, gram_in, info_in, got1, got2, got3, forget, gram, info, msg1, msg2, msg3, held, even, odd, sem
):
    core, stn = at[0], at[1]
    copy = pltpu.make_async_copy(gram_in, held, sem)
    copy.start()
    for n, got in enumerate((got1, got3, got2)):
        rows = jnp.concatenate([got[384:392, :], got[392:400, 0:128]], axis=1)
        add_block(got[0:384, :], rows, even, odd, info, n == 0)
    info[...] += info_in[...]
    copy.wait()
    for t in range(4):
        for n in range(3):
            gram[t, n] = held[t, n] + gram_block(even, odd, t, n)
    row, col = decay(forget[...], stn)
    ahead, behind = {}, {}
    for n, (i, j) in enumerate(BLOCKS):
        g = [gram[t, n] for t in range(4)]
        f = [col[t][i] * row[t][j] for t in range(4)]
        acc = g[0]
        for t in range(1, 4):
            acc = f[t] * acc + g[t]
        ahead[i, j] = acc
        acc = f[3] * g[3]
        for t in (2, 1, 0):
            acc = f[t] * (acc + g[t])
        behind[i, j] = acc
    vec_f, vec_b = [], []
    for h in range(2):
        v = [info[4 + t : 5 + t, 128 * h : 128 * h + 128] for t in range(4)]
        f = [row[t][h] for t in range(4)]
        acc = v[0]
        for t in range(1, 4):
            acc = f[t] * acc + v[t]
        vec_f.append(acc)
        acc = f[3] * v[3]
        for t in (2, 1, 0):
            acc = f[t] * (acc + v[t])
        vec_b.append(acc)
    lanes = lax.broadcasted_iota(jnp.int32, (128, 128), 1)
    rows_at = lax.broadcasted_iota(jnp.int32, (128, 128), 0)
    edge = lax.broadcasted_iota(jnp.int32, (8, 128), 0)

    def rows_of(blocks, vec):
        diagonal = jnp.sum(jnp.where(lanes == rows_at, blocks[1, 1], 0.0), axis=0, keepdims=True)
        return (
            jnp.where(lanes <= rows_at, blocks[0, 0], blocks[1, 1]),
            blocks[0, 1],
            jnp.where(edge == 0, vec[0], jnp.where(edge == 1, diagonal, 0.0)),
            jnp.where(edge == 0, vec[1], 0.0),
        )

    f, b = rows_of(ahead, vec_f), rows_of(behind, vec_b)
    for o, msg in enumerate((msg1, msg2, msg3)):
        later = lax.rem(stn + (o + 1), 4) > stn
        for n in range(4):
            rows = slice(128, 136) if n >= 2 else slice(0, 128)
            msg[rows, 128 * (n % 2) : 128 * (n % 2) + 128] = jnp.where(later, f[n], b[n])


def moved(x, n):
    return jnp.concatenate([x[-n:], x[:-n]], axis=0)


def shifted(x, n, fill, up):
    edge = jnp.full((n, x.shape[1]), fill, f32)
    if up:
        return jnp.concatenate([x[n:], edge], axis=0)
    return jnp.concatenate([edge, x[:-n]], axis=0)


def running(gain, value, up):
    n = 4
    while n < 128:
        value = value + gain * shifted(value, n, 0.0, up)
        if n < 64:
            gain = gain * shifted(gain, n, 1.0, up)
        n *= 2
    value = shifted(value, 4, 0.0, up)
    rows_at = lax.broadcasted_iota(jnp.int32, (128, 128), 0)
    value = jnp.where(lax.rem(rows_at, 4) == 0, value, 0.0)
    value = value + moved(value, 1)
    return value + moved(value, 2)


def carry_kernel(at, got, out):
    place = at[2]
    lanes = lax.broadcasted_iota(jnp.int32, (128, 128), 1)
    last = got[:, 512:640]
    swapped = pltpu.roll(last, 64, 1)
    low = jnp.where(lanes < 64, swapped, moved(last, -1))
    high = jnp.where(lanes < 64, moved(swapped, -2), moved(last, -3))
    here = lanes == place
    at_low = jnp.sum(jnp.where(here, low, 0.0), axis=1, keepdims=True)
    at_high = jnp.sum(jnp.where(here, high, 0.0), axis=1, keepdims=True)
    extra = jnp.where(lanes < 2, at_high * at_high, jnp.where((lanes == 2) | (lanes == 4), at_low, at_high))
    gain = [jnp.where(lanes <= place, at_low * low, at_high * high), at_low * high, extra]

    def total(x):
        x = x + moved(x, -1)
        return x + moved(x, -2)

    last = total(jnp.where(lanes < 6, last, 0.0))
    enter = [running(g, v, False) for g, v in zip(gain, (total(got[:, 0:128]), total(got[:, 128:256]), last))]
    leave = [running(g, v, True) for g, v in zip(gain, (total(got[:, 256:384]), total(got[:, 384:512]), last))]
    ahead_lane = (lanes == 0) | (lanes == 2) | (lanes == 3)
    parts = (enter[0], enter[1], leave[0], leave[1], jnp.where(ahead_lane, enter[2], leave[2]))
    for n, part in enumerate(parts):
        out[:, 128 * n : 128 * n + 128] = part


def final_kernel(
    at, got, quarter1, quarter2, quarter3, gram, info, forget, filtered, smoothed, quarters,
    t_ref, b_ref, pan_ref, pn_ref, px_ref, bx_ref,
):
    stn = at[1]
    lanes = lax.broadcasted_iota(jnp.int32, (128, 128), 1)
    rows_at = lax.broadcasted_iota(jnp.int32, (128, 128), 0)
    eye = lanes == rows_at
    lower = lanes <= rows_at
    unit = jnp.where(eye, ridge, 0.0)
    for o, quarter in enumerate((quarter1, quarter2, quarter3)):
        quarters[lax.rem(stn + (3 - o), 4)] = quarter[...]
    last = got[:, 512:640]

    def lane_row(n):
        col = jnp.sum(jnp.where(lanes == n, last, 0.0), axis=1, keepdims=True)
        return jnp.sum(jnp.where(eye, col, 0.0), axis=0, keepdims=True)

    first = [got[:, 0:128], got[:, 128:256], lane_row(2), lane_row(3), lane_row(0)]
    second = [got[:, 256:384], got[:, 384:512], lane_row(4), lane_row(5), lane_row(1)]

    def past_quarter(q, state, use):
        gain = forget[4 * q : 4 * q + 1, :]
        for t in range(1, 4):
            gain = gain * forget[4 * q + t : 4 * q + t + 1, :]
        low, high = gain[:, 0:128], gain[:, 128:256]
        clow, chigh = column(low), column(high)
        gains = (jnp.where(lower, clow * low, chigh * high), clow * high, low, high, high * high)
        own = (
            quarters[q, 0:128, 0:128],
            quarters[q, 0:128, 128:256],
            quarters[q, 128:129, 0:128],
            quarters[q, 128:129, 128:256],
            quarters[q, 129:130, 0:128],
        )
        return [jnp.where(use, g * v + w, v) for g, v, w in zip(gains, state, own)]

    for q in (0, 1, 2):
        first = past_quarter(q, first, q < stn)
    for q in (3, 2, 1):
        second = past_quarter(q, second, q > stn)

    def unpack(state):
        packed = state[0]
        turned = packed.T
        one = jnp.where(lower, packed, turned)
        two = jnp.where(eye, state[4], jnp.where(lower, turned, packed))
        return {(0, 0): one, (0, 1): state[1], (1, 1): two}

    ahead = unpack(first)
    behind = unpack(second)
    row, col = decay(forget[...], stn)
    for n, (i, j) in enumerate(BLOCKS):
        f = [col[t][i] * row[t][j] for t in range(4)]
        acc = ahead[i, j]
        held = []
        for t in range(4):
            acc = f[t] * acc + gram[t, n]
            full = acc + unit if i == j else acc
            held.append(full)
            t_ref[j, 256 * t + 128 * i : 256 * t + 128 * i + 128, :] = full
        acc = behind[i, j]
        for t in (3, 2, 1, 0):
            at_row = 256 * (4 + t) + 128 * i
            t_ref[j, at_row : at_row + 128, :] = held[t] + acc
            if t:
                acc = f[t] * (acc + gram[t, n])
    for h in range(2):
        vec = first[2 + h]
        held = []
        for t in range(4):
            vec = row[t][h] * vec + info[4 + t : 5 + t, 128 * h : 128 * h + 128]
            held.append(vec)
        vec = second[2 + h]
        both = [None] * 4
        for t in (3, 2, 1, 0):
            both[t] = held[t] + vec
            if t:
                vec = row[t][h] * (vec + info[4 + t : 5 + t, 128 * h : 128 * h + 128])
        b_ref[h] = jnp.concatenate(held + both, axis=0)
    x = solve_in_place(t_ref, b_ref, pan_ref, pn_ref, px_ref, bx_ref)
    for h in range(2):
        filtered[:, 128 * h : 128 * h + 128] = x[h][0:4]
        smoothed[:, 128 * h : 128 * h + 128] = x[h][4:8]


def call(kernel, outs, scratch, operands, flops=1e6, away=()):
    return pl.pallas_call(
        kernel,
        out_shape=[jax.ShapeDtypeStruct(s, f32) for s in outs],
        in_specs=[pl.BlockSpec(memory_space=pltpu.SMEM)]
        + [pl.BlockSpec(memory_space=pl.ANY if n in away else pltpu.VMEM) for n in range(1, len(operands))],
        out_specs=[pl.BlockSpec(memory_space=pltpu.VMEM)] * len(outs),
        scratch_shapes=scratch,
        compiler_params=pltpu.CompilerParams(vmem_limit_bytes=VMEM),
        cost_estimate=pl.CostEstimate(flops=int(flops), bytes_accessed=1 << 20, transcendentals=0),
    )(*operands)


def ring(count, shift):
    return [(i, (i + shift) % count) for i in range(count)]


def body(readings, gap_mask, transfer, channel_weight, pole_site, forget):
    at = scalars()
    parts = [pltpu.VMEM((4, 256, 256), f32)] * 2
    with jax.named_scope("design"):
        design, own, *msgs = call(
            prepare_kernel,
            [(384, 256), (32, 384)] + [(400, 256)] * 3,
            [],
            (at, transfer, pole_site[None], channel_weight[None], gap_mask, readings),
        )
    with jax.named_scope("gather"):
        got = [lax.ppermute(m, "stn", ring(4, o + 1)) for o, m in enumerate(msgs)]
    with jax.named_scope("block"):
        gram, info, totals = call(
            block_kernel,
            [(4, 3, 128, 128), (8, 256), (128, 640)],
            [
                pltpu.VMEM((16, 3, 128, 128), f32),
                pltpu.VMEM((16, 256), f32),
                pltpu.VMEM((3, 128, 128), f32),
                pltpu.VMEM((3, 128, 128), f32),
            ],
            (at, design, own, forget),
            6e9,
        )
    with jax.named_scope("carry"):
        mine = lax.all_to_all(totals, ("tm", "stn"), 0, 0, tiled=True)
    with jax.named_scope("gram"):
        gram, info, *totals = call(
            gram_kernel,
            [(4, 3, 128, 128), (8, 256)] + [(136, 256)] * 3,
            [pltpu.VMEM((4, 3, 128, 128), f32)] + parts + [pltpu.SemaphoreType.DMA(())],
            (at, gram, info, *got, forget),
            2e9,
            away=(1,),
        )
    mine, *totals = lax.optimization_barrier((mine, *totals))
    with jax.named_scope("quarters"):
        quarters = [lax.ppermute(m, "stn", ring(4, o + 1)) for o, m in enumerate(totals)]
    with jax.named_scope("carry"):
        (entering,) = call(carry_kernel, [(128, 640)], [], (at, mine))
        entering = lax.all_to_all(entering, ("tm", "stn"), 0, 0, tiled=True)
    with jax.named_scope("solve"):
        filtered, smoothed = call(
            final_kernel,
            [(4, 256)] * 2,
            [pltpu.VMEM((4, 136, 256), f32)] + SOLVE_SCRATCH,
            (at, entering, *quarters, gram, info, forget),
        )
    return (filtered, smoothed)


def solution(mesh):
    in_specs = (P("tm", "stn"), P("tm", "stn"), P("stn", None), P("stn"), P("stn"), P("tm", None))
    out_specs = (P(("tm", "stn"), None), P(("tm", "stn"), None))
    return jax.shard_map(body, mesh=mesh, in_specs=in_specs, out_specs=out_specs, check_vma=False)
```

```python
import jax
import jax.numpy as jnp
from jax import lax
from jax.experimental import pallas as pl
from jax.experimental.pallas import tpu as pltpu
from jax.sharding import PartitionSpec as P

near_gain = 0.5
ridge = 1.0
VMEM = 24 << 20
PANEL = 16
SUB = 16
PITCH = PANEL + 1
STEPS = 128 // PANEL
f32 = jnp.float32
bf16 = jnp.bfloat16


def split3(x):
    high = x.astype(bf16)
    rest = x - high.astype(f32)
    mid = rest.astype(bf16)
    low = (rest - mid.astype(f32)).astype(bf16)
    return high, mid, low


def inverse(x):
    return pl.reciprocal(x, approx=True)


def spread(rows, lane):
    n = rows.shape[0]
    flat = rows.reshape(n * 8, 128)
    index = jnp.full((n * 8, 128), lane, jnp.int32)
    return jnp.take_along_axis(flat, index, axis=1).reshape(n, 8, 128)


def panel_solve(parts, lane0):
    parts = [[p[SUB * s : SUB * s + SUB] for s in range(PANEL // SUB)] for p in parts]
    for s in range(PANEL // SUB):
        lane = lane0 + SUB * s
        block = parts[0][s]
        e = {}
        for i in range(SUB):
            for j in range(i, SUB):
                e[i, j] = spread(block[i : i + 1], lane + j)[0]
        mult = {}
        for q in range(PANEL // SUB):
            if q != s:
                mult[q] = [spread(parts[0][q], lane + j) for j in range(SUB)]
        low = {}
        dinv = []
        for j in range(SUB):
            d = inverse(e[j, j])
            dinv.append(d)
            for i in range(j + 1, SUB):
                low[i, j] = e[j, i] * d
            for i in range(j + 1, SUB):
                for c in range(i, SUB):
                    e[i, c] = e[i, c] - low[i, j] * e[j, c]
        for p in parts:
            rows = [p[s][i] for i in range(SUB)]
            for j in range(SUB):
                for i in range(j + 1, SUB):
                    rows[i] = rows[i] - low[i, j] * rows[j]
            rows = [rows[j] * dinv[j] for j in range(SUB)]
            for j in range(SUB - 1, 0, -1):
                for i in range(j):
                    rows[i] = rows[i] - low[j, i] * rows[j]
            p[s] = jnp.stack(rows)
            for q in range(PANEL // SUB):
                if q != s:
                    new = p[q]
                    for j in range(SUB):
                        new = new - mult[q][j] * rows[j][None]
                    p[q] = new
    return [jnp.concatenate(p, axis=0) for p in parts]


def solve_in_place(t_ref, b_ref, pan_ref, pn_ref, px_ref, bx_ref):
    def step(k, half):
        row0 = k * PANEL
        lane0 = row0 - 128 * half
        halves = [half] if half else [0, 1]

        for h in halves:
            for m in range(8):
                pan_ref[h, m * PITCH : m * PITCH + PANEL, :] = t_ref[h, pl.ds(m * 256 + row0, PANEL), :]

        def load(h):
            return jnp.stack([pan_ref[h, pl.ds(i, 8, stride=PITCH), :] for i in range(PANEL)])

        original = [load(h) for h in halves]
        vec = b_ref[half]
        right = jnp.stack([spread(vec[None], lane0 + i)[0] for i in range(PANEL)])
        done = panel_solve(original + [right], lane0)
        for h, p in zip(halves, done):
            px_ref[h, pl.ds(row0, PANEL)] = p
            for i in range(PANEL):
                pn_ref[h, pl.ds(i, 8, stride=PITCH), :] = p[i]
        bx_ref[pl.ds(row0, PANEL)] = done[-1]
        for n, h in enumerate(halves):
            b_ref[h] = b_ref[h] - jnp.sum(original[n] * done[-1], axis=0)
        def cat(x, pick):
            pieces = split3(x)
            return jnp.concatenate([pieces[c] for c in pick], axis=0)

        def dot(a, b):
            return lax.dot_general(a, b, (((0,), (0,)), ((), ())), preferred_element_type=f32)

        left = [[cat(t_ref[h, pl.ds(m * 256 + row0, PANEL), :], (0, 0, 0, 1, 1, 2)) for h in halves] for m in range(8)]
        rgt = [[cat(pn_ref[h, m * PITCH : m * PITCH + PANEL, :], (0, 1, 2, 0, 1, 0)) for h in halves] for m in range(8)]
        for m in range(8):
            top = pl.ds(m * 256, 128)
            bottom = pl.ds(m * 256 + 128, 128)
            if half:
                t_ref[1, bottom, :] = t_ref[1, bottom, :] - dot(left[m][0], rgt[m][0])
            else:
                t_ref[0, top, :] = t_ref[0, top, :] - dot(left[m][0], rgt[m][0])
                t_ref[1, top, :] = t_ref[1, top, :] - dot(left[m][0], rgt[m][1])
                t_ref[1, bottom, :] = t_ref[1, bottom, :] - dot(left[m][1], rgt[m][1])

    @pl.loop(0, STEPS)
    def _(k):
        step(k, 0)

    @pl.loop(STEPS, 2 * STEPS)
    def _(k):
        step(k, 1)

    lanes = lax.broadcasted_iota(jnp.int32, (PANEL, 8, 128), 2)
    order = lax.broadcasted_iota(jnp.int32, (PANEL, 8, 128), 0)
    zero = jnp.zeros((8, 128), f32)

    def back(k, x_halves, half):
        row0 = k * PANEL
        total = sum(px_ref[h, pl.ds(row0, PANEL)] * x_halves[h][None] for h in range(half, 2))
        x_new = bx_ref[pl.ds(row0, PANEL)] - jnp.sum(total, axis=2, keepdims=True)
        keep = jnp.where(lanes == order + (row0 - 128 * half), x_new, 0.0)
        add = jnp.sum(keep, axis=0)
        return (x_halves[0] + add, x_halves[1]) if half == 0 else (x_halves[0], x_halves[1] + add)

    x = lax.fori_loop(0, STEPS, lambda n, x: back(2 * STEPS - 1 - n, x, 1), (zero, zero))
    x = lax.fori_loop(0, STEPS, lambda n, x: back(STEPS - 1 - n, x, 0), x)
    return x


SOLVE_SCRATCH = [
    pltpu.VMEM((2, 8 * 256, 128), f32),
    pltpu.VMEM((2, 8, 128), f32),
    pltpu.VMEM((2, 8 * PITCH, 128), f32),
    pltpu.VMEM((2, 8 * PITCH, 128), f32),
    pltpu.VMEM((2, 256, 8, 128), f32),
    pltpu.VMEM((256, 8, 128), f32),
]


def scalars():
    tm = lax.axis_index("tm")
    stn = lax.axis_index("stn")
    return jnp.stack([lax.rem(tm, 2), stn, tm * 4 + stn]).astype(jnp.int32)


def column(row):
    return jnp.broadcast_to(row, (128, 128)).T


def quarter_rows(rows, quarter):
    out = rows[0:4]
    for q in range(1, 4):
        out = jnp.where(quarter == q, rows[4 * q : 4 * q + 4], out)
    return out


def prepare_kernel(at, transfer, site, weight, mask, readings, design, own, msg1, msg2, msg3):
    core, stn = at[0], at[1]
    for c in range(3):
        rows = pl.ds(128 * c, 128)
        root = column(jnp.sqrt(weight[:, 128 * c : 128 * c + 128]))
        where_site = column(site[:, 128 * c : 128 * c + 128].astype(f32))
        for h in range(2):
            pole = lax.broadcasted_iota(jnp.int32, (128, 128), 1).astype(f32) + 128.0 * h
            near = jnp.where(pole == where_site, near_gain, 0.0)
            design[rows, 128 * h : 128 * h + 128] = (transfer[rows, 128 * h : 128 * h + 128] + near) * root
    masks = mask[...].astype(f32)
    scaled = masks * jnp.sqrt(weight[...]) * readings[...]

    def piece(quarter):
        return jnp.concatenate([quarter_rows(masks, quarter), quarter_rows(scaled, quarter)], axis=0)

    own[0:16, :] = masks
    own[16:32, :] = scaled
    for o, msg in enumerate((msg1, msg2, msg3)):
        rows = piece(lax.rem(stn + (o + 1), 4))
        msg[0:384, :] = design[...]
        msg[384:392, :] = rows[:, 0:256]
        msg[392:400, 0:128] = rows[:, 256:384]
        msg[392:400, 128:256] = jnp.zeros((8, 128), f32)


def decay(forget, quarter):
    rows = quarter_rows(forget, quarter)
    row = [[rows[t : t + 1, 128 * h : 128 * h + 128] for h in range(2)] for t in range(4)]
    col = [[column(row[t][h]) for h in range(2)] for t in range(4)]
    return row, col


BLOCKS = ((0, 0), (0, 1), (1, 1))


def products(x, keeps, extra=None):
    high, mid, low = split3(x)
    turned = x.T
    thigh = turned.astype(bf16)
    tmid = (turned - thigh.astype(f32)).astype(bf16)
    right = jnp.concatenate([high, mid], axis=0), jnp.concatenate([mid, low], axis=0)

    def four(q):
        out = [], []
        for t in range(4):
            keep = keeps[4 * q + t : 4 * q + t + 1, :].astype(bf16)
            a, b = thigh * keep, tmid * keep
            for n, left in enumerate((jnp.concatenate([a, b], axis=1), jnp.concatenate([a, a], axis=1))):
                if t == 3 and extra is not None:
                    left = jnp.concatenate([left, extra[n]], axis=0)
                out[n].append(jnp.dot(left, right[n], preferred_element_type=f32))
        return out

    return four


def add_block(x, rows, even, odd, info, first):
    high, mid, low = (p.astype(f32) for p in split3(rows[4:8, :]))
    blank = jnp.zeros((4, 384), f32)

    def chunk(*quarters):
        return jnp.concatenate(quarters, axis=0).astype(bf16)

    top = chunk(high, blank, blank, blank)
    extra = (
        jnp.concatenate([chunk(high, mid, low, blank), chunk(mid, blank, blank, blank)], axis=1),
        jnp.concatenate([top, top], axis=1),
    )
    same, cross = products(x, rows, extra)(0)
    tail, cross_tail = same[3][256:272], cross[3][256:272]
    part = tail[0:4] + tail[4:8] + tail[8:12] + cross_tail[0:4]
    info[4:8, :] = part if first else info[4:8, :] + part
    for t in range(4):
        even[t] = same[t][0:256] if first else even[t] + same[t][0:256]
        odd[t] = cross[t][0:256] if first else odd[t] + cross[t][0:256]


def gram_block(even, odd, t, n):
    i, j = BLOCKS[n]
    rs, cs = slice(128 * i, 128 * i + 128), slice(128 * j, 128 * j + 128)
    return even[t, rs, cs] + (odd[t, rs, cs] + odd[t, cs, rs].T)


def pack(ahead, behind, vec_f, vec_b):
    lanes = lax.broadcasted_iota(jnp.int32, (128, 128), 1)
    rows_at = lax.broadcasted_iota(jnp.int32, (128, 128), 0)
    eye = lanes == rows_at
    lower = lanes <= rows_at
    last = jnp.zeros((128, 128), f32)
    for n, e in enumerate([ahead[1, 1], behind[1, 1], vec_f[0], vec_f[1], vec_b[0], vec_b[1]]):
        last = jnp.where(lanes == n, jnp.sum(jnp.where(eye, e, 0.0), axis=1, keepdims=True), last)
    return (
        (jnp.where(lower, ahead[0, 0], ahead[1, 1]), ahead[0, 1]),
        (jnp.where(lower, behind[0, 0], behind[1, 1]), behind[0, 1]),
        last,
    )


def block_kernel(at, design, own, forget, gram, info, msg, grams, infos, ahead, behind):
    stn = at[1]
    x = design[...]
    four = products(x, own)
    infos[...] = jnp.dot(own[16:32, :], x, precision=lax.Precision.HIGHEST, preferred_element_type=f32)
    all_row, all_col = None, None
    vec_f, vec_b = [None, None], [None, None]
    for t in range(16):
        if t % 4 == 0:
            all_same, all_cross = four(t // 4)
        same, cross = all_same[t % 4], all_cross[t % 4]
        row = [forget[t : t + 1, 128 * h : 128 * h + 128] for h in range(2)]
        col = [column(r) for r in row]
        all_row = row if t == 0 else [p * q for p, q in zip(all_row, row)]
        all_col = col if t == 0 else [p * q for p, q in zip(all_col, col)]
        for n, (i, j) in enumerate(BLOCKS):
            rs, cs = slice(128 * i, 128 * i + 128), slice(128 * j, 128 * j + 128)
            g = same[rs, cs] + (cross[rs, cs] + cross[cs, rs].T)
            grams[t, n] = g
            past = (all_col[i] * all_row[j]) * g
            if t == 0:
                ahead[n] = g
                behind[n] = past
            else:
                ahead[n] = (col[i] * row[j]) * ahead[n] + g
                behind[n] += past
        for h in range(2):
            v = infos[t : t + 1, 128 * h : 128 * h + 128]
            vec_f[h] = v if t == 0 else row[h] * vec_f[h] + v
            vec_b[h] = all_row[h] * v if t == 0 else vec_b[h] + all_row[h] * v
    for t in range(4):
        for n in range(3):
            gram[t, n] = grams[4 * stn + t, n]
    info[0:4, :] = jnp.zeros((4, 256), f32)
    info[4:8, :] = quarter_rows(infos[...], stn)
    f, b, last = pack(
        {k: ahead[n] for n, k in enumerate(BLOCKS)}, {k: behind[n] for n, k in enumerate(BLOCKS)}, vec_f, vec_b
    )
    wide = [jnp.broadcast_to(r, (128, 128)) for r in all_row]
    share = jnp.where(stn == 1, wide[0], wide[1])
    turned_share = pltpu.roll(jnp.where(stn == 0, wide[0], wide[1]), 64, 1)
    share = jnp.where((stn == 0) | (stn == 2), turned_share, share)
    lanes = lax.broadcasted_iota(jnp.int32, (128, 128), 1)
    for n, part in enumerate((*f, *b, jnp.where(lanes < 64, last, share))):
        msg[:, 128 * n : 128 * n + 128] = part


def gram_kernel(
    at, gram_in, info_in, got1, got2, got3, forget, gram, info, msg1, msg2, msg3, held, even, odd, sem
):
    core, stn = at[0], at[1]
    copy = pltpu.make_async_copy(gram_in, held, sem)
    copy.start()
    for n, got in enumerate((got1, got3, got2)):
        rows = jnp.concatenate([got[384:392, :], got[392:400, 0:128]], axis=1)
        add_block(got[0:384, :], rows, even, odd, info, n == 0)
    info[0:4, :] = jnp.zeros((4, 256), f32)
    info[4:8, :] += info_in[4:8, :]
    copy.wait()
    for t in range(4):
        for n in range(3):
            gram[t, n] = held[t, n] + gram_block(even, odd, t, n)
    row, col = decay(forget[...], stn)
    ahead, behind = {}, {}
    for n, (i, j) in enumerate(BLOCKS):
        g = [gram[t, n] for t in range(4)]
        f = [col[t][i] * row[t][j] for t in range(4)]
        acc = g[0]
        for t in range(1, 4):
            acc = f[t] * acc + g[t]
        ahead[i, j] = acc
        acc = f[3] * g[3]
        for t in (2, 1, 0):
            acc = f[t] * (acc + g[t])
        behind[i, j] = acc
    vec_f, vec_b = [], []
    for h in range(2):
        v = [info[4 + t : 5 + t, 128 * h : 128 * h + 128] for t in range(4)]
        f = [row[t][h] for t in range(4)]
        acc = v[0]
        for t in range(1, 4):
            acc = f[t] * acc + v[t]
        vec_f.append(acc)
        acc = f[3] * v[3]
        for t in (2, 1, 0):
            acc = f[t] * (acc + v[t])
        vec_b.append(acc)
    lanes = lax.broadcasted_iota(jnp.int32, (128, 128), 1)
    rows_at = lax.broadcasted_iota(jnp.int32, (128, 128), 0)
    edge = lax.broadcasted_iota(jnp.int32, (8, 128), 0)

    def rows_of(blocks, vec):
        diagonal = jnp.sum(jnp.where(lanes == rows_at, blocks[1, 1], 0.0), axis=0, keepdims=True)
        return (
            jnp.where(lanes <= rows_at, blocks[0, 0], blocks[1, 1]),
            blocks[0, 1],
            jnp.where(edge == 0, vec[0], jnp.where(edge == 1, diagonal, 0.0)),
            jnp.where(edge == 0, vec[1], 0.0),
        )

    f, b = rows_of(ahead, vec_f), rows_of(behind, vec_b)
    for o, msg in enumerate((msg1, msg2, msg3)):
        later = lax.rem(stn + (o + 1), 4) > stn
        for n in range(4):
            rows = slice(128, 136) if n >= 2 else slice(0, 128)
            msg[rows, 128 * (n % 2) : 128 * (n % 2) + 128] = jnp.where(later, f[n], b[n])


def moved(x, n):
    return jnp.concatenate([x[-n:], x[:-n]], axis=0)


def shifted(x, n, fill, up):
    edge = jnp.full((n, x.shape[1]), fill, f32)
    if up:
        return jnp.concatenate([x[n:], edge], axis=0)
    return jnp.concatenate([edge, x[:-n]], axis=0)


def running(gain, value, up):
    n = 4
    while n < 128:
        value = value + gain * shifted(value, n, 0.0, up)
        if n < 64:
            gain = gain * shifted(gain, n, 1.0, up)
        n *= 2
    value = shifted(value, 4, 0.0, up)
    rows_at = lax.broadcasted_iota(jnp.int32, (128, 128), 0)
    value = jnp.where(lax.rem(rows_at, 4) == 0, value, 0.0)
    value = value + moved(value, 1)
    return value + moved(value, 2)


def carry_kernel(at, got, token, out):
    place = at[2]
    lanes = lax.broadcasted_iota(jnp.int32, (128, 128), 1)
    last = got[:, 512:640]
    swapped = pltpu.roll(last, 64, 1)
    low = jnp.where(lanes < 64, swapped, moved(last, -1))
    high = jnp.where(lanes < 64, moved(swapped, -2), moved(last, -3))
    here = lanes == place
    at_low = jnp.sum(jnp.where(here, low, 0.0), axis=1, keepdims=True)
    at_high = jnp.sum(jnp.where(here, high, 0.0), axis=1, keepdims=True)
    extra = jnp.where(lanes < 2, at_high * at_high, jnp.where((lanes == 2) | (lanes == 4), at_low, at_high))
    gain = [jnp.where(lanes <= place, at_low * low, at_high * high), at_low * high, extra]

    def total(x):
        x = x + moved(x, -1)
        return x + moved(x, -2)

    last = total(jnp.where(lanes < 6, last, 0.0))
    enter = [running(g, v, False) for g, v in zip(gain, (total(got[:, 0:128]), total(got[:, 128:256]), last))]
    leave = [running(g, v, True) for g, v in zip(gain, (total(got[:, 256:384]), total(got[:, 384:512]), last))]
    ahead_lane = (lanes == 0) | (lanes == 2) | (lanes == 3)
    parts = (enter[0], enter[1], leave[0], leave[1], jnp.where(ahead_lane, enter[2], leave[2]))
    for n, part in enumerate(parts):
        out[:, 128 * n : 128 * n + 128] = part


def final_kernel(
    at, got, quarter1, quarter2, quarter3, gram, info, forget, filtered, smoothed, quarters,
    t_ref, b_ref, pan_ref, pn_ref, px_ref, bx_ref,
):
    stn = at[1]
    lanes = lax.broadcasted_iota(jnp.int32, (128, 128), 1)
    rows_at = lax.broadcasted_iota(jnp.int32, (128, 128), 0)
    eye = lanes == rows_at
    lower = lanes <= rows_at
    unit = jnp.where(eye, ridge, 0.0)
    for o, quarter in enumerate((quarter1, quarter2, quarter3)):
        quarters[lax.rem(stn + (3 - o), 4)] = quarter[...]
    last = got[:, 512:640]

    def lane_row(n):
        col = jnp.sum(jnp.where(lanes == n, last, 0.0), axis=1, keepdims=True)
        return jnp.sum(jnp.where(eye, col, 0.0), axis=0, keepdims=True)

    first = [got[:, 0:128], got[:, 128:256], lane_row(2), lane_row(3), lane_row(0)]
    second = [got[:, 256:384], got[:, 384:512], lane_row(4), lane_row(5), lane_row(1)]

    def past_quarter(q, state, use):
        gain = forget[4 * q : 4 * q + 1, :]
        for t in range(1, 4):
            gain = gain * forget[4 * q + t : 4 * q + t + 1, :]
        low, high = gain[:, 0:128], gain[:, 128:256]
        clow, chigh = column(low), column(high)
        gains = (jnp.where(lower, clow * low, chigh * high), clow * high, low, high, high * high)
        own = (
            quarters[q, 0:128, 0:128],
            quarters[q, 0:128, 128:256],
            quarters[q, 128:129, 0:128],
            quarters[q, 128:129, 128:256],
            quarters[q, 129:130, 0:128],
        )
        return [jnp.where(use, g * v + w, v) for g, v, w in zip(gains, state, own)]

    for q in (0, 1, 2):
        first = past_quarter(q, first, q < stn)
    for q in (3, 2, 1):
        second = past_quarter(q, second, q > stn)

    def unpack(state):
        packed = state[0]
        turned = packed.T
        one = jnp.where(lower, packed, turned)
        two = jnp.where(eye, state[4], jnp.where(lower, turned, packed))
        return {(0, 0): one, (0, 1): state[1], (1, 1): two}

    ahead = unpack(first)
    behind = unpack(second)
    row, col = decay(forget[...], stn)
    for n, (i, j) in enumerate(BLOCKS):
        f = [col[t][i] * row[t][j] for t in range(4)]
        acc = ahead[i, j]
        held = []
        for t in range(4):
            acc = f[t] * acc + gram[t, n]
            full = acc + unit if i == j else acc
            held.append(full)
            t_ref[j, 256 * t + 128 * i : 256 * t + 128 * i + 128, :] = full
        acc = behind[i, j]
        for t in (3, 2, 1, 0):
            at_row = 256 * (4 + t) + 128 * i
            t_ref[j, at_row : at_row + 128, :] = held[t] + acc
            if t:
                acc = f[t] * (acc + gram[t, n])
    for h in range(2):
        vec = first[2 + h]
        held = []
        for t in range(4):
            vec = row[t][h] * vec + info[4 + t : 5 + t, 128 * h : 128 * h + 128]
            held.append(vec)
        vec = second[2 + h]
        both = [None] * 4
        for t in (3, 2, 1, 0):
            both[t] = held[t] + vec
            if t:
                vec = row[t][h] * (vec + info[4 + t : 5 + t, 128 * h : 128 * h + 128])
        b_ref[h] = jnp.concatenate(held + both, axis=0)
    x = solve_in_place(t_ref, b_ref, pan_ref, pn_ref, px_ref, bx_ref)
    for h in range(2):
        filtered[:, 128 * h : 128 * h + 128] = x[h][0:4]
        smoothed[:, 128 * h : 128 * h + 128] = x[h][4:8]


def call(kernel, outs, scratch, operands, flops=1e6, away=()):
    return pl.pallas_call(
        kernel,
        out_shape=[jax.ShapeDtypeStruct(s, f32) for s in outs],
        in_specs=[pl.BlockSpec(memory_space=pltpu.SMEM)]
        + [pl.BlockSpec(memory_space=pl.ANY if n in away else pltpu.VMEM) for n in range(1, len(operands))],
        out_specs=[pl.BlockSpec(memory_space=pltpu.VMEM)] * len(outs),
        scratch_shapes=scratch,
        compiler_params=pltpu.CompilerParams(vmem_limit_bytes=VMEM),
        cost_estimate=pl.CostEstimate(flops=int(flops), bytes_accessed=1 << 20, transcendentals=0),
    )(*operands)


def ring(count, shift):
    return [(i, (i + shift) % count) for i in range(count)]


SWAP = [(i, i ^ 1) for i in range(32)]


def body(readings, gap_mask, transfer, channel_weight, pole_site, forget):
    at = scalars()
    parts = [pltpu.VMEM((4, 256, 256), f32)] * 2
    with jax.named_scope("design"):
        design, own, *msgs = call(
            prepare_kernel,
            [(384, 256), (32, 384)] + [(400, 256)] * 3,
            [],
            (at, transfer, pole_site[None], channel_weight[None], gap_mask, readings),
        )
    with jax.named_scope("gather"):
        got = [lax.ppermute(m, "stn", ring(4, o + 1)) for o, m in enumerate(msgs)]
    with jax.named_scope("block"):
        gram, info, totals = call(
            block_kernel,
            [(4, 3, 128, 128), (8, 256), (128, 640)],
            [
                pltpu.VMEM((16, 3, 128, 128), f32),
                pltpu.VMEM((16, 256), f32),
                pltpu.VMEM((3, 128, 128), f32),
                pltpu.VMEM((3, 128, 128), f32),
            ],
            (at, design, own, forget),
            6e9,
        )
    with jax.named_scope("carry"):
        mine = lax.all_to_all(totals, ("tm", "stn"), 0, 0, tiled=True)
    with jax.named_scope("gram"):
        gram, info, *totals = call(
            gram_kernel,
            [(4, 3, 128, 128), (8, 256)] + [(136, 256)] * 3,
            [pltpu.VMEM((4, 3, 128, 128), f32)] + parts + [pltpu.SemaphoreType.DMA(())],
            (at, gram, info, *got, forget),
            2e9,
            away=(1,),
        )
    with jax.named_scope("token"):
        token = lax.ppermute(info, "tm", SWAP)
    with jax.named_scope("quarters"):
        quarters = [lax.ppermute(m, "stn", ring(4, o + 1)) for o, m in enumerate(totals)]
    with jax.named_scope("carry"):
        (entering,) = call(carry_kernel, [(128, 640)], [], (at, mine, token), away=(2,))
        entering = lax.all_to_all(entering, ("tm", "stn"), 0, 0, tiled=True)
    with jax.named_scope("solve"):
        filtered, smoothed = call(
            final_kernel,
            [(4, 256)] * 2,
            [pltpu.VMEM((4, 136, 256), f32)] + SOLVE_SCRATCH,
            (at, entering, *quarters, gram, info, forget),
        )
    return (filtered, smoothed)


def solution(mesh):
    in_specs = (P("tm", "stn"), P("tm", "stn"), P("stn", None), P("stn"), P("stn"), P("tm", None))
    out_specs = (P(("tm", "stn"), None), P(("tm", "stn"), None))
    return jax.shard_map(body, mesh=mesh, in_specs=in_specs, out_specs=out_specs, check_vma=False)
```

```python
import jax
import jax.numpy as jnp
from jax import lax
from jax.experimental import pallas as pl
from jax.experimental.pallas import tpu as pltpu
from jax.sharding import PartitionSpec as P

near_gain = 0.5
ridge = 1.0
VMEM = 24 << 20
PANEL = 16
SUB = 16
PITCH = PANEL + 1
STEPS = 128 // PANEL
f32 = jnp.float32
bf16 = jnp.bfloat16


def split3(x):
    high = x.astype(bf16)
    rest = x - high.astype(f32)
    mid = rest.astype(bf16)
    low = (rest - mid.astype(f32)).astype(bf16)
    return high, mid, low


def inverse(x):
    return pl.reciprocal(x, approx=True)


def spread(rows, lane):
    n = rows.shape[0]
    flat = rows.reshape(n * 8, 128)
    index = jnp.full((n * 8, 128), lane, jnp.int32)
    return jnp.take_along_axis(flat, index, axis=1).reshape(n, 8, 128)


def panel_solve(parts, lane0):
    parts = [[p[SUB * s : SUB * s + SUB] for s in range(PANEL // SUB)] for p in parts]
    for s in range(PANEL // SUB):
        lane = lane0 + SUB * s
        block = parts[0][s]
        e = {}
        for i in range(SUB):
            for j in range(i, SUB):
                e[i, j] = spread(block[i : i + 1], lane + j)[0]
        mult = {}
        for q in range(PANEL // SUB):
            if q != s:
                mult[q] = [spread(parts[0][q], lane + j) for j in range(SUB)]
        low = {}
        dinv = []
        for j in range(SUB):
            d = inverse(e[j, j])
            dinv.append(d)
            for i in range(j + 1, SUB):
                low[i, j] = e[j, i] * d
            for i in range(j + 1, SUB):
                for c in range(i, SUB):
                    e[i, c] = e[i, c] - low[i, j] * e[j, c]
        for p in parts:
            rows = [p[s][i] for i in range(SUB)]
            for j in range(SUB):
                for i in range(j + 1, SUB):
                    rows[i] = rows[i] - low[i, j] * rows[j]
            rows = [rows[j] * dinv[j] for j in range(SUB)]
            for j in range(SUB - 1, 0, -1):
                for i in range(j):
                    rows[i] = rows[i] - low[j, i] * rows[j]
            p[s] = jnp.stack(rows)
            for q in range(PANEL // SUB):
                if q != s:
                    new = p[q]
                    for j in range(SUB):
                        new = new - mult[q][j] * rows[j][None]
                    p[q] = new
    return [jnp.concatenate(p, axis=0) for p in parts]


def solve_in_place(t_ref, b_ref, pan_ref, pn_ref, px_ref, bx_ref):
    def step(k, half):
        row0 = k * PANEL
        lane0 = row0 - 128 * half
        halves = [half] if half else [0, 1]

        for h in halves:
            for m in range(8):
                pan_ref[h, m * PITCH : m * PITCH + PANEL, :] = t_ref[h, pl.ds(m * 256 + row0, PANEL), :]

        def load(h):
            return jnp.stack([pan_ref[h, pl.ds(i, 8, stride=PITCH), :] for i in range(PANEL)])

        original = [load(h) for h in halves]
        vec = b_ref[half]
        right = jnp.stack([spread(vec[None], lane0 + i)[0] for i in range(PANEL)])
        done = panel_solve(original + [right], lane0)
        for h, p in zip(halves, done):
            px_ref[h, pl.ds(row0, PANEL)] = p
            for i in range(PANEL):
                pn_ref[h, pl.ds(i, 8, stride=PITCH), :] = p[i]
        bx_ref[pl.ds(row0, PANEL)] = done[-1]
        for n, h in enumerate(halves):
            b_ref[h] = b_ref[h] - jnp.sum(original[n] * done[-1], axis=0)
        def cat(x, pick):
            pieces = split3(x)
            return jnp.concatenate([pieces[c] for c in pick], axis=0)

        def dot(a, b):
            return lax.dot_general(a, b, (((0,), (0,)), ((), ())), preferred_element_type=f32)

        left = [[cat(t_ref[h, pl.ds(m * 256 + row0, PANEL), :], (0, 0, 0, 1, 1, 2)) for h in halves] for m in range(8)]
        rgt = [[cat(pn_ref[h, m * PITCH : m * PITCH + PANEL, :], (0, 1, 2, 0, 1, 0)) for h in halves] for m in range(8)]
        for m in range(8):
            top = pl.ds(m * 256, 128)
            bottom = pl.ds(m * 256 + 128, 128)
            if half:
                t_ref[1, bottom, :] = t_ref[1, bottom, :] - dot(left[m][0], rgt[m][0])
            else:
                t_ref[0, top, :] = t_ref[0, top, :] - dot(left[m][0], rgt[m][0])
                t_ref[1, top, :] = t_ref[1, top, :] - dot(left[m][0], rgt[m][1])
                t_ref[1, bottom, :] = t_ref[1, bottom, :] - dot(left[m][1], rgt[m][1])

    @pl.loop(0, STEPS)
    def _(k):
        step(k, 0)

    @pl.loop(STEPS, 2 * STEPS)
    def _(k):
        step(k, 1)

    lanes = lax.broadcasted_iota(jnp.int32, (PANEL, 8, 128), 2)
    order = lax.broadcasted_iota(jnp.int32, (PANEL, 8, 128), 0)
    zero = jnp.zeros((8, 128), f32)

    def back(k, x_halves, half):
        row0 = k * PANEL
        total = sum(px_ref[h, pl.ds(row0, PANEL)] * x_halves[h][None] for h in range(half, 2))
        x_new = bx_ref[pl.ds(row0, PANEL)] - jnp.sum(total, axis=2, keepdims=True)
        keep = jnp.where(lanes == order + (row0 - 128 * half), x_new, 0.0)
        add = jnp.sum(keep, axis=0)
        return (x_halves[0] + add, x_halves[1]) if half == 0 else (x_halves[0], x_halves[1] + add)

    x = lax.fori_loop(0, STEPS, lambda n, x: back(2 * STEPS - 1 - n, x, 1), (zero, zero))
    x = lax.fori_loop(0, STEPS, lambda n, x: back(STEPS - 1 - n, x, 0), x)
    return x


SOLVE_SCRATCH = [
    pltpu.VMEM((2, 8 * 256, 128), f32),
    pltpu.VMEM((2, 8, 128), f32),
    pltpu.VMEM((2, 8 * PITCH, 128), f32),
    pltpu.VMEM((2, 8 * PITCH, 128), f32),
    pltpu.VMEM((2, 256, 8, 128), f32),
    pltpu.VMEM((256, 8, 128), f32),
]


def scalars():
    tm = lax.axis_index("tm")
    stn = lax.axis_index("stn")
    return jnp.stack([lax.rem(tm, 2), stn, tm * 4 + stn]).astype(jnp.int32)


def column(row):
    return jnp.broadcast_to(row, (128, 128)).T


def quarter_rows(rows, quarter):
    out = rows[0:4]
    for q in range(1, 4):
        out = jnp.where(quarter == q, rows[4 * q : 4 * q + 4], out)
    return out


def prepare_kernel(at, transfer, site, weight, mask, readings, design, own, msg1, msg2, msg3):
    core, stn = at[0], at[1]
    for c in range(3):
        rows = pl.ds(128 * c, 128)
        root = column(jnp.sqrt(weight[:, 128 * c : 128 * c + 128]))
        where_site = column(site[:, 128 * c : 128 * c + 128].astype(f32))
        for h in range(2):
            pole = lax.broadcasted_iota(jnp.int32, (128, 128), 1).astype(f32) + 128.0 * h
            near = jnp.where(pole == where_site, near_gain, 0.0)
            design[rows, 128 * h : 128 * h + 128] = (transfer[rows, 128 * h : 128 * h + 128] + near) * root
    half = design[pl.ds(192 * core, 192), :]
    masks = mask[...].astype(f32)
    scaled = masks * jnp.sqrt(weight[...]) * readings[...]

    def piece(quarter):
        return jnp.concatenate([quarter_rows(masks, quarter), quarter_rows(scaled, quarter)], axis=0)

    own[0:16, :] = masks
    own[16:32, :] = scaled
    for o, msg in enumerate((msg1, msg2, msg3)):
        rows = piece(lax.rem(stn + (o + 1), 4))
        msg[0:192, :] = half
        msg[192:200, :] = rows[:, 0:256]
        msg[200:208, 0:128] = rows[:, 256:384]
        msg[200:208, 128:256] = jnp.zeros((8, 128), f32)


def decay(forget, quarter):
    rows = quarter_rows(forget, quarter)
    row = [[rows[t : t + 1, 128 * h : 128 * h + 128] for h in range(2)] for t in range(4)]
    col = [[column(row[t][h]) for h in range(2)] for t in range(4)]
    return row, col


BLOCKS = ((0, 0), (0, 1), (1, 1))


def products(x, keeps, extra=None):
    high, mid, low = split3(x)
    turned = x.T
    thigh = turned.astype(bf16)
    tmid = (turned - thigh.astype(f32)).astype(bf16)
    right = jnp.concatenate([high, mid], axis=0), jnp.concatenate([mid, low], axis=0)

    def four(q):
        out = [], []
        for t in range(4):
            keep = keeps[4 * q + t : 4 * q + t + 1, :].astype(bf16)
            a, b = thigh * keep, tmid * keep
            for n, left in enumerate((jnp.concatenate([a, b], axis=1), jnp.concatenate([a, a], axis=1))):
                if t == 3 and extra is not None:
                    left = jnp.concatenate([left, extra[n]], axis=0)
                out[n].append(jnp.dot(left, right[n], preferred_element_type=f32))
        return out

    return four


def add_block(x, rows, even, odd, info, first, fresh=False):
    high, mid, low = (p.astype(f32) for p in split3(rows[4:8, :]))
    blank = jnp.zeros((4, 384), f32)

    def chunk(*quarters):
        return jnp.concatenate(quarters, axis=0).astype(bf16)

    top = chunk(high, blank, blank, blank)
    extra = (
        jnp.concatenate([chunk(high, mid, low, blank), chunk(mid, blank, blank, blank)], axis=1),
        jnp.concatenate([top, top], axis=1),
    )
    same, cross = products(x, rows, extra)(0)
    tail, cross_tail = same[3][256:272], cross[3][256:272]
    part = tail[0:4] + tail[4:8] + tail[8:12] + cross_tail[0:4]
    info[4:8, :] = part if first else info[4:8, :] + part
    for t in range(4):
        even[t] = same[t][0:256] if first or fresh else even[t] + same[t][0:256]
        odd[t] = cross[t][0:256] if first or fresh else odd[t] + cross[t][0:256]


def gram_block(even, odd, t, n):
    i, j = BLOCKS[n]
    rs, cs = slice(128 * i, 128 * i + 128), slice(128 * j, 128 * j + 128)
    return even[t, rs, cs] + (odd[t, rs, cs] + odd[t, cs, rs].T)


def pack(ahead, behind, vec_f, vec_b):
    lanes = lax.broadcasted_iota(jnp.int32, (128, 128), 1)
    rows_at = lax.broadcasted_iota(jnp.int32, (128, 128), 0)
    eye = lanes == rows_at
    lower = lanes <= rows_at
    last = jnp.zeros((128, 128), f32)
    for n, e in enumerate([ahead[1, 1], behind[1, 1], vec_f[0], vec_f[1], vec_b[0], vec_b[1]]):
        last = jnp.where(lanes == n, jnp.sum(jnp.where(eye, e, 0.0), axis=1, keepdims=True), last)
    return (
        (jnp.where(lower, ahead[0, 0], ahead[1, 1]), ahead[0, 1]),
        (jnp.where(lower, behind[0, 0], behind[1, 1]), behind[0, 1]),
        last,
    )


def block_kernel(at, design, own, forget, msg, infos, ahead, behind):
    stn = at[1]
    x = design[...]
    four = products(x, own)
    infos[...] = jnp.dot(own[16:32, :], x, precision=lax.Precision.HIGHEST, preferred_element_type=f32)
    all_row, all_col = None, None
    vec_f, vec_b = [None, None], [None, None]
    for t in range(16):
        if t % 4 == 0:
            all_same, all_cross = four(t // 4)
        same, cross = all_same[t % 4], all_cross[t % 4]
        row = [forget[t : t + 1, 128 * h : 128 * h + 128] for h in range(2)]
        col = [column(r) for r in row]
        all_row = row if t == 0 else [p * q for p, q in zip(all_row, row)]
        all_col = col if t == 0 else [p * q for p, q in zip(all_col, col)]
        for n, (i, j) in enumerate(BLOCKS):
            rs, cs = slice(128 * i, 128 * i + 128), slice(128 * j, 128 * j + 128)
            g = same[rs, cs] + (cross[rs, cs] + cross[cs, rs].T)
            past = (all_col[i] * all_row[j]) * g
            if t == 0:
                ahead[n] = g
                behind[n] = past
            else:
                ahead[n] = (col[i] * row[j]) * ahead[n] + g
                behind[n] += past
        for h in range(2):
            v = infos[t : t + 1, 128 * h : 128 * h + 128]
            vec_f[h] = v if t == 0 else row[h] * vec_f[h] + v
            vec_b[h] = all_row[h] * v if t == 0 else vec_b[h] + all_row[h] * v
    f, b, last = pack(
        {k: ahead[n] for n, k in enumerate(BLOCKS)}, {k: behind[n] for n, k in enumerate(BLOCKS)}, vec_f, vec_b
    )
    wide = [jnp.broadcast_to(r, (128, 128)) for r in all_row]
    share = jnp.where(stn == 1, wide[0], wide[1])
    turned_share = pltpu.roll(jnp.where(stn == 0, wide[0], wide[1]), 64, 1)
    share = jnp.where((stn == 0) | (stn == 2), turned_share, share)
    lanes = lax.broadcasted_iota(jnp.int32, (128, 128), 1)
    for n, part in enumerate((*f, *b, jnp.where(lanes < 64, last, share))):
        msg[:, 128 * n : 128 * n + 128] = part


def early_gram_kernel(at, design, own, gram, info, even, odd):
    stn = at[1]
    info[0:4, :] = jnp.zeros((4, 256), f32)
    rows = jnp.concatenate([quarter_rows(own[0:16, :], stn), quarter_rows(own[16:32, :], stn)], axis=0)
    add_block(design[...], rows, even, odd, info, True)
    for t in range(4):
        for n in range(3):
            gram[t, n] = gram_block(even, odd, t, n)


def gram_kernel(
    at, gram_in, info_in, got1, got2, got3, oth1, oth2, oth3, forget, gram, info, msg1, msg2, msg3, block, even, odd
):
    core, stn = at[0], at[1]
    info[...] = info_in[...]
    for n, (got, oth) in enumerate(((got1, oth1), (got3, oth3), (got2, oth2))):
        block[n, pl.ds(192 * core, 192), :] = got[0:192, :]
        block[n, pl.ds(192 * (1 - core), 192), :] = oth[0:192, :]
        rows = jnp.concatenate([got[192:200, :], got[200:208, 0:128]], axis=1)
        add_block(block[n], rows, even, odd, info, False, n == 0)
    for t in range(4):
        for n in range(3):
            gram[t, n] = gram_in[t, n] + gram_block(even, odd, t, n)
    row, col = decay(forget[...], stn)
    ahead, behind = {}, {}
    for n, (i, j) in enumerate(BLOCKS):
        g = [gram[t, n] for t in range(4)]
        f = [col[t][i] * row[t][j] for t in range(4)]
        acc = g[0]
        for t in range(1, 4):
            acc = f[t] * acc + g[t]
        ahead[i, j] = acc
        acc = f[3] * g[3]
        for t in (2, 1, 0):
            acc = f[t] * (acc + g[t])
        behind[i, j] = acc
    vec_f, vec_b = [], []
    for h in range(2):
        v = [info[4 + t : 5 + t, 128 * h : 128 * h + 128] for t in range(4)]
        f = [row[t][h] for t in range(4)]
        acc = v[0]
        for t in range(1, 4):
            acc = f[t] * acc + v[t]
        vec_f.append(acc)
        acc = f[3] * v[3]
        for t in (2, 1, 0):
            acc = f[t] * (acc + v[t])
        vec_b.append(acc)
    lanes = lax.broadcasted_iota(jnp.int32, (128, 128), 1)
    rows_at = lax.broadcasted_iota(jnp.int32, (128, 128), 0)
    edge = lax.broadcasted_iota(jnp.int32, (8, 128), 0)

    def rows_of(blocks, vec):
        diagonal = jnp.sum(jnp.where(lanes == rows_at, blocks[1, 1], 0.0), axis=0, keepdims=True)
        return (
            jnp.where(lanes <= rows_at, blocks[0, 0], blocks[1, 1]),
            blocks[0, 1],
            jnp.where(edge == 0, vec[0], jnp.where(edge == 1, diagonal, 0.0)),
            jnp.where(edge == 0, vec[1], 0.0),
        )

    f, b = rows_of(ahead, vec_f), rows_of(behind, vec_b)
    for o, msg in enumerate((msg1, msg2, msg3)):
        later = lax.rem(stn + (o + 1), 4) > stn
        for n in range(4):
            rows = slice(128, 136) if n >= 2 else slice(0, 128)
            msg[rows, 128 * (n % 2) : 128 * (n % 2) + 128] = jnp.where(later, f[n], b[n])


def moved(x, n):
    return jnp.concatenate([x[-n:], x[:-n]], axis=0)


def shifted(x, n, fill, up):
    edge = jnp.full((n, x.shape[1]), fill, f32)
    if up:
        return jnp.concatenate([x[n:], edge], axis=0)
    return jnp.concatenate([edge, x[:-n]], axis=0)


def running(gain, value, up):
    n = 4
    while n < 128:
        value = value + gain * shifted(value, n, 0.0, up)
        if n < 64:
            gain = gain * shifted(gain, n, 1.0, up)
        n *= 2
    value = shifted(value, 4, 0.0, up)
    rows_at = lax.broadcasted_iota(jnp.int32, (128, 128), 0)
    value = jnp.where(lax.rem(rows_at, 4) == 0, value, 0.0)
    value = value + moved(value, 1)
    return value + moved(value, 2)


def carry_kernel(at, got, token, out):
    place = at[2]
    lanes = lax.broadcasted_iota(jnp.int32, (128, 128), 1)
    last = got[:, 512:640]
    swapped = pltpu.roll(last, 64, 1)
    low = jnp.where(lanes < 64, swapped, moved(last, -1))
    high = jnp.where(lanes < 64, moved(swapped, -2), moved(last, -3))
    here = lanes == place
    at_low = jnp.sum(jnp.where(here, low, 0.0), axis=1, keepdims=True)
    at_high = jnp.sum(jnp.where(here, high, 0.0), axis=1, keepdims=True)
    extra = jnp.where(lanes < 2, at_high * at_high, jnp.where((lanes == 2) | (lanes == 4), at_low, at_high))
    gain = [jnp.where(lanes <= place, at_low * low, at_high * high), at_low * high, extra]

    def total(x):
        x = x + moved(x, -1)
        return x + moved(x, -2)

    last = total(jnp.where(lanes < 6, last, 0.0))
    enter = [running(g, v, False) for g, v in zip(gain, (total(got[:, 0:128]), total(got[:, 128:256]), last))]
    leave = [running(g, v, True) for g, v in zip(gain, (total(got[:, 256:384]), total(got[:, 384:512]), last))]
    ahead_lane = (lanes == 0) | (lanes == 2) | (lanes == 3)
    parts = (enter[0], enter[1], leave[0], leave[1], jnp.where(ahead_lane, enter[2], leave[2]))
    for n, part in enumerate(parts):
        out[:, 128 * n : 128 * n + 128] = part


def final_kernel(
    at, got, quarter1, quarter2, quarter3, gram, info, forget, filtered, smoothed, quarters,
    t_ref, b_ref, pan_ref, pn_ref, px_ref, bx_ref,
):
    stn = at[1]
    lanes = lax.broadcasted_iota(jnp.int32, (128, 128), 1)
    rows_at = lax.broadcasted_iota(jnp.int32, (128, 128), 0)
    eye = lanes == rows_at
    lower = lanes <= rows_at
    unit = jnp.where(eye, ridge, 0.0)
    for o, quarter in enumerate((quarter1, quarter2, quarter3)):
        quarters[lax.rem(stn + (3 - o), 4)] = quarter[...]
    last = got[:, 512:640]

    def lane_row(n):
        col = jnp.sum(jnp.where(lanes == n, last, 0.0), axis=1, keepdims=True)
        return jnp.sum(jnp.where(eye, col, 0.0), axis=0, keepdims=True)

    first = [got[:, 0:128], got[:, 128:256], lane_row(2), lane_row(3), lane_row(0)]
    second = [got[:, 256:384], got[:, 384:512], lane_row(4), lane_row(5), lane_row(1)]

    def past_quarter(q, state, use):
        gain = forget[4 * q : 4 * q + 1, :]
        for t in range(1, 4):
            gain = gain * forget[4 * q + t : 4 * q + t + 1, :]
        low, high = gain[:, 0:128], gain[:, 128:256]
        clow, chigh = column(low), column(high)
        gains = (jnp.where(lower, clow * low, chigh * high), clow * high, low, high, high * high)
        own = (
            quarters[q, 0:128, 0:128],
            quarters[q, 0:128, 128:256],
            quarters[q, 128:129, 0:128],
            quarters[q, 128:129, 128:256],
            quarters[q, 129:130, 0:128],
        )
        return [jnp.where(use, g * v + w, v) for g, v, w in zip(gains, state, own)]

    for q in (0, 1, 2):
        first = past_quarter(q, first, q < stn)
    for q in (3, 2, 1):
        second = past_quarter(q, second, q > stn)

    def unpack(state):
        packed = state[0]
        turned = packed.T
        one = jnp.where(lower, packed, turned)
        two = jnp.where(eye, state[4], jnp.where(lower, turned, packed))
        return {(0, 0): one, (0, 1): state[1], (1, 1): two}

    ahead = unpack(first)
    behind = unpack(second)
    row, col = decay(forget[...], stn)
    for n, (i, j) in enumerate(BLOCKS):
        f = [col[t][i] * row[t][j] for t in range(4)]
        acc = ahead[i, j]
        held = []
        for t in range(4):
            acc = f[t] * acc + gram[t, n]
            full = acc + unit if i == j else acc
            held.append(full)
            t_ref[j, 256 * t + 128 * i : 256 * t + 128 * i + 128, :] = full
        acc = behind[i, j]
        for t in (3, 2, 1, 0):
            at_row = 256 * (4 + t) + 128 * i
            t_ref[j, at_row : at_row + 128, :] = held[t] + acc
            if t:
                acc = f[t] * (acc + gram[t, n])
    for h in range(2):
        vec = first[2 + h]
        held = []
        for t in range(4):
            vec = row[t][h] * vec + info[4 + t : 5 + t, 128 * h : 128 * h + 128]
            held.append(vec)
        vec = second[2 + h]
        both = [None] * 4
        for t in (3, 2, 1, 0):
            both[t] = held[t] + vec
            if t:
                vec = row[t][h] * (vec + info[4 + t : 5 + t, 128 * h : 128 * h + 128])
        b_ref[h] = jnp.concatenate(held + both, axis=0)
    x = solve_in_place(t_ref, b_ref, pan_ref, pn_ref, px_ref, bx_ref)
    for h in range(2):
        filtered[:, 128 * h : 128 * h + 128] = x[h][0:4]
        smoothed[:, 128 * h : 128 * h + 128] = x[h][4:8]


def call(kernel, outs, scratch, operands, flops=1e6, away=()):
    return pl.pallas_call(
        kernel,
        out_shape=[jax.ShapeDtypeStruct(s, f32) for s in outs],
        in_specs=[pl.BlockSpec(memory_space=pltpu.SMEM)]
        + [pl.BlockSpec(memory_space=pl.ANY if n in away else pltpu.VMEM) for n in range(1, len(operands))],
        out_specs=[pl.BlockSpec(memory_space=pltpu.VMEM)] * len(outs),
        scratch_shapes=scratch,
        compiler_params=pltpu.CompilerParams(vmem_limit_bytes=VMEM),
        cost_estimate=pl.CostEstimate(flops=int(flops), bytes_accessed=1 << 20, transcendentals=0),
    )(*operands)


def ring(count, shift):
    return [(i, (i + shift) % count) for i in range(count)]


SWAP = [(i, i ^ 1) for i in range(32)]


def body(readings, gap_mask, transfer, channel_weight, pole_site, forget):
    at = scalars()
    parts = [pltpu.VMEM((4, 256, 256), f32)] * 2
    with jax.named_scope("design"):
        design, own, *msgs = call(
            prepare_kernel,
            [(384, 256), (32, 384)] + [(208, 256)] * 3,
            [],
            (at, transfer, pole_site[None], channel_weight[None], gap_mask, readings),
        )
    with jax.named_scope("gather"):
        got = [lax.ppermute(m, "stn", ring(4, o + 1)) for o, m in enumerate(msgs)]
    with jax.named_scope("block"):
        (totals,) = call(
            block_kernel,
            [(128, 640)],
            [
                pltpu.VMEM((16, 256), f32),
                pltpu.VMEM((3, 128, 128), f32),
                pltpu.VMEM((3, 128, 128), f32),
            ],
            (at, design, own, forget),
            6e9,
        )
    with jax.named_scope("carry"):
        mine = lax.all_to_all(totals, ("tm", "stn"), 0, 0, tiled=True)
    with jax.named_scope("swap"):
        other = [lax.ppermute(g, "tm", SWAP) for g in got]
    with jax.named_scope("early_gram"):
        gram, info = call(early_gram_kernel, [(4, 3, 128, 128), (8, 256)], parts, (at, design, own), 2e10)
    with jax.named_scope("gram"):
        gram, info, *totals = call(
            gram_kernel,
            [(4, 3, 128, 128), (8, 256)] + [(136, 256)] * 3,
            [pltpu.VMEM((3, 384, 256), f32)] + parts,
            (at, gram, info, *got, *other, forget),
            2e9,
        )
    with jax.named_scope("token"):
        token = lax.ppermute(info, "tm", SWAP)
    with jax.named_scope("quarters"):
        quarters = [lax.ppermute(m, "stn", ring(4, o + 1)) for o, m in enumerate(totals)]
    with jax.named_scope("carry"):
        (entering,) = call(carry_kernel, [(128, 640)], [], (at, mine, token), away=(2,))
        entering = lax.all_to_all(entering, ("tm", "stn"), 0, 0, tiled=True)
    with jax.named_scope("solve"):
        filtered, smoothed = call(
            final_kernel,
            [(4, 256)] * 2,
            [pltpu.VMEM((4, 136, 256), f32)] + SOLVE_SCRATCH,
            (at, entering, *quarters, gram, info, forget),
        )
    return (filtered, smoothed)


def solution(mesh):
    in_specs = (P("tm", "stn"), P("tm", "stn"), P("stn", None), P("stn"), P("stn"), P("tm", None))
    out_specs = (P(("tm", "stn"), None), P(("tm", "stn"), None))
    return jax.shard_map(body, mesh=mesh, in_specs=in_specs, out_specs=out_specs, check_vma=False)
```

```python
import jax
import jax.numpy as jnp
from jax import lax
from jax.experimental import pallas as pl
from jax.experimental.pallas import tpu as pltpu
from jax.sharding import PartitionSpec as P

near_gain = 0.5
ridge = 1.0
VMEM = 24 << 20
PANEL = 16
SUB = 16
PITCH = PANEL + 1
STEPS = 128 // PANEL
f32 = jnp.float32
bf16 = jnp.bfloat16


def split3(x):
    high = x.astype(bf16)
    rest = x - high.astype(f32)
    mid = rest.astype(bf16)
    low = (rest - mid.astype(f32)).astype(bf16)
    return high, mid, low


def inverse(x):
    return pl.reciprocal(x, approx=True)


def spread(rows, lane):
    n = rows.shape[0]
    flat = rows.reshape(n * 8, 128)
    index = jnp.full((n * 8, 128), lane, jnp.int32)
    return jnp.take_along_axis(flat, index, axis=1).reshape(n, 8, 128)


def panel_solve(parts, lane0):
    parts = [[p[SUB * s : SUB * s + SUB] for s in range(PANEL // SUB)] for p in parts]
    for s in range(PANEL // SUB):
        lane = lane0 + SUB * s
        block = parts[0][s]
        e = {}
        for i in range(SUB):
            for j in range(i, SUB):
                e[i, j] = spread(block[i : i + 1], lane + j)[0]
        mult = {}
        for q in range(PANEL // SUB):
            if q != s:
                mult[q] = [spread(parts[0][q], lane + j) for j in range(SUB)]
        low = {}
        dinv = []
        for j in range(SUB):
            d = inverse(e[j, j])
            dinv.append(d)
            for i in range(j + 1, SUB):
                low[i, j] = e[j, i] * d
            for i in range(j + 1, SUB):
                for c in range(i, SUB):
                    e[i, c] = e[i, c] - low[i, j] * e[j, c]
        for p in parts:
            rows = [p[s][i] for i in range(SUB)]
            for j in range(SUB):
                for i in range(j + 1, SUB):
                    rows[i] = rows[i] - low[i, j] * rows[j]
            rows = [rows[j] * dinv[j] for j in range(SUB)]
            for j in range(SUB - 1, 0, -1):
                for i in range(j):
                    rows[i] = rows[i] - low[j, i] * rows[j]
            p[s] = jnp.stack(rows)
            for q in range(PANEL // SUB):
                if q != s:
                    new = p[q]
                    for j in range(SUB):
                        new = new - mult[q][j] * rows[j][None]
                    p[q] = new
    return [jnp.concatenate(p, axis=0) for p in parts]


def solve_in_place(t_ref, b_ref, pan_ref, pn_ref, px_ref, bx_ref):
    def step(k, half):
        row0 = k * PANEL
        lane0 = row0 - 128 * half
        halves = [half] if half else [0, 1]

        for h in halves:
            for m in range(8):
                pan_ref[h, m * PITCH : m * PITCH + PANEL, :] = t_ref[h, pl.ds(m * 256 + row0, PANEL), :]

        def load(h):
            return jnp.stack([pan_ref[h, pl.ds(i, 8, stride=PITCH), :] for i in range(PANEL)])

        original = [load(h) for h in halves]
        vec = b_ref[half]
        right = jnp.stack([spread(vec[None], lane0 + i)[0] for i in range(PANEL)])
        done = panel_solve(original + [right], lane0)
        for h, p in zip(halves, done):
            px_ref[h, pl.ds(row0, PANEL)] = p
            for i in range(PANEL):
                pn_ref[h, pl.ds(i, 8, stride=PITCH), :] = p[i]
        bx_ref[pl.ds(row0, PANEL)] = done[-1]
        for n, h in enumerate(halves):
            b_ref[h] = b_ref[h] - jnp.sum(original[n] * done[-1], axis=0)
        def cat(x, pick):
            pieces = split3(x)
            return jnp.concatenate([pieces[c] for c in pick], axis=0)

        def dot(a, b):
            return lax.dot_general(a, b, (((0,), (0,)), ((), ())), preferred_element_type=f32)

        left = [[cat(t_ref[h, pl.ds(m * 256 + row0, PANEL), :], (0, 0, 0, 1, 1, 2)) for h in halves] for m in range(8)]
        rgt = [[cat(pn_ref[h, m * PITCH : m * PITCH + PANEL, :], (0, 1, 2, 0, 1, 0)) for h in halves] for m in range(8)]
        for m in range(8):
            top = pl.ds(m * 256, 128)
            bottom = pl.ds(m * 256 + 128, 128)
            if half:
                t_ref[1, bottom, :] = t_ref[1, bottom, :] - dot(left[m][0], rgt[m][0])
            else:
                t_ref[0, top, :] = t_ref[0, top, :] - dot(left[m][0], rgt[m][0])
                t_ref[1, top, :] = t_ref[1, top, :] - dot(left[m][0], rgt[m][1])
                t_ref[1, bottom, :] = t_ref[1, bottom, :] - dot(left[m][1], rgt[m][1])

    @pl.loop(0, STEPS)
    def _(k):
        step(k, 0)

    @pl.loop(STEPS, 2 * STEPS)
    def _(k):
        step(k, 1)

    lanes = lax.broadcasted_iota(jnp.int32, (PANEL, 8, 128), 2)
    order = lax.broadcasted_iota(jnp.int32, (PANEL, 8, 128), 0)
    zero = jnp.zeros((8, 128), f32)

    def back(k, x_halves, half):
        row0 = k * PANEL
        total = sum(px_ref[h, pl.ds(row0, PANEL)] * x_halves[h][None] for h in range(half, 2))
        x_new = bx_ref[pl.ds(row0, PANEL)] - jnp.sum(total, axis=2, keepdims=True)
        keep = jnp.where(lanes == order + (row0 - 128 * half), x_new, 0.0)
        add = jnp.sum(keep, axis=0)
        return (x_halves[0] + add, x_halves[1]) if half == 0 else (x_halves[0], x_halves[1] + add)

    x = lax.fori_loop(0, STEPS, lambda n, x: back(2 * STEPS - 1 - n, x, 1), (zero, zero))
    x = lax.fori_loop(0, STEPS, lambda n, x: back(STEPS - 1 - n, x, 0), x)
    return x


SOLVE_SCRATCH = [
    pltpu.VMEM((2, 8 * 256, 128), f32),
    pltpu.VMEM((2, 8, 128), f32),
    pltpu.VMEM((2, 8 * PITCH, 128), f32),
    pltpu.VMEM((2, 8 * PITCH, 128), f32),
    pltpu.VMEM((2, 256, 8, 128), f32),
    pltpu.VMEM((256, 8, 128), f32),
]


def scalars():
    tm = lax.axis_index("tm")
    stn = lax.axis_index("stn")
    return jnp.stack([lax.rem(tm, 2), stn, tm * 4 + stn]).astype(jnp.int32)


def column(row):
    return jnp.broadcast_to(row, (128, 128)).T


def quarter_rows(rows, quarter):
    out = rows[0:4]
    for q in range(1, 4):
        out = jnp.where(quarter == q, rows[4 * q : 4 * q + 4], out)
    return out


def prepare_kernel(at, transfer, site, weight, mask, readings, design, own, msg1, msg2, msg3):
    core, stn = at[0], at[1]
    for c in range(3):
        rows = pl.ds(128 * c, 128)
        root = column(jnp.sqrt(weight[:, 128 * c : 128 * c + 128]))
        where_site = column(site[:, 128 * c : 128 * c + 128].astype(f32))
        for h in range(2):
            pole = lax.broadcasted_iota(jnp.int32, (128, 128), 1).astype(f32) + 128.0 * h
            near = jnp.where(pole == where_site, near_gain, 0.0)
            design[rows, 128 * h : 128 * h + 128] = (transfer[rows, 128 * h : 128 * h + 128] + near) * root
    half = design[pl.ds(192 * core, 192), :]
    masks = mask[...].astype(f32)
    scaled = masks * jnp.sqrt(weight[...]) * readings[...]

    def piece(quarter):
        return jnp.concatenate([quarter_rows(masks, quarter), quarter_rows(scaled, quarter)], axis=0)

    own[0:16, :] = masks
    own[16:32, :] = scaled
    for o, msg in enumerate((msg1, msg2, msg3)):
        rows = piece(lax.rem(stn + (o + 1), 4))
        msg[0:192, :] = half
        msg[192:200, :] = rows[:, 0:256]
        msg[200:208, 0:128] = rows[:, 256:384]
        msg[200:208, 128:256] = jnp.zeros((8, 128), f32)


def decay(forget, quarter):
    rows = quarter_rows(forget, quarter)
    row = [[rows[t : t + 1, 128 * h : 128 * h + 128] for h in range(2)] for t in range(4)]
    col = [[column(row[t][h]) for h in range(2)] for t in range(4)]
    return row, col


BLOCKS = ((0, 0), (0, 1), (1, 1))


def products(x, keeps, extra=None):
    high, mid, low = split3(x)
    turned = x.T
    thigh = turned.astype(bf16)
    tmid = (turned - thigh.astype(f32)).astype(bf16)
    right = jnp.concatenate([high, mid], axis=0), jnp.concatenate([mid, low], axis=0)

    def four(q):
        out = [], []
        for t in range(4):
            keep = keeps[4 * q + t : 4 * q + t + 1, :].astype(bf16)
            a, b = thigh * keep, tmid * keep
            for n, left in enumerate((jnp.concatenate([a, b], axis=1), jnp.concatenate([a, a], axis=1))):
                if t == 3 and extra is not None:
                    left = jnp.concatenate([left, extra[n]], axis=0)
                out[n].append(jnp.dot(left, right[n], preferred_element_type=f32))
        return out

    return four


def add_block(x, rows, even, odd, info, first, fresh=False):
    high, mid, low = (p.astype(f32) for p in split3(rows[4:8, :]))
    blank = jnp.zeros((4, 384), f32)

    def chunk(*quarters):
        return jnp.concatenate(quarters, axis=0).astype(bf16)

    top = chunk(high, blank, blank, blank)
    extra = (
        jnp.concatenate([chunk(high, mid, low, blank), chunk(mid, blank, blank, blank)], axis=1),
        jnp.concatenate([top, top], axis=1),
    )
    same, cross = products(x, rows, extra)(0)
    tail, cross_tail = same[3][256:272], cross[3][256:272]
    part = tail[0:4] + tail[4:8] + tail[8:12] + cross_tail[0:4]
    info[4:8, :] = part if first else info[4:8, :] + part
    for t in range(4):
        even[t] = same[t][0:256] if first or fresh else even[t] + same[t][0:256]
        odd[t] = cross[t][0:256] if first or fresh else odd[t] + cross[t][0:256]


def gram_block(even, odd, t, n):
    i, j = BLOCKS[n]
    rs, cs = slice(128 * i, 128 * i + 128), slice(128 * j, 128 * j + 128)
    return even[t, rs, cs] + (odd[t, rs, cs] + odd[t, cs, rs].T)


def part_of(message, n):
    return message.at[pl.ds(n, 128, stride=5), :]


def pack(ahead, behind, vec_f, vec_b):
    lanes = lax.broadcasted_iota(jnp.int32, (128, 128), 1)
    rows_at = lax.broadcasted_iota(jnp.int32, (128, 128), 0)
    eye = lanes == rows_at
    lower = lanes <= rows_at
    last = jnp.zeros((128, 128), f32)
    for n, e in enumerate([ahead[1, 1], behind[1, 1], vec_f[0], vec_f[1], vec_b[0], vec_b[1]]):
        last = jnp.where(lanes == n, jnp.sum(jnp.where(eye, e, 0.0), axis=1, keepdims=True), last)
    return (
        (jnp.where(lower, ahead[0, 0], ahead[1, 1]), ahead[0, 1]),
        (jnp.where(lower, behind[0, 0], behind[1, 1]), behind[0, 1]),
        last,
    )


def block_kernel(at, design, own, forget, msg, infos, ahead, behind):
    stn = at[1]
    x = design[...]
    four = products(x, own)
    infos[...] = jnp.dot(own[16:32, :], x, precision=lax.Precision.HIGHEST, preferred_element_type=f32)
    all_row, all_col = None, None
    vec_f, vec_b = [None, None], [None, None]
    for t in range(16):
        if t % 4 == 0:
            all_same, all_cross = four(t // 4)
        same, cross = all_same[t % 4], all_cross[t % 4]
        row = [forget[t : t + 1, 128 * h : 128 * h + 128] for h in range(2)]
        col = [column(r) for r in row]
        all_row = row if t == 0 else [p * q for p, q in zip(all_row, row)]
        all_col = col if t == 0 else [p * q for p, q in zip(all_col, col)]
        for n, (i, j) in enumerate(BLOCKS):
            rs, cs = slice(128 * i, 128 * i + 128), slice(128 * j, 128 * j + 128)
            g = same[rs, cs] + (cross[rs, cs] + cross[cs, rs].T)
            past = (all_col[i] * all_row[j]) * g
            if t == 0:
                ahead[n] = g
                behind[n] = past
            else:
                ahead[n] = (col[i] * row[j]) * ahead[n] + g
                behind[n] += past
        for h in range(2):
            v = infos[t : t + 1, 128 * h : 128 * h + 128]
            vec_f[h] = v if t == 0 else row[h] * vec_f[h] + v
            vec_b[h] = all_row[h] * v if t == 0 else vec_b[h] + all_row[h] * v
    f, b, last = pack(
        {k: ahead[n] for n, k in enumerate(BLOCKS)}, {k: behind[n] for n, k in enumerate(BLOCKS)}, vec_f, vec_b
    )
    wide = [jnp.broadcast_to(r, (128, 128)) for r in all_row]
    share = jnp.where(stn == 1, wide[0], wide[1])
    turned_share = pltpu.roll(jnp.where(stn == 0, wide[0], wide[1]), 64, 1)
    share = jnp.where((stn == 0) | (stn == 2), turned_share, share)
    lanes = lax.broadcasted_iota(jnp.int32, (128, 128), 1)
    for n, part in enumerate((*f, *b, jnp.where(lanes < 64, last, share))):
        part_of(msg, n)[...] = part


def early_gram_kernel(at, design, own, gram, info, even, odd):
    stn = at[1]
    info[0:4, :] = jnp.zeros((4, 256), f32)
    rows = jnp.concatenate([quarter_rows(own[0:16, :], stn), quarter_rows(own[16:32, :], stn)], axis=0)
    add_block(design[...], rows, even, odd, info, True)
    for t in range(4):
        for n in range(3):
            gram[t, n] = gram_block(even, odd, t, n)


def gram_kernel(
    at, gram_in, info_in, got1, got2, got3, oth1, oth2, oth3, forget, gram, info, msg1, msg2, msg3, block, even, odd
):
    core, stn = at[0], at[1]
    info[...] = info_in[...]
    for n, (got, oth) in enumerate(((got1, oth1), (got3, oth3), (got2, oth2))):
        block[n, pl.ds(192 * core, 192), :] = got[0:192, :]
        block[n, pl.ds(192 * (1 - core), 192), :] = oth[0:192, :]
        rows = jnp.concatenate([got[192:200, :], got[200:208, 0:128]], axis=1)
        add_block(block[n], rows, even, odd, info, False, n == 0)
    for t in range(4):
        for n in range(3):
            gram[t, n] = gram_in[t, n] + gram_block(even, odd, t, n)
    row, col = decay(forget[...], stn)
    ahead, behind = {}, {}
    for n, (i, j) in enumerate(BLOCKS):
        g = [gram[t, n] for t in range(4)]
        f = [col[t][i] * row[t][j] for t in range(4)]
        acc = g[0]
        for t in range(1, 4):
            acc = f[t] * acc + g[t]
        ahead[i, j] = acc
        acc = f[3] * g[3]
        for t in (2, 1, 0):
            acc = f[t] * (acc + g[t])
        behind[i, j] = acc
    vec_f, vec_b = [], []
    for h in range(2):
        v = [info[4 + t : 5 + t, 128 * h : 128 * h + 128] for t in range(4)]
        f = [row[t][h] for t in range(4)]
        acc = v[0]
        for t in range(1, 4):
            acc = f[t] * acc + v[t]
        vec_f.append(acc)
        acc = f[3] * v[3]
        for t in (2, 1, 0):
            acc = f[t] * (acc + v[t])
        vec_b.append(acc)
    lanes = lax.broadcasted_iota(jnp.int32, (128, 128), 1)
    rows_at = lax.broadcasted_iota(jnp.int32, (128, 128), 0)
    edge = lax.broadcasted_iota(jnp.int32, (8, 128), 0)

    def rows_of(blocks, vec):
        diagonal = jnp.sum(jnp.where(lanes == rows_at, blocks[1, 1], 0.0), axis=0, keepdims=True)
        return (
            jnp.where(lanes <= rows_at, blocks[0, 0], blocks[1, 1]),
            blocks[0, 1],
            jnp.where(edge == 0, vec[0], jnp.where(edge == 1, diagonal, 0.0)),
            jnp.where(edge == 0, vec[1], 0.0),
        )

    f, b = rows_of(ahead, vec_f), rows_of(behind, vec_b)
    for o, msg in enumerate((msg1, msg2, msg3)):
        later = lax.rem(stn + (o + 1), 4) > stn
        for n in range(4):
            rows = slice(128, 136) if n >= 2 else slice(0, 128)
            msg[rows, 128 * (n % 2) : 128 * (n % 2) + 128] = jnp.where(later, f[n], b[n])


def moved(x, n):
    return jnp.concatenate([x[-n:], x[:-n]], axis=0)


def shifted(x, n, fill, up):
    edge = jnp.full((n, x.shape[1]), fill, f32)
    if up:
        return jnp.concatenate([x[n:], edge], axis=0)
    return jnp.concatenate([edge, x[:-n]], axis=0)


def running(gain, value, up):
    n = 4
    while n < 128:
        value = value + gain * shifted(value, n, 0.0, up)
        if n < 64:
            gain = gain * shifted(gain, n, 1.0, up)
        n *= 2
    value = shifted(value, 4, 0.0, up)
    rows_at = lax.broadcasted_iota(jnp.int32, (128, 128), 0)
    value = jnp.where(lax.rem(rows_at, 4) == 0, value, 0.0)
    value = value + moved(value, 1)
    return value + moved(value, 2)


def carry_kernel(at, got, token, out):
    place = at[2]
    lanes = lax.broadcasted_iota(jnp.int32, (128, 128), 1)
    got = [part_of(got, n)[...] for n in range(5)]
    last = got[4]
    swapped = pltpu.roll(last, 64, 1)
    low = jnp.where(lanes < 64, swapped, moved(last, -1))
    high = jnp.where(lanes < 64, moved(swapped, -2), moved(last, -3))
    here = lanes == place
    at_low = jnp.sum(jnp.where(here, low, 0.0), axis=1, keepdims=True)
    at_high = jnp.sum(jnp.where(here, high, 0.0), axis=1, keepdims=True)
    extra = jnp.where(lanes < 2, at_high * at_high, jnp.where((lanes == 2) | (lanes == 4), at_low, at_high))
    gain = [jnp.where(lanes <= place, at_low * low, at_high * high), at_low * high, extra]

    def total(x):
        x = x + moved(x, -1)
        return x + moved(x, -2)

    last = total(jnp.where(lanes < 6, last, 0.0))
    enter = [running(g, v, False) for g, v in zip(gain, (total(got[0]), total(got[1]), last))]
    leave = [running(g, v, True) for g, v in zip(gain, (total(got[2]), total(got[3]), last))]
    ahead_lane = (lanes == 0) | (lanes == 2) | (lanes == 3)
    parts = (enter[0], enter[1], leave[0], leave[1], jnp.where(ahead_lane, enter[2], leave[2]))
    for n, part in enumerate(parts):
        part_of(out, n)[...] = part


def final_kernel(
    at, got, quarter1, quarter2, quarter3, gram, info, forget, filtered, smoothed, quarters,
    t_ref, b_ref, pan_ref, pn_ref, px_ref, bx_ref,
):
    stn = at[1]
    lanes = lax.broadcasted_iota(jnp.int32, (128, 128), 1)
    rows_at = lax.broadcasted_iota(jnp.int32, (128, 128), 0)
    eye = lanes == rows_at
    lower = lanes <= rows_at
    unit = jnp.where(eye, ridge, 0.0)
    for o, quarter in enumerate((quarter1, quarter2, quarter3)):
        quarters[lax.rem(stn + (3 - o), 4)] = quarter[...]
    got = [part_of(got, n)[...] for n in range(5)]
    last = got[4]

    def lane_row(n):
        col = jnp.sum(jnp.where(lanes == n, last, 0.0), axis=1, keepdims=True)
        return jnp.sum(jnp.where(eye, col, 0.0), axis=0, keepdims=True)

    first = [got[0], got[1], lane_row(2), lane_row(3), lane_row(0)]
    second = [got[2], got[3], lane_row(4), lane_row(5), lane_row(1)]

    def past_quarter(q, state, use):
        gain = forget[4 * q : 4 * q + 1, :]
        for t in range(1, 4):
            gain = gain * forget[4 * q + t : 4 * q + t + 1, :]
        low, high = gain[:, 0:128], gain[:, 128:256]
        clow, chigh = column(low), column(high)
        gains = (jnp.where(lower, clow * low, chigh * high), clow * high, low, high, high * high)
        own = (
            quarters[q, 0:128, 0:128],
            quarters[q, 0:128, 128:256],
            quarters[q, 128:129, 0:128],
            quarters[q, 128:129, 128:256],
            quarters[q, 129:130, 0:128],
        )
        return [jnp.where(use, g * v + w, v) for g, v, w in zip(gains, state, own)]

    for q in (0, 1, 2):
        first = past_quarter(q, first, q < stn)
    for q in (3, 2, 1):
        second = past_quarter(q, second, q > stn)

    def unpack(state):
        packed = state[0]
        turned = packed.T
        one = jnp.where(lower, packed, turned)
        two = jnp.where(eye, state[4], jnp.where(lower, turned, packed))
        return {(0, 0): one, (0, 1): state[1], (1, 1): two}

    ahead = unpack(first)
    behind = unpack(second)
    row, col = decay(forget[...], stn)
    for n, (i, j) in enumerate(BLOCKS):
        f = [col[t][i] * row[t][j] for t in range(4)]
        acc = ahead[i, j]
        held = []
        for t in range(4):
            acc = f[t] * acc + gram[t, n]
            full = acc + unit if i == j else acc
            held.append(full)
            t_ref[j, 256 * t + 128 * i : 256 * t + 128 * i + 128, :] = full
        acc = behind[i, j]
        for t in (3, 2, 1, 0):
            at_row = 256 * (4 + t) + 128 * i
            t_ref[j, at_row : at_row + 128, :] = held[t] + acc
            if t:
                acc = f[t] * (acc + gram[t, n])
    for h in range(2):
        vec = first[2 + h]
        held = []
        for t in range(4):
            vec = row[t][h] * vec + info[4 + t : 5 + t, 128 * h : 128 * h + 128]
            held.append(vec)
        vec = second[2 + h]
        both = [None] * 4
        for t in (3, 2, 1, 0):
            both[t] = held[t] + vec
            if t:
                vec = row[t][h] * (vec + info[4 + t : 5 + t, 128 * h : 128 * h + 128])
        b_ref[h] = jnp.concatenate(held + both, axis=0)
    x = solve_in_place(t_ref, b_ref, pan_ref, pn_ref, px_ref, bx_ref)
    for h in range(2):
        filtered[:, 128 * h : 128 * h + 128] = x[h][0:4]
        smoothed[:, 128 * h : 128 * h + 128] = x[h][4:8]


def call(kernel, outs, scratch, operands, flops=1e6, away=()):
    return pl.pallas_call(
        kernel,
        out_shape=[jax.ShapeDtypeStruct(s, f32) for s in outs],
        in_specs=[pl.BlockSpec(memory_space=pltpu.SMEM)]
        + [pl.BlockSpec(memory_space=pl.ANY if n in away else pltpu.VMEM) for n in range(1, len(operands))],
        out_specs=[pl.BlockSpec(memory_space=pltpu.VMEM)] * len(outs),
        scratch_shapes=scratch,
        compiler_params=pltpu.CompilerParams(vmem_limit_bytes=VMEM),
        cost_estimate=pl.CostEstimate(flops=int(flops), bytes_accessed=1 << 20, transcendentals=0),
    )(*operands)


def ring(count, shift):
    return [(i, (i + shift) % count) for i in range(count)]


SWAP = [(i, i ^ 1) for i in range(32)]


def exchange(message):
    out = lax.all_to_all(message.reshape(128, 1, 640), ("tm", "stn"), 0, 0, tiled=True)
    return out.reshape(640, 128)


def body(readings, gap_mask, transfer, channel_weight, pole_site, forget):
    at = scalars()
    parts = [pltpu.VMEM((4, 256, 256), f32)] * 2
    with jax.named_scope("design"):
        design, own, *msgs = call(
            prepare_kernel,
            [(384, 256), (32, 384)] + [(208, 256)] * 3,
            [],
            (at, transfer, pole_site[None], channel_weight[None], gap_mask, readings),
        )
    with jax.named_scope("gather"):
        got = [lax.ppermute(m, "stn", ring(4, o + 1)) for o, m in enumerate(msgs)]
    with jax.named_scope("block"):
        (totals,) = call(
            block_kernel,
            [(640, 128)],
            [
                pltpu.VMEM((16, 256), f32),
                pltpu.VMEM((3, 128, 128), f32),
                pltpu.VMEM((3, 128, 128), f32),
            ],
            (at, design, own, forget),
            6e9,
        )
    with jax.named_scope("carry"):
        mine = exchange(totals)
    with jax.named_scope("swap"):
        other = [lax.ppermute(g, "tm", SWAP) for g in got]
    with jax.named_scope("early_gram"):
        gram, info = call(early_gram_kernel, [(4, 3, 128, 128), (8, 256)], parts, (at, design, own), 2e10)
    with jax.named_scope("gram"):
        gram, info, *totals = call(
            gram_kernel,
            [(4, 3, 128, 128), (8, 256)] + [(136, 256)] * 3,
            [pltpu.VMEM((3, 384, 256), f32)] + parts,
            (at, gram, info, *got, *other, forget),
            2e9,
        )
    with jax.named_scope("token"):
        token = lax.ppermute(info, "tm", SWAP)
    with jax.named_scope("quarters"):
        quarters = [lax.ppermute(m, "stn", ring(4, o + 1)) for o, m in enumerate(totals)]
    with jax.named_scope("carry"):
        (entering,) = call(carry_kernel, [(640, 128)], [], (at, mine, token), away=(2,))
        entering = exchange(entering)
    with jax.named_scope("solve"):
        filtered, smoothed = call(
            final_kernel,
            [(4, 256)] * 2,
            [pltpu.VMEM((4, 136, 256), f32)] + SOLVE_SCRATCH,
            (at, entering, *quarters, gram, info, forget),
        )
    return (filtered, smoothed)


def solution(mesh):
    in_specs = (P("tm", "stn"), P("tm", "stn"), P("stn", None), P("stn"), P("stn"), P("tm", None))
    out_specs = (P(("tm", "stn"), None), P(("tm", "stn"), None))
    return jax.shard_map(body, mesh=mesh, in_specs=in_specs, out_specs=out_specs, check_vma=False)
```

```python
import jax
import jax.numpy as jnp
from jax import lax
from jax.experimental import pallas as pl
from jax.experimental.pallas import tpu as pltpu
from jax.sharding import PartitionSpec as P

near_gain = 0.5
ridge = 1.0
VMEM = 24 << 20
PANEL = 16
SUB = 16
PITCH = PANEL + 1
STEPS = 128 // PANEL
f32 = jnp.float32
bf16 = jnp.bfloat16


def split3(x):
    high = x.astype(bf16)
    rest = x - high.astype(f32)
    mid = rest.astype(bf16)
    low = (rest - mid.astype(f32)).astype(bf16)
    return high, mid, low


def inverse(x):
    return pl.reciprocal(x, approx=True)


def spread(rows, lane):
    n = rows.shape[0]
    flat = rows.reshape(n * 8, 128)
    index = jnp.full((n * 8, 128), lane, jnp.int32)
    return jnp.take_along_axis(flat, index, axis=1).reshape(n, 8, 128)


def panel_solve(parts, lane0):
    parts = [[p[SUB * s : SUB * s + SUB] for s in range(PANEL // SUB)] for p in parts]
    for s in range(PANEL // SUB):
        lane = lane0 + SUB * s
        block = parts[0][s]
        e = {}
        for i in range(SUB):
            for j in range(i, SUB):
                e[i, j] = spread(block[i : i + 1], lane + j)[0]
        mult = {}
        for q in range(PANEL // SUB):
            if q != s:
                mult[q] = [spread(parts[0][q], lane + j) for j in range(SUB)]
        low = {}
        dinv = []
        for j in range(SUB):
            d = inverse(e[j, j])
            dinv.append(d)
            for i in range(j + 1, SUB):
                low[i, j] = e[j, i] * d
            for i in range(j + 1, SUB):
                for c in range(i, SUB):
                    e[i, c] = e[i, c] - low[i, j] * e[j, c]
        for p in parts:
            rows = [p[s][i] for i in range(SUB)]
            for j in range(SUB):
                for i in range(j + 1, SUB):
                    rows[i] = rows[i] - low[i, j] * rows[j]
            rows = [rows[j] * dinv[j] for j in range(SUB)]
            for j in range(SUB - 1, 0, -1):
                for i in range(j):
                    rows[i] = rows[i] - low[j, i] * rows[j]
            p[s] = jnp.stack(rows)
            for q in range(PANEL // SUB):
                if q != s:
                    new = p[q]
                    for j in range(SUB):
                        new = new - mult[q][j] * rows[j][None]
                    p[q] = new
    return [jnp.concatenate(p, axis=0) for p in parts]


def solve_in_place(t_ref, b_ref, pan_ref, pn_ref, px_ref, bx_ref):
    def step(k, half):
        row0 = k * PANEL
        lane0 = row0 - 128 * half
        halves = [half] if half else [0, 1]

        for h in halves:
            for m in range(8):
                pan_ref[h, m * PITCH : m * PITCH + PANEL, :] = t_ref[h, pl.ds(m * 256 + row0, PANEL), :]

        def load(h):
            return jnp.stack([pan_ref[h, pl.ds(i, 8, stride=PITCH), :] for i in range(PANEL)])

        original = [load(h) for h in halves]
        vec = b_ref[half]
        right = jnp.stack([spread(vec[None], lane0 + i)[0] for i in range(PANEL)])
        done = panel_solve(original + [right], lane0)
        for h, p in zip(halves, done):
            px_ref[h, pl.ds(row0, PANEL)] = p
            for i in range(PANEL):
                pn_ref[h, pl.ds(i, 8, stride=PITCH), :] = p[i]
        bx_ref[pl.ds(row0, PANEL)] = done[-1]
        for n, h in enumerate(halves):
            b_ref[h] = b_ref[h] - jnp.sum(original[n] * done[-1], axis=0)
        def cat(x, pick):
            pieces = split3(x)
            return jnp.concatenate([pieces[c] for c in pick], axis=0)

        def dot(a, b):
            return lax.dot_general(a, b, (((0,), (0,)), ((), ())), preferred_element_type=f32)

        left = [[cat(t_ref[h, pl.ds(m * 256 + row0, PANEL), :], (0, 0, 0, 1, 1, 2)) for h in halves] for m in range(8)]
        rgt = [[cat(pn_ref[h, m * PITCH : m * PITCH + PANEL, :], (0, 1, 2, 0, 1, 0)) for h in halves] for m in range(8)]
        for m in range(8):
            top = pl.ds(m * 256, 128)
            bottom = pl.ds(m * 256 + 128, 128)
            if half:
                t_ref[1, bottom, :] = t_ref[1, bottom, :] - dot(left[m][0], rgt[m][0])
            else:
                t_ref[0, top, :] = t_ref[0, top, :] - dot(left[m][0], rgt[m][0])
                t_ref[1, top, :] = t_ref[1, top, :] - dot(left[m][0], rgt[m][1])
                t_ref[1, bottom, :] = t_ref[1, bottom, :] - dot(left[m][1], rgt[m][1])

    @pl.loop(0, STEPS)
    def _(k):
        step(k, 0)

    @pl.loop(STEPS, 2 * STEPS)
    def _(k):
        step(k, 1)

    lanes = lax.broadcasted_iota(jnp.int32, (PANEL, 8, 128), 2)
    order = lax.broadcasted_iota(jnp.int32, (PANEL, 8, 128), 0)
    zero = jnp.zeros((8, 128), f32)

    def back(k, x_halves, half):
        row0 = k * PANEL
        total = sum(px_ref[h, pl.ds(row0, PANEL)] * x_halves[h][None] for h in range(half, 2))
        x_new = bx_ref[pl.ds(row0, PANEL)] - jnp.sum(total, axis=2, keepdims=True)
        keep = jnp.where(lanes == order + (row0 - 128 * half), x_new, 0.0)
        add = jnp.sum(keep, axis=0)
        return (x_halves[0] + add, x_halves[1]) if half == 0 else (x_halves[0], x_halves[1] + add)

    x = lax.fori_loop(0, STEPS, lambda n, x: back(2 * STEPS - 1 - n, x, 1), (zero, zero))
    x = lax.fori_loop(0, STEPS, lambda n, x: back(STEPS - 1 - n, x, 0), x)
    return x


SOLVE_SCRATCH = [
    pltpu.VMEM((2, 8 * 256, 128), f32),
    pltpu.VMEM((2, 8, 128), f32),
    pltpu.VMEM((2, 8 * PITCH, 128), f32),
    pltpu.VMEM((2, 8 * PITCH, 128), f32),
    pltpu.VMEM((2, 256, 8, 128), f32),
    pltpu.VMEM((256, 8, 128), f32),
]


def scalars():
    tm = lax.axis_index("tm")
    stn = lax.axis_index("stn")
    return jnp.stack([lax.rem(tm, 2), stn, tm * 4 + stn]).astype(jnp.int32)


def column(row):
    return jnp.broadcast_to(row, (128, 128)).T


def quarter_rows(rows, quarter):
    out = rows[0:4]
    for q in range(1, 4):
        out = jnp.where(quarter == q, rows[4 * q : 4 * q + 4], out)
    return out


def prepare_kernel(at, transfer, site, weight, mask, readings, design, own, msg1, msg2, msg3):
    core, stn = at[0], at[1]
    for c in range(3):
        rows = pl.ds(128 * c, 128)
        root = column(jnp.sqrt(weight[:, 128 * c : 128 * c + 128]))
        where_site = column(site[:, 128 * c : 128 * c + 128].astype(f32))
        for h in range(2):
            pole = lax.broadcasted_iota(jnp.int32, (128, 128), 1).astype(f32) + 128.0 * h
            near = jnp.where(pole == where_site, near_gain, 0.0)
            design[rows, 128 * h : 128 * h + 128] = (transfer[rows, 128 * h : 128 * h + 128] + near) * root
    half = design[pl.ds(192 * core, 192), :]
    masks = mask[...].astype(f32)
    scaled = masks * jnp.sqrt(weight[...]) * readings[...]

    def piece(quarter):
        return jnp.concatenate([quarter_rows(masks, quarter), quarter_rows(scaled, quarter)], axis=0)

    own[0:16, :] = masks
    own[16:32, :] = scaled
    for o, msg in enumerate((msg1, msg2, msg3)):
        rows = piece(lax.rem(stn + (o + 1), 4))
        msg[0:192, :] = half
        msg[192:200, :] = rows[:, 0:256]
        msg[200:208, 0:128] = rows[:, 256:384]
        msg[200:208, 128:256] = jnp.zeros((8, 128), f32)


def decay(forget, quarter):
    rows = quarter_rows(forget, quarter)
    row = [[rows[t : t + 1, 128 * h : 128 * h + 128] for h in range(2)] for t in range(4)]
    col = [[column(row[t][h]) for h in range(2)] for t in range(4)]
    return row, col


BLOCKS = ((0, 0), (0, 1), (1, 1))


def products(x, keeps, extra=None):
    high, mid, low = split3(x)
    turned = x.T
    thigh = turned.astype(bf16)
    tmid = (turned - thigh.astype(f32)).astype(bf16)
    right = jnp.concatenate([high, mid], axis=0), jnp.concatenate([mid, low], axis=0)

    def four(q):
        out = [], []
        for t in range(4):
            keep = keeps[4 * q + t : 4 * q + t + 1, :].astype(bf16)
            a, b = thigh * keep, tmid * keep
            for n, left in enumerate((jnp.concatenate([a, b], axis=1), jnp.concatenate([a, a], axis=1))):
                if t == 3 and extra is not None:
                    left = jnp.concatenate([left, extra[n]], axis=0)
                out[n].append(jnp.dot(left, right[n], preferred_element_type=f32))
        return out

    return four


def add_block(x, rows, even, odd, info, first, fresh=False):
    high, mid, low = (p.astype(f32) for p in split3(rows[4:8, :]))
    blank = jnp.zeros((4, 384), f32)

    def chunk(*quarters):
        return jnp.concatenate(quarters, axis=0).astype(bf16)

    top = chunk(high, blank, blank, blank)
    extra = (
        jnp.concatenate([chunk(high, mid, low, blank), chunk(mid, blank, blank, blank)], axis=1),
        jnp.concatenate([top, top], axis=1),
    )
    same, cross = products(x, rows, extra)(0)
    tail, cross_tail = same[3][256:272], cross[3][256:272]
    part = tail[0:4] + tail[4:8] + tail[8:12] + cross_tail[0:4]
    info[4:8, :] = part if first else info[4:8, :] + part
    for t in range(4):
        even[t] = same[t][0:256] if first or fresh else even[t] + same[t][0:256]
        odd[t] = cross[t][0:256] if first or fresh else odd[t] + cross[t][0:256]


def gram_block(even, odd, t, n):
    i, j = BLOCKS[n]
    rs, cs = slice(128 * i, 128 * i + 128), slice(128 * j, 128 * j + 128)
    return even[t, rs, cs] + (odd[t, rs, cs] + odd[t, cs, rs].T)


def part_of(message, n):
    return message.at[pl.ds(n, 128, stride=5), :]


def pack(ahead, behind, vec_f, vec_b):
    lanes = lax.broadcasted_iota(jnp.int32, (128, 128), 1)
    rows_at = lax.broadcasted_iota(jnp.int32, (128, 128), 0)
    eye = lanes == rows_at
    lower = lanes <= rows_at
    last = jnp.zeros((128, 128), f32)
    for n, e in enumerate([ahead[1, 1], behind[1, 1], vec_f[0], vec_f[1], vec_b[0], vec_b[1]]):
        last = jnp.where(lanes == n, jnp.sum(jnp.where(eye, e, 0.0), axis=1, keepdims=True), last)
    return (
        (jnp.where(lower, ahead[0, 0], ahead[1, 1]), ahead[0, 1]),
        (jnp.where(lower, behind[0, 0], behind[1, 1]), behind[0, 1]),
        last,
    )


def block_kernel(at, design, own, forget, msg, infos, ahead, behind):
    stn = at[1]
    x = design[...]
    four = products(x, own)
    infos[...] = jnp.dot(own[16:32, :], x, precision=lax.Precision.HIGHEST, preferred_element_type=f32)
    all_row, all_col = None, None
    vec_f, vec_b = [None, None], [None, None]
    for t in range(16):
        if t % 4 == 0:
            all_same, all_cross = four(t // 4)
        same, cross = all_same[t % 4], all_cross[t % 4]
        row = [forget[t : t + 1, 128 * h : 128 * h + 128] for h in range(2)]
        col = [column(r) for r in row]
        all_row = row if t == 0 else [p * q for p, q in zip(all_row, row)]
        all_col = col if t == 0 else [p * q for p, q in zip(all_col, col)]
        for n, (i, j) in enumerate(BLOCKS):
            rs, cs = slice(128 * i, 128 * i + 128), slice(128 * j, 128 * j + 128)
            g = same[rs, cs] + (cross[rs, cs] + cross[cs, rs].T)
            past = (all_col[i] * all_row[j]) * g
            if t == 0:
                ahead[n] = g
                behind[n] = past
            else:
                ahead[n] = (col[i] * row[j]) * ahead[n] + g
                behind[n] += past
        for h in range(2):
            v = infos[t : t + 1, 128 * h : 128 * h + 128]
            vec_f[h] = v if t == 0 else row[h] * vec_f[h] + v
            vec_b[h] = all_row[h] * v if t == 0 else vec_b[h] + all_row[h] * v
    f, b, last = pack(
        {k: ahead[n] for n, k in enumerate(BLOCKS)}, {k: behind[n] for n, k in enumerate(BLOCKS)}, vec_f, vec_b
    )
    wide = [jnp.broadcast_to(r, (128, 128)) for r in all_row]
    share = jnp.where(stn == 1, wide[0], wide[1])
    turned_share = pltpu.roll(jnp.where(stn == 0, wide[0], wide[1]), 64, 1)
    share = jnp.where((stn == 0) | (stn == 2), turned_share, share)
    lanes = lax.broadcasted_iota(jnp.int32, (128, 128), 1)
    for n, part in enumerate((*f, *b, jnp.where(lanes < 64, last, share))):
        part_of(msg, n)[...] = part


def early_gram_kernel(at, design, own, gram, info, even, odd):
    stn = at[1]
    info[0:4, :] = jnp.zeros((4, 256), f32)
    rows = jnp.concatenate([quarter_rows(own[0:16, :], stn), quarter_rows(own[16:32, :], stn)], axis=0)
    add_block(design[...], rows, even, odd, info, True)
    for t in range(4):
        for n in range(3):
            gram[t, n] = gram_block(even, odd, t, n)


def gram_kernel(
    at, gram_in, info_in, got1, got2, got3, oth1, oth2, oth3, forget, gram, info, msg1, msg2, msg3, block, even, odd
):
    core, stn = at[0], at[1]
    info[...] = info_in[...]
    for n, (got, oth) in enumerate(((got1, oth1), (got3, oth3), (got2, oth2))):
        block[n, pl.ds(192 * core, 192), :] = got[0:192, :]
        block[n, pl.ds(192 * (1 - core), 192), :] = oth[0:192, :]
        rows = jnp.concatenate([got[192:200, :], got[200:208, 0:128]], axis=1)
        add_block(block[n], rows, even, odd, info, False, n == 0)
    for t in range(4):
        for n in range(3):
            gram[t, n] = gram_in[t, n] + gram_block(even, odd, t, n)
    row, col = decay(forget[...], stn)
    ahead, behind = {}, {}
    for n, (i, j) in enumerate(BLOCKS):
        g = [gram[t, n] for t in range(4)]
        f = [col[t][i] * row[t][j] for t in range(4)]
        acc = g[0]
        for t in range(1, 4):
            acc = f[t] * acc + g[t]
        ahead[i, j] = acc
        acc = f[3] * g[3]
        for t in (2, 1, 0):
            acc = f[t] * (acc + g[t])
        behind[i, j] = acc
    vec_f, vec_b = [], []
    for h in range(2):
        v = [info[4 + t : 5 + t, 128 * h : 128 * h + 128] for t in range(4)]
        f = [row[t][h] for t in range(4)]
        acc = v[0]
        for t in range(1, 4):
            acc = f[t] * acc + v[t]
        vec_f.append(acc)
        acc = f[3] * v[3]
        for t in (2, 1, 0):
            acc = f[t] * (acc + v[t])
        vec_b.append(acc)
    lanes = lax.broadcasted_iota(jnp.int32, (128, 128), 1)
    rows_at = lax.broadcasted_iota(jnp.int32, (128, 128), 0)
    edge = lax.broadcasted_iota(jnp.int32, (8, 128), 0)

    def rows_of(blocks, vec):
        diagonal = jnp.sum(jnp.where(lanes == rows_at, blocks[1, 1], 0.0), axis=0, keepdims=True)
        return (
            jnp.where(lanes <= rows_at, blocks[0, 0], blocks[1, 1]),
            blocks[0, 1],
            jnp.where(edge == 0, vec[0], jnp.where(edge == 1, diagonal, 0.0)),
            jnp.where(edge == 0, vec[1], 0.0),
        )

    f, b = rows_of(ahead, vec_f), rows_of(behind, vec_b)
    for o, msg in enumerate((msg1, msg2, msg3)):
        later = lax.rem(stn + (o + 1), 4) > stn
        for n in range(4):
            rows = slice(128, 136) if n >= 2 else slice(0, 128)
            msg[rows, 128 * (n % 2) : 128 * (n % 2) + 128] = jnp.where(later, f[n], b[n])


def shifted(x, n, fill, up):
    edge = jnp.full((n, x.shape[1]), fill, f32)
    if up:
        return jnp.concatenate([x[n:], edge], axis=0)
    return jnp.concatenate([edge, x[:-n]], axis=0)


def running(gain, value, up):
    n = 1
    while n < 32:
        value = value + gain * shifted(value, n, 0.0, up)
        if n < 16:
            gain = gain * shifted(gain, n, 1.0, up)
        n *= 2
    return shifted(value, 1, 0.0, up)


def carry_kernel(at, got, token, out):
    place = at[2]
    lanes = lax.broadcasted_iota(jnp.int32, (32, 128), 1)

    def rows(n, quarter):
        return pl.ds(5 * quarter + n, 32, stride=20)

    lasts = [got[rows(4, q), :] for q in range(4)]
    low = jnp.where(lanes < 64, pltpu.roll(lasts[0], 64, 1), lasts[1])
    high = jnp.where(lanes < 64, pltpu.roll(lasts[2], 64, 1), lasts[3])
    here = lanes == place
    at_low = jnp.sum(jnp.where(here, low, 0.0), axis=1, keepdims=True)
    at_high = jnp.sum(jnp.where(here, high, 0.0), axis=1, keepdims=True)
    extra = jnp.where(lanes < 2, at_high * at_high, jnp.where((lanes == 2) | (lanes == 4), at_low, at_high))
    gain = [jnp.where(lanes <= place, at_low * low, at_high * high), at_low * high, extra]

    def total(n):
        return (got[rows(n, 0), :] + got[rows(n, 1), :]) + (got[rows(n, 2), :] + got[rows(n, 3), :])

    last = jnp.where(lanes < 6, (lasts[0] + lasts[1]) + (lasts[2] + lasts[3]), 0.0)
    enter = [running(g, v, False) for g, v in zip(gain, (total(0), total(1), last))]
    leave = [running(g, v, True) for g, v in zip(gain, (total(2), total(3), last))]
    ahead_lane = (lanes == 0) | (lanes == 2) | (lanes == 3)
    parts = (enter[0], enter[1], leave[0], leave[1], jnp.where(ahead_lane, enter[2], leave[2]))
    for n, part in enumerate(parts):
        for q in range(4):
            out[rows(n, q), :] = part


def final_kernel(
    at, got, quarter1, quarter2, quarter3, gram, info, forget, filtered, smoothed, quarters,
    t_ref, b_ref, pan_ref, pn_ref, px_ref, bx_ref,
):
    stn = at[1]
    lanes = lax.broadcasted_iota(jnp.int32, (128, 128), 1)
    rows_at = lax.broadcasted_iota(jnp.int32, (128, 128), 0)
    eye = lanes == rows_at
    lower = lanes <= rows_at
    unit = jnp.where(eye, ridge, 0.0)
    for o, quarter in enumerate((quarter1, quarter2, quarter3)):
        quarters[lax.rem(stn + (3 - o), 4)] = quarter[...]
    got = [part_of(got, n)[...] for n in range(5)]
    last = got[4]

    def lane_row(n):
        col = jnp.sum(jnp.where(lanes == n, last, 0.0), axis=1, keepdims=True)
        return jnp.sum(jnp.where(eye, col, 0.0), axis=0, keepdims=True)

    first = [got[0], got[1], lane_row(2), lane_row(3), lane_row(0)]
    second = [got[2], got[3], lane_row(4), lane_row(5), lane_row(1)]

    def past_quarter(q, state, use):
        gain = forget[4 * q : 4 * q + 1, :]
        for t in range(1, 4):
            gain = gain * forget[4 * q + t : 4 * q + t + 1, :]
        low, high = gain[:, 0:128], gain[:, 128:256]
        clow, chigh = column(low), column(high)
        gains = (jnp.where(lower, clow * low, chigh * high), clow * high, low, high, high * high)
        own = (
            quarters[q, 0:128, 0:128],
            quarters[q, 0:128, 128:256],
            quarters[q, 128:129, 0:128],
            quarters[q, 128:129, 128:256],
            quarters[q, 129:130, 0:128],
        )
        return [jnp.where(use, g * v + w, v) for g, v, w in zip(gains, state, own)]

    for q in (0, 1, 2):
        first = past_quarter(q, first, q < stn)
    for q in (3, 2, 1):
        second = past_quarter(q, second, q > stn)

    def unpack(state):
        packed = state[0]
        turned = packed.T
        one = jnp.where(lower, packed, turned)
        two = jnp.where(eye, state[4], jnp.where(lower, turned, packed))
        return {(0, 0): one, (0, 1): state[1], (1, 1): two}

    ahead = unpack(first)
    behind = unpack(second)
    row, col = decay(forget[...], stn)
    for n, (i, j) in enumerate(BLOCKS):
        f = [col[t][i] * row[t][j] for t in range(4)]
        acc = ahead[i, j]
        held = []
        for t in range(4):
            acc = f[t] * acc + gram[t, n]
            full = acc + unit if i == j else acc
            held.append(full)
            t_ref[j, 256 * t + 128 * i : 256 * t + 128 * i + 128, :] = full
        acc = behind[i, j]
        for t in (3, 2, 1, 0):
            at_row = 256 * (4 + t) + 128 * i
            t_ref[j, at_row : at_row + 128, :] = held[t] + acc
            if t:
                acc = f[t] * (acc + gram[t, n])
    for h in range(2):
        vec = first[2 + h]
        held = []
        for t in range(4):
            vec = row[t][h] * vec + info[4 + t : 5 + t, 128 * h : 128 * h + 128]
            held.append(vec)
        vec = second[2 + h]
        both = [None] * 4
        for t in (3, 2, 1, 0):
            both[t] = held[t] + vec
            if t:
                vec = row[t][h] * (vec + info[4 + t : 5 + t, 128 * h : 128 * h + 128])
        b_ref[h] = jnp.concatenate(held + both, axis=0)
    x = solve_in_place(t_ref, b_ref, pan_ref, pn_ref, px_ref, bx_ref)
    for h in range(2):
        filtered[:, 128 * h : 128 * h + 128] = x[h][0:4]
        smoothed[:, 128 * h : 128 * h + 128] = x[h][4:8]


def call(kernel, outs, scratch, operands, flops=1e6, away=()):
    return pl.pallas_call(
        kernel,
        out_shape=[jax.ShapeDtypeStruct(s, f32) for s in outs],
        in_specs=[pl.BlockSpec(memory_space=pltpu.SMEM)]
        + [pl.BlockSpec(memory_space=pl.ANY if n in away else pltpu.VMEM) for n in range(1, len(operands))],
        out_specs=[pl.BlockSpec(memory_space=pltpu.VMEM)] * len(outs),
        scratch_shapes=scratch,
        compiler_params=pltpu.CompilerParams(vmem_limit_bytes=VMEM),
        cost_estimate=pl.CostEstimate(flops=int(flops), bytes_accessed=1 << 20, transcendentals=0),
    )(*operands)


def ring(count, shift):
    return [(i, (i + shift) % count) for i in range(count)]


SWAP = [(i, i ^ 1) for i in range(32)]


def exchange(message):
    out = lax.all_to_all(message.reshape(128, 1, 640), ("tm", "stn"), 0, 0, tiled=True)
    return out.reshape(640, 128)


def body(readings, gap_mask, transfer, channel_weight, pole_site, forget):
    at = scalars()
    parts = [pltpu.VMEM((4, 256, 256), f32)] * 2
    with jax.named_scope("design"):
        design, own, *msgs = call(
            prepare_kernel,
            [(384, 256), (32, 384)] + [(208, 256)] * 3,
            [],
            (at, transfer, pole_site[None], channel_weight[None], gap_mask, readings),
        )
    with jax.named_scope("gather"):
        got = [lax.ppermute(m, "stn", ring(4, o + 1)) for o, m in enumerate(msgs)]
    with jax.named_scope("block"):
        (totals,) = call(
            block_kernel,
            [(640, 128)],
            [
                pltpu.VMEM((16, 256), f32),
                pltpu.VMEM((3, 128, 128), f32),
                pltpu.VMEM((3, 128, 128), f32),
            ],
            (at, design, own, forget),
            6e9,
        )
    with jax.named_scope("carry"):
        mine = exchange(totals)
    with jax.named_scope("swap"):
        other = [lax.ppermute(g, "tm", SWAP) for g in got]
    with jax.named_scope("early_gram"):
        gram, info = call(early_gram_kernel, [(4, 3, 128, 128), (8, 256)], parts, (at, design, own), 2e10)
    with jax.named_scope("gram"):
        gram, info, *totals = call(
            gram_kernel,
            [(4, 3, 128, 128), (8, 256)] + [(136, 256)] * 3,
            [pltpu.VMEM((3, 384, 256), f32)] + parts,
            (at, gram, info, *got, *other, forget),
            2e9,
        )
    with jax.named_scope("token"):
        token = lax.ppermute(info, "tm", SWAP)
    with jax.named_scope("quarters"):
        quarters = [lax.ppermute(m, "stn", ring(4, o + 1)) for o, m in enumerate(totals)]
    with jax.named_scope("carry"):
        (entering,) = call(carry_kernel, [(640, 128)], [], (at, mine, token), away=(2,))
        entering = exchange(entering)
    with jax.named_scope("solve"):
        filtered, smoothed = call(
            final_kernel,
            [(4, 256)] * 2,
            [pltpu.VMEM((4, 136, 256), f32)] + SOLVE_SCRATCH,
            (at, entering, *quarters, gram, info, forget),
        )
    return (filtered, smoothed)


def solution(mesh):
    in_specs = (P("tm", "stn"), P("tm", "stn"), P("stn", None), P("stn"), P("stn"), P("tm", None))
    out_specs = (P(("tm", "stn"), None), P(("tm", "stn"), None))
    return jax.shard_map(body, mesh=mesh, in_specs=in_specs, out_specs=out_specs, check_vma=False)
```

```python
import jax
import jax.numpy as jnp
from jax import lax
from jax.experimental import pallas as pl
from jax.experimental.pallas import tpu as pltpu
from jax.sharding import PartitionSpec as P

near_gain = 0.5
ridge = 1.0
VMEM = 24 << 20
PANEL = 16
SUB = 16
PITCH = PANEL + 1
STEPS = 128 // PANEL
f32 = jnp.float32
bf16 = jnp.bfloat16


def split3(x):
    high = x.astype(bf16)
    rest = x - high.astype(f32)
    mid = rest.astype(bf16)
    low = (rest - mid.astype(f32)).astype(bf16)
    return high, mid, low


def inverse(x):
    return pl.reciprocal(x, approx=True)


def spread(rows, lane):
    n = rows.shape[0]
    flat = rows.reshape(n * 8, 128)
    index = jnp.full((n * 8, 128), lane, jnp.int32)
    return jnp.take_along_axis(flat, index, axis=1).reshape(n, 8, 128)


def panel_solve(parts, lane0):
    parts = [[p[SUB * s : SUB * s + SUB] for s in range(PANEL // SUB)] for p in parts]
    for s in range(PANEL // SUB):
        lane = lane0 + SUB * s
        block = parts[0][s]
        e = {}
        for i in range(SUB):
            for j in range(i, SUB):
                e[i, j] = spread(block[i : i + 1], lane + j)[0]
        mult = {}
        for q in range(PANEL // SUB):
            if q != s:
                mult[q] = [spread(parts[0][q], lane + j) for j in range(SUB)]
        low = {}
        dinv = []
        for j in range(SUB):
            d = inverse(e[j, j])
            dinv.append(d)
            for i in range(j + 1, SUB):
                low[i, j] = e[j, i] * d
            for i in range(j + 1, SUB):
                for c in range(i, SUB):
                    e[i, c] = e[i, c] - low[i, j] * e[j, c]
        for p in parts:
            rows = [p[s][i] for i in range(SUB)]
            for j in range(SUB):
                for i in range(j + 1, SUB):
                    rows[i] = rows[i] - low[i, j] * rows[j]
            rows = [rows[j] * dinv[j] for j in range(SUB)]
            for j in range(SUB - 1, 0, -1):
                for i in range(j):
                    rows[i] = rows[i] - low[j, i] * rows[j]
            p[s] = jnp.stack(rows)
            for q in range(PANEL // SUB):
                if q != s:
                    new = p[q]
                    for j in range(SUB):
                        new = new - mult[q][j] * rows[j][None]
                    p[q] = new
    return [jnp.concatenate(p, axis=0) for p in parts]


def solve_in_place(t_ref, b_ref, pan_ref, pn_ref, px_ref, bx_ref):
    def step(k, half, final=False):
        row0 = k * PANEL
        lane0 = row0 - 128 * half
        halves = [half] if half else [0, 1]

        for h in halves:
            for m in range(8):
                pan_ref[h, m * PITCH : m * PITCH + PANEL, :] = t_ref[h, pl.ds(m * 256 + row0, PANEL), :]

        def load(h):
            return jnp.stack([pan_ref[h, pl.ds(i, 8, stride=PITCH), :] for i in range(PANEL)])

        original = [load(h) for h in halves]
        vec = b_ref[half]
        right = jnp.stack([spread(vec[None], lane0 + i)[0] for i in range(PANEL)])
        done = panel_solve(original + [right], lane0)
        for h, p in zip(halves, done):
            px_ref[h, pl.ds(row0, PANEL)] = p
            for i in range(PANEL):
                pn_ref[h, pl.ds(i, 8, stride=PITCH), :] = p[i]
        bx_ref[pl.ds(row0, PANEL)] = done[-1]
        for n, h in enumerate(halves):
            b_ref[h] = b_ref[h] - jnp.sum(original[n] * done[-1], axis=0)
        def cat(x, pick):
            pieces = split3(x)
            return jnp.concatenate([pieces[c] for c in pick], axis=0)

        def dot(a, b):
            return lax.dot_general(a, b, (((0,), (0,)), ((), ())), preferred_element_type=f32)

        left = [[cat(t_ref[h, pl.ds(m * 256 + row0, PANEL), :], (0, 0, 0, 1, 1, 2)) for h in halves] for m in range(8)]
        rgt = [[cat(pn_ref[h, m * PITCH : m * PITCH + PANEL, :], (0, 1, 2, 0, 1, 0)) for h in halves] for m in range(8)]
        for m in range(0 if half and final else 8):
            top = pl.ds(m * 256, 128)
            bottom = pl.ds(m * 256 + 128, 128)
            if half:
                t_ref[1, bottom, :] = t_ref[1, bottom, :] - dot(left[m][0], rgt[m][0])
            else:
                if not final:
                    t_ref[0, top, :] = t_ref[0, top, :] - dot(left[m][0], rgt[m][0])
                    t_ref[1, top, :] = t_ref[1, top, :] - dot(left[m][0], rgt[m][1])
                t_ref[1, bottom, :] = t_ref[1, bottom, :] - dot(left[m][1], rgt[m][1])

    for half in range(2):
        end = (half + 1) * STEPS - 1

        @pl.loop(half * STEPS, end)
        def _(k):
            step(k, half)

        step(end, half, True)

    lanes = lax.broadcasted_iota(jnp.int32, (PANEL, 8, 128), 2)
    order = lax.broadcasted_iota(jnp.int32, (PANEL, 8, 128), 0)
    zero = jnp.zeros((8, 128), f32)

    def back(k, x_halves, half):
        row0 = k * PANEL
        total = sum(px_ref[h, pl.ds(row0, PANEL)] * x_halves[h][None] for h in range(half, 2))
        x_new = bx_ref[pl.ds(row0, PANEL)] - jnp.sum(total, axis=2, keepdims=True)
        keep = jnp.where(lanes == order + (row0 - 128 * half), x_new, 0.0)
        add = jnp.sum(keep, axis=0)
        return (x_halves[0] + add, x_halves[1]) if half == 0 else (x_halves[0], x_halves[1] + add)

    x = lax.fori_loop(0, STEPS, lambda n, x: back(2 * STEPS - 1 - n, x, 1), (zero, zero))
    x = lax.fori_loop(0, STEPS, lambda n, x: back(STEPS - 1 - n, x, 0), x)
    return x


SOLVE_SCRATCH = [
    pltpu.VMEM((2, 8 * 256, 128), f32),
    pltpu.VMEM((2, 8, 128), f32),
    pltpu.VMEM((2, 8 * PITCH, 128), f32),
    pltpu.VMEM((2, 8 * PITCH, 128), f32),
    pltpu.VMEM((2, 256, 8, 128), f32),
    pltpu.VMEM((256, 8, 128), f32),
]


def scalars():
    tm = lax.axis_index("tm")
    stn = lax.axis_index("stn")
    return jnp.stack([lax.rem(tm, 2), stn, tm * 4 + stn]).astype(jnp.int32)


def column(row):
    return jnp.broadcast_to(row, (128, 128)).T


def quarter_rows(rows, quarter):
    out = rows[0:4]
    for q in range(1, 4):
        out = jnp.where(quarter == q, rows[4 * q : 4 * q + 4], out)
    return out


def prepare_kernel(at, transfer, site, weight, mask, readings, design, own, msg1, msg2, msg3):
    core, stn = at[0], at[1]
    for c in range(3):
        rows = pl.ds(128 * c, 128)
        root = column(jnp.sqrt(weight[:, 128 * c : 128 * c + 128]))
        where_site = column(site[:, 128 * c : 128 * c + 128].astype(f32))
        for h in range(2):
            pole = lax.broadcasted_iota(jnp.int32, (128, 128), 1).astype(f32) + 128.0 * h
            near = jnp.where(pole == where_site, near_gain, 0.0)
            design[rows, 128 * h : 128 * h + 128] = (transfer[rows, 128 * h : 128 * h + 128] + near) * root
    half = design[pl.ds(192 * core, 192), :]
    masks = mask[...].astype(f32)
    scaled = masks * jnp.sqrt(weight[...]) * readings[...]

    def piece(quarter):
        return jnp.concatenate([quarter_rows(masks, quarter), quarter_rows(scaled, quarter)], axis=0)

    own[0:16, :] = masks
    own[16:32, :] = scaled
    for o, msg in enumerate((msg1, msg2, msg3)):
        rows = piece(lax.rem(stn + (o + 1), 4))
        msg[0:192, :] = half
        msg[192:200, :] = rows[:, 0:256]
        msg[200:208, 0:128] = rows[:, 256:384]
        msg[200:208, 128:256] = jnp.zeros((8, 128), f32)


def decay(forget, quarter):
    rows = quarter_rows(forget, quarter)
    row = [[rows[t : t + 1, 128 * h : 128 * h + 128] for h in range(2)] for t in range(4)]
    col = [[column(row[t][h]) for h in range(2)] for t in range(4)]
    return row, col


BLOCKS = ((0, 0), (0, 1), (1, 1))


def products(x, keeps, extra=None):
    high, mid, low = split3(x)
    turned = x.T
    thigh = turned.astype(bf16)
    tmid = (turned - thigh.astype(f32)).astype(bf16)
    right = jnp.concatenate([high, mid], axis=0), jnp.concatenate([mid, low], axis=0)

    def four(q):
        out = [], []
        for t in range(4):
            keep = keeps[4 * q + t : 4 * q + t + 1, :].astype(bf16)
            a, b = thigh * keep, tmid * keep
            for n, left in enumerate((jnp.concatenate([a, b], axis=1), jnp.concatenate([a, a], axis=1))):
                if t == 3 and extra is not None:
                    left = jnp.concatenate([left, extra[n]], axis=0)
                out[n].append(jnp.dot(left, right[n], preferred_element_type=f32))
        return out

    return four


def add_block(x, rows, even, odd, info, first, fresh=False):
    high, mid, low = (p.astype(f32) for p in split3(rows[4:8, :]))
    blank = jnp.zeros((4, 384), f32)

    def chunk(*quarters):
        return jnp.concatenate(quarters, axis=0).astype(bf16)

    top = chunk(high, blank, blank, blank)
    extra = (
        jnp.concatenate([chunk(high, mid, low, blank), chunk(mid, blank, blank, blank)], axis=1),
        jnp.concatenate([top, top], axis=1),
    )
    same, cross = products(x, rows, extra)(0)
    tail, cross_tail = same[3][256:272], cross[3][256:272]
    part = tail[0:4] + tail[4:8] + tail[8:12] + cross_tail[0:4]
    info[4:8, :] = part if first else info[4:8, :] + part
    for t in range(4):
        even[t] = same[t][0:256] if first or fresh else even[t] + same[t][0:256]
        odd[t] = cross[t][0:256] if first or fresh else odd[t] + cross[t][0:256]


def gram_block(even, odd, t, n):
    i, j = BLOCKS[n]
    rs, cs = slice(128 * i, 128 * i + 128), slice(128 * j, 128 * j + 128)
    return even[t, rs, cs] + (odd[t, rs, cs] + odd[t, cs, rs].T)


def part_of(message, n):
    return message.at[pl.ds(n, 128, stride=5), :]


def pack(ahead, behind, vec_f, vec_b):
    lanes = lax.broadcasted_iota(jnp.int32, (128, 128), 1)
    rows_at = lax.broadcasted_iota(jnp.int32, (128, 128), 0)
    eye = lanes == rows_at
    lower = lanes <= rows_at
    last = jnp.zeros((128, 128), f32)
    for n, e in enumerate([ahead[1, 1], behind[1, 1], vec_f[0], vec_f[1], vec_b[0], vec_b[1]]):
        last = jnp.where(lanes == n, jnp.sum(jnp.where(eye, e, 0.0), axis=1, keepdims=True), last)
    return (
        (jnp.where(lower, ahead[0, 0], ahead[1, 1]), ahead[0, 1]),
        (jnp.where(lower, behind[0, 0], behind[1, 1]), behind[0, 1]),
        last,
    )


def block_kernel(at, design, own, forget, msg, infos, ahead, behind):
    stn = at[1]
    x = design[...]
    four = products(x, own)
    infos[...] = jnp.dot(own[16:32, :], x, precision=lax.Precision.HIGHEST, preferred_element_type=f32)
    all_row, all_col = None, None
    vec_f, vec_b = [None, None], [None, None]
    for t in range(16):
        if t % 4 == 0:
            all_same, all_cross = four(t // 4)
        same, cross = all_same[t % 4], all_cross[t % 4]
        row = [forget[t : t + 1, 128 * h : 128 * h + 128] for h in range(2)]
        col = [column(r) for r in row]
        all_row = row if t == 0 else [p * q for p, q in zip(all_row, row)]
        all_col = col if t == 0 else [p * q for p, q in zip(all_col, col)]
        for n, (i, j) in enumerate(BLOCKS):
            rs, cs = slice(128 * i, 128 * i + 128), slice(128 * j, 128 * j + 128)
            g = same[rs, cs] + (cross[rs, cs] + cross[cs, rs].T)
            past = (all_col[i] * all_row[j]) * g
            if t == 0:
                ahead[n] = g
                behind[n] = past
            else:
                ahead[n] = (col[i] * row[j]) * ahead[n] + g
                behind[n] += past
        for h in range(2):
            v = infos[t : t + 1, 128 * h : 128 * h + 128]
            vec_f[h] = v if t == 0 else row[h] * vec_f[h] + v
            vec_b[h] = all_row[h] * v if t == 0 else vec_b[h] + all_row[h] * v
    f, b, last = pack(
        {k: ahead[n] for n, k in enumerate(BLOCKS)}, {k: behind[n] for n, k in enumerate(BLOCKS)}, vec_f, vec_b
    )
    wide = [jnp.broadcast_to(r, (128, 128)) for r in all_row]
    share = jnp.where(stn == 1, wide[0], wide[1])
    turned_share = pltpu.roll(jnp.where(stn == 0, wide[0], wide[1]), 64, 1)
    share = jnp.where((stn == 0) | (stn == 2), turned_share, share)
    lanes = lax.broadcasted_iota(jnp.int32, (128, 128), 1)
    for n, part in enumerate((*f, *b, jnp.where(lanes < 64, last, share))):
        part_of(msg, n)[...] = part


def early_gram_kernel(at, design, own, gram, info, even, odd):
    stn = at[1]
    info[0:4, :] = jnp.zeros((4, 256), f32)
    rows = jnp.concatenate([quarter_rows(own[0:16, :], stn), quarter_rows(own[16:32, :], stn)], axis=0)
    add_block(design[...], rows, even, odd, info, True)
    for t in range(4):
        for n in range(3):
            gram[t, n] = gram_block(even, odd, t, n)


def gram_kernel(
    at, gram_in, info_in, got1, got2, got3, oth1, oth2, oth3, forget, gram, info, msg1, msg2, msg3, block, even, odd
):
    core, stn = at[0], at[1]
    info[...] = info_in[...]
    for n, (got, oth) in enumerate(((got1, oth1), (got3, oth3), (got2, oth2))):
        block[n, pl.ds(192 * core, 192), :] = got[0:192, :]
        block[n, pl.ds(192 * (1 - core), 192), :] = oth[0:192, :]
        rows = jnp.concatenate([got[192:200, :], got[200:208, 0:128]], axis=1)
        add_block(block[n], rows, even, odd, info, False, n == 0)
    for t in range(4):
        for n in range(3):
            gram[t, n] = gram_in[t, n] + gram_block(even, odd, t, n)
    row, col = decay(forget[...], stn)
    ahead, behind = {}, {}
    for n, (i, j) in enumerate(BLOCKS):
        g = [gram[t, n] for t in range(4)]
        f = [col[t][i] * row[t][j] for t in range(4)]
        acc = g[0]
        for t in range(1, 4):
            acc = f[t] * acc + g[t]
        ahead[i, j] = acc
        acc = f[3] * g[3]
        for t in (2, 1, 0):
            acc = f[t] * (acc + g[t])
        behind[i, j] = acc
    vec_f, vec_b = [], []
    for h in range(2):
        v = [info[4 + t : 5 + t, 128 * h : 128 * h + 128] for t in range(4)]
        f = [row[t][h] for t in range(4)]
        acc = v[0]
        for t in range(1, 4):
            acc = f[t] * acc + v[t]
        vec_f.append(acc)
        acc = f[3] * v[3]
        for t in (2, 1, 0):
            acc = f[t] * (acc + v[t])
        vec_b.append(acc)
    lanes = lax.broadcasted_iota(jnp.int32, (128, 128), 1)
    rows_at = lax.broadcasted_iota(jnp.int32, (128, 128), 0)
    edge = lax.broadcasted_iota(jnp.int32, (8, 128), 0)

    def rows_of(blocks, vec):
        diagonal = jnp.sum(jnp.where(lanes == rows_at, blocks[1, 1], 0.0), axis=0, keepdims=True)
        return (
            jnp.where(lanes <= rows_at, blocks[0, 0], blocks[1, 1]),
            blocks[0, 1],
            jnp.where(edge == 0, vec[0], jnp.where(edge == 1, diagonal, 0.0)),
            jnp.where(edge == 0, vec[1], 0.0),
        )

    f, b = rows_of(ahead, vec_f), rows_of(behind, vec_b)
    for o, msg in enumerate((msg1, msg2, msg3)):
        later = lax.rem(stn + (o + 1), 4) > stn
        for n in range(4):
            rows = slice(128, 136) if n >= 2 else slice(0, 128)
            msg[rows, 128 * (n % 2) : 128 * (n % 2) + 128] = jnp.where(later, f[n], b[n])


def shifted(x, n, fill, up):
    edge = jnp.full((n, x.shape[1]), fill, f32)
    if up:
        return jnp.concatenate([x[n:], edge], axis=0)
    return jnp.concatenate([edge, x[:-n]], axis=0)


def running(gain, value, up):
    n = 1
    while n < 32:
        value = value + gain * shifted(value, n, 0.0, up)
        if n < 16:
            gain = gain * shifted(gain, n, 1.0, up)
        n *= 2
    return shifted(value, 1, 0.0, up)


def carry_kernel(at, got, token, out):
    place = at[2]
    lanes = lax.broadcasted_iota(jnp.int32, (32, 128), 1)

    def rows(n, quarter):
        return pl.ds(5 * quarter + n, 32, stride=20)

    lasts = [got[rows(4, q), :] for q in range(4)]
    low = jnp.where(lanes < 64, pltpu.roll(lasts[0], 64, 1), lasts[1])
    high = jnp.where(lanes < 64, pltpu.roll(lasts[2], 64, 1), lasts[3])
    here = lanes == place
    at_low = jnp.sum(jnp.where(here, low, 0.0), axis=1, keepdims=True)
    at_high = jnp.sum(jnp.where(here, high, 0.0), axis=1, keepdims=True)
    extra = jnp.where(lanes < 2, at_high * at_high, jnp.where((lanes == 2) | (lanes == 4), at_low, at_high))
    gain = [jnp.where(lanes <= place, at_low * low, at_high * high), at_low * high, extra]

    def total(n):
        return (got[rows(n, 0), :] + got[rows(n, 1), :]) + (got[rows(n, 2), :] + got[rows(n, 3), :])

    last = jnp.where(lanes < 6, (lasts[0] + lasts[1]) + (lasts[2] + lasts[3]), 0.0)
    enter = [running(g, v, False) for g, v in zip(gain, (total(0), total(1), last))]
    leave = [running(g, v, True) for g, v in zip(gain, (total(2), total(3), last))]
    ahead_lane = (lanes == 0) | (lanes == 2) | (lanes == 3)
    parts = (enter[0], enter[1], leave[0], leave[1], jnp.where(ahead_lane, enter[2], leave[2]))
    for n, part in enumerate(parts):
        for q in range(4):
            out[rows(n, q), :] = part


def final_kernel(
    at, got, quarter1, quarter2, quarter3, gram, info, forget, filtered, smoothed, quarters,
    t_ref, b_ref, pan_ref, pn_ref, px_ref, bx_ref,
):
    stn = at[1]
    lanes = lax.broadcasted_iota(jnp.int32, (128, 128), 1)
    rows_at = lax.broadcasted_iota(jnp.int32, (128, 128), 0)
    eye = lanes == rows_at
    lower = lanes <= rows_at
    unit = jnp.where(eye, ridge, 0.0)
    for o, quarter in enumerate((quarter1, quarter2, quarter3)):
        quarters[lax.rem(stn + (3 - o), 4)] = quarter[...]
    got = [part_of(got, n)[...] for n in range(5)]
    last = got[4]

    def lane_row(n):
        col = jnp.sum(jnp.where(lanes == n, last, 0.0), axis=1, keepdims=True)
        return jnp.sum(jnp.where(eye, col, 0.0), axis=0, keepdims=True)

    first = [got[0], got[1], lane_row(2), lane_row(3), lane_row(0)]
    second = [got[2], got[3], lane_row(4), lane_row(5), lane_row(1)]

    def past_quarter(q, state, use):
        gain = forget[4 * q : 4 * q + 1, :]
        for t in range(1, 4):
            gain = gain * forget[4 * q + t : 4 * q + t + 1, :]
        low, high = gain[:, 0:128], gain[:, 128:256]
        clow, chigh = column(low), column(high)
        gains = (jnp.where(lower, clow * low, chigh * high), clow * high, low, high, high * high)
        own = (
            quarters[q, 0:128, 0:128],
            quarters[q, 0:128, 128:256],
            quarters[q, 128:129, 0:128],
            quarters[q, 128:129, 128:256],
            quarters[q, 129:130, 0:128],
        )
        return [jnp.where(use, g * v + w, v) for g, v, w in zip(gains, state, own)]

    for q in (0, 1, 2):
        first = past_quarter(q, first, q < stn)
    for q in (3, 2, 1):
        second = past_quarter(q, second, q > stn)

    def unpack(state):
        packed = state[0]
        turned = packed.T
        one = jnp.where(lower, packed, turned)
        two = jnp.where(eye, state[4], jnp.where(lower, turned, packed))
        return {(0, 0): one, (0, 1): state[1], (1, 1): two}

    ahead = unpack(first)
    behind = unpack(second)
    row, col = decay(forget[...], stn)
    for n, (i, j) in enumerate(BLOCKS):
        f = [col[t][i] * row[t][j] for t in range(4)]
        acc = ahead[i, j]
        held = []
        for t in range(4):
            acc = f[t] * acc + gram[t, n]
            full = acc + unit if i == j else acc
            held.append(full)
            t_ref[j, 256 * t + 128 * i : 256 * t + 128 * i + 128, :] = full
        acc = behind[i, j]
        for t in (3, 2, 1, 0):
            at_row = 256 * (4 + t) + 128 * i
            t_ref[j, at_row : at_row + 128, :] = held[t] + acc
            if t:
                acc = f[t] * (acc + gram[t, n])
    for h in range(2):
        vec = first[2 + h]
        held = []
        for t in range(4):
            vec = row[t][h] * vec + info[4 + t : 5 + t, 128 * h : 128 * h + 128]
            held.append(vec)
        vec = second[2 + h]
        both = [None] * 4
        for t in (3, 2, 1, 0):
            both[t] = held[t] + vec
            if t:
                vec = row[t][h] * (vec + info[4 + t : 5 + t, 128 * h : 128 * h + 128])
        b_ref[h] = jnp.concatenate(held + both, axis=0)
    x = solve_in_place(t_ref, b_ref, pan_ref, pn_ref, px_ref, bx_ref)
    for h in range(2):
        filtered[:, 128 * h : 128 * h + 128] = x[h][0:4]
        smoothed[:, 128 * h : 128 * h + 128] = x[h][4:8]


def call(kernel, outs, scratch, operands, flops=1e6, away=()):
    return pl.pallas_call(
        kernel,
        out_shape=[jax.ShapeDtypeStruct(s, f32) for s in outs],
        in_specs=[pl.BlockSpec(memory_space=pltpu.SMEM)]
        + [pl.BlockSpec(memory_space=pl.ANY if n in away else pltpu.VMEM) for n in range(1, len(operands))],
        out_specs=[pl.BlockSpec(memory_space=pltpu.VMEM)] * len(outs),
        scratch_shapes=scratch,
        compiler_params=pltpu.CompilerParams(vmem_limit_bytes=VMEM),
        cost_estimate=pl.CostEstimate(flops=int(flops), bytes_accessed=1 << 20, transcendentals=0),
    )(*operands)


def ring(count, shift):
    return [(i, (i + shift) % count) for i in range(count)]


SWAP = [(i, i ^ 1) for i in range(32)]


def exchange(message):
    out = lax.all_to_all(message.reshape(128, 1, 640), ("tm", "stn"), 0, 0, tiled=True)
    return out.reshape(640, 128)


def body(readings, gap_mask, transfer, channel_weight, pole_site, forget):
    at = scalars()
    parts = [pltpu.VMEM((4, 256, 256), f32)] * 2
    with jax.named_scope("design"):
        design, own, *msgs = call(
            prepare_kernel,
            [(384, 256), (32, 384)] + [(208, 256)] * 3,
            [],
            (at, transfer, pole_site[None], channel_weight[None], gap_mask, readings),
        )
    with jax.named_scope("gather"):
        got = [lax.ppermute(m, "stn", ring(4, o + 1)) for o, m in enumerate(msgs)]
    with jax.named_scope("block"):
        (totals,) = call(
            block_kernel,
            [(640, 128)],
            [
                pltpu.VMEM((16, 256), f32),
                pltpu.VMEM((3, 128, 128), f32),
                pltpu.VMEM((3, 128, 128), f32),
            ],
            (at, design, own, forget),
            6e9,
        )
    with jax.named_scope("carry"):
        mine = exchange(totals)
    with jax.named_scope("swap"):
        other = [lax.ppermute(g, "tm", SWAP) for g in got]
    with jax.named_scope("early_gram"):
        gram, info = call(early_gram_kernel, [(4, 3, 128, 128), (8, 256)], parts, (at, design, own), 2e10)
    with jax.named_scope("gram"):
        gram, info, *totals = call(
            gram_kernel,
            [(4, 3, 128, 128), (8, 256)] + [(136, 256)] * 3,
            [pltpu.VMEM((3, 384, 256), f32)] + parts,
            (at, gram, info, *got, *other, forget),
            2e9,
        )
    with jax.named_scope("token"):
        token = lax.ppermute(info, "tm", SWAP)
    with jax.named_scope("quarters"):
        quarters = [lax.ppermute(m, "stn", ring(4, o + 1)) for o, m in enumerate(totals)]
    with jax.named_scope("carry"):
        (entering,) = call(carry_kernel, [(640, 128)], [], (at, mine, token), away=(2,))
        entering = exchange(entering)
    with jax.named_scope("solve"):
        filtered, smoothed = call(
            final_kernel,
            [(4, 256)] * 2,
            [pltpu.VMEM((4, 136, 256), f32)] + SOLVE_SCRATCH,
            (at, entering, *quarters, gram, info, forget),
        )
    return (filtered, smoothed)


def solution(mesh):
    in_specs = (P("tm", "stn"), P("tm", "stn"), P("stn", None), P("stn"), P("stn"), P("tm", None))
    out_specs = (P(("tm", "stn"), None), P(("tm", "stn"), None))
    return jax.shard_map(body, mesh=mesh, in_specs=in_specs, out_specs=out_specs, check_vma=False)
```

```python
import jax
import jax.numpy as jnp
from jax import lax
from jax.experimental import pallas as pl
from jax.experimental.pallas import tpu as pltpu
from jax.sharding import PartitionSpec as P

near_gain = 0.5
ridge = 1.0
VMEM = 24 << 20
PANEL = 16
SUB = 16
PITCH = PANEL + 1
STEPS = 128 // PANEL
f32 = jnp.float32
bf16 = jnp.bfloat16


def split3(x):
    high = x.astype(bf16)
    rest = x - high.astype(f32)
    mid = rest.astype(bf16)
    low = (rest - mid.astype(f32)).astype(bf16)
    return high, mid, low


def inverse(x):
    return pl.reciprocal(x, approx=True)


def spread(rows, lane):
    n = rows.shape[0]
    flat = rows.reshape(n * 8, 128)
    index = jnp.full((n * 8, 128), lane, jnp.int32)
    return jnp.take_along_axis(flat, index, axis=1).reshape(n, 8, 128)


def panel_solve(parts, lane0):
    parts = [[p[SUB * s : SUB * s + SUB] for s in range(PANEL // SUB)] for p in parts]
    for s in range(PANEL // SUB):
        lane = lane0 + SUB * s
        block = parts[0][s]
        e = {}
        for i in range(SUB):
            for j in range(i, SUB):
                e[i, j] = spread(block[i : i + 1], lane + j)[0]
        mult = {}
        for q in range(PANEL // SUB):
            if q != s:
                mult[q] = [spread(parts[0][q], lane + j) for j in range(SUB)]
        low = {}
        dinv = []
        for j in range(SUB):
            d = inverse(e[j, j])
            dinv.append(d)
            for i in range(j + 1, SUB):
                low[i, j] = e[j, i] * d
            for i in range(j + 1, SUB):
                for c in range(i, SUB):
                    e[i, c] = e[i, c] - low[i, j] * e[j, c]
        for p in parts:
            rows = [p[s][i] for i in range(SUB)]
            for j in range(SUB):
                for i in range(j + 1, SUB):
                    rows[i] = rows[i] - low[i, j] * rows[j]
            rows = [rows[j] * dinv[j] for j in range(SUB)]
            for j in range(SUB - 1, 0, -1):
                for i in range(j):
                    rows[i] = rows[i] - low[j, i] * rows[j]
            p[s] = jnp.stack(rows)
            for q in range(PANEL // SUB):
                if q != s:
                    new = p[q]
                    for j in range(SUB):
                        new = new - mult[q][j] * rows[j][None]
                    p[q] = new
    return [jnp.concatenate(p, axis=0) for p in parts]


def solve_in_place(t_ref, b_ref, pan_ref, pn_ref, px_ref, bx_ref):
    def step(k, half, final=False):
        row0 = k * PANEL
        lane0 = row0 - 128 * half
        halves = [half] if half else [0, 1]

        for h in halves:
            for m in range(8):
                pan_ref[h, m * PITCH : m * PITCH + PANEL, :] = t_ref[h, pl.ds(m * 256 + row0, PANEL), :]

        def load(h):
            return jnp.stack([pan_ref[h, pl.ds(i, 8, stride=PITCH), :] for i in range(PANEL)])

        original = [load(h) for h in halves]
        vec = b_ref[half]
        right = jnp.stack([spread(vec[None], lane0 + i)[0] for i in range(PANEL)])
        done = panel_solve(original + [right], lane0)
        for h, p in zip(halves, done):
            px_ref[h, pl.ds(row0, PANEL)] = p
            for i in range(PANEL):
                pn_ref[h, pl.ds(i, 8, stride=PITCH), :] = p[i]
        bx_ref[pl.ds(row0, PANEL)] = done[-1]
        for n, h in enumerate(halves):
            b_ref[h] = b_ref[h] - jnp.sum(original[n] * done[-1], axis=0)
        def cat(x, pick):
            pieces = split3(x)
            return jnp.concatenate([pieces[c] for c in pick], axis=0)

        def dot(a, b):
            return lax.dot_general(a, b, (((0,), (0,)), ((), ())), preferred_element_type=f32)

        left = [[cat(t_ref[h, pl.ds(m * 256 + row0, PANEL), :], (0, 0, 0, 1, 1, 2)) for h in halves] for m in range(8)]
        rgt = [[cat(pn_ref[h, m * PITCH : m * PITCH + PANEL, :], (0, 1, 2, 0, 1, 0)) for h in halves] for m in range(8)]
        for m in range(0 if half and final else 8):
            top = pl.ds(m * 256, 128)
            bottom = pl.ds(m * 256 + 128, 128)
            if half:
                t_ref[1, bottom, :] = t_ref[1, bottom, :] - dot(left[m][0], rgt[m][0])
            else:
                if not final:
                    t_ref[0, top, :] = t_ref[0, top, :] - dot(left[m][0], rgt[m][0])
                    t_ref[1, top, :] = t_ref[1, top, :] - dot(left[m][0], rgt[m][1])
                t_ref[1, bottom, :] = t_ref[1, bottom, :] - dot(left[m][1], rgt[m][1])

    for half in range(2):
        end = (half + 1) * STEPS - 1

        @pl.loop(half * STEPS, end)
        def _(k):
            step(k, half)

        step(end, half, True)

    lanes = lax.broadcasted_iota(jnp.int32, (PANEL, 8, 128), 2)
    order = lax.broadcasted_iota(jnp.int32, (PANEL, 8, 128), 0)
    zero = jnp.zeros((8, 128), f32)

    def back(k, x_halves, half):
        row0 = k * PANEL
        total = sum(px_ref[h, pl.ds(row0, PANEL)] * x_halves[h][None] for h in range(half, 2))
        x_new = bx_ref[pl.ds(row0, PANEL)] - jnp.sum(total, axis=2, keepdims=True)
        keep = jnp.where(lanes == order + (row0 - 128 * half), x_new, 0.0)
        add = jnp.sum(keep, axis=0)
        return (x_halves[0] + add, x_halves[1]) if half == 0 else (x_halves[0], x_halves[1] + add)

    x = lax.fori_loop(0, STEPS, lambda n, x: back(2 * STEPS - 1 - n, x, 1), (zero, zero), unroll=True)
    x = lax.fori_loop(0, STEPS, lambda n, x: back(STEPS - 1 - n, x, 0), x, unroll=True)
    return x


SOLVE_SCRATCH = [
    pltpu.VMEM((2, 8 * 256, 128), f32),
    pltpu.VMEM((2, 8, 128), f32),
    pltpu.VMEM((2, 8 * PITCH, 128), f32),
    pltpu.VMEM((2, 8 * PITCH, 128), f32),
    pltpu.VMEM((2, 256, 8, 128), f32),
    pltpu.VMEM((256, 8, 128), f32),
]


def scalars():
    tm = lax.axis_index("tm")
    stn = lax.axis_index("stn")
    return jnp.stack([lax.rem(tm, 2), stn, tm * 4 + stn]).astype(jnp.int32)


def column(row):
    return jnp.broadcast_to(row, (128, 128)).T


def quarter_rows(rows, quarter):
    out = rows[0:4]
    for q in range(1, 4):
        out = jnp.where(quarter == q, rows[4 * q : 4 * q + 4], out)
    return out


def prepare_kernel(at, transfer, site, weight, mask, readings, design, own, msg1, msg2, msg3):
    core, stn = at[0], at[1]
    for c in range(3):
        rows = pl.ds(128 * c, 128)
        root = column(jnp.sqrt(weight[:, 128 * c : 128 * c + 128]))
        where_site = column(site[:, 128 * c : 128 * c + 128].astype(f32))
        for h in range(2):
            pole = lax.broadcasted_iota(jnp.int32, (128, 128), 1).astype(f32) + 128.0 * h
            near = jnp.where(pole == where_site, near_gain, 0.0)
            design[rows, 128 * h : 128 * h + 128] = (transfer[rows, 128 * h : 128 * h + 128] + near) * root
    half = design[pl.ds(192 * core, 192), :]
    masks = mask[...].astype(f32)
    scaled = masks * jnp.sqrt(weight[...]) * readings[...]

    def piece(quarter):
        return jnp.concatenate([quarter_rows(masks, quarter), quarter_rows(scaled, quarter)], axis=0)

    own[0:16, :] = masks
    own[16:32, :] = scaled
    for o, msg in enumerate((msg1, msg2, msg3)):
        rows = piece(lax.rem(stn + (o + 1), 4))
        msg[0:192, :] = half
        msg[192:200, :] = rows[:, 0:256]
        msg[200:208, 0:128] = rows[:, 256:384]
        msg[200:208, 128:256] = jnp.zeros((8, 128), f32)


def decay(forget, quarter):
    rows = quarter_rows(forget, quarter)
    row = [[rows[t : t + 1, 128 * h : 128 * h + 128] for h in range(2)] for t in range(4)]
    col = [[column(row[t][h]) for h in range(2)] for t in range(4)]
    return row, col


BLOCKS = ((0, 0), (0, 1), (1, 1))


def products(x, keeps, extra=None):
    high, mid, low = split3(x)
    turned = x.T
    thigh = turned.astype(bf16)
    tmid = (turned - thigh.astype(f32)).astype(bf16)
    right = jnp.concatenate([high, mid], axis=0), jnp.concatenate([mid, low], axis=0)

    def four(q):
        out = [], []
        for t in range(4):
            keep = keeps[4 * q + t : 4 * q + t + 1, :].astype(bf16)
            a, b = thigh * keep, tmid * keep
            for n, left in enumerate((jnp.concatenate([a, b], axis=1), jnp.concatenate([a, a], axis=1))):
                if t == 3 and extra is not None:
                    left = jnp.concatenate([left, extra[n]], axis=0)
                out[n].append(jnp.dot(left, right[n], preferred_element_type=f32))
        return out

    return four


def add_block(x, rows, even, odd, info, first, fresh=False):
    high, mid, low = (p.astype(f32) for p in split3(rows[4:8, :]))
    blank = jnp.zeros((4, 384), f32)

    def chunk(*quarters):
        return jnp.concatenate(quarters, axis=0).astype(bf16)

    top = chunk(high, blank, blank, blank)
    extra = (
        jnp.concatenate([chunk(high, mid, low, blank), chunk(mid, blank, blank, blank)], axis=1),
        jnp.concatenate([top, top], axis=1),
    )
    same, cross = products(x, rows, extra)(0)
    tail, cross_tail = same[3][256:272], cross[3][256:272]
    part = tail[0:4] + tail[4:8] + tail[8:12] + cross_tail[0:4]
    info[4:8, :] = part if first else info[4:8, :] + part
    for t in range(4):
        even[t] = same[t][0:256] if first or fresh else even[t] + same[t][0:256]
        odd[t] = cross[t][0:256] if first or fresh else odd[t] + cross[t][0:256]


def gram_block(even, odd, t, n):
    i, j = BLOCKS[n]
    rs, cs = slice(128 * i, 128 * i + 128), slice(128 * j, 128 * j + 128)
    return even[t, rs, cs] + (odd[t, rs, cs] + odd[t, cs, rs].T)


def part_of(message, n):
    return message.at[pl.ds(n, 128, stride=5), :]


def pack(ahead, behind, vec_f, vec_b):
    lanes = lax.broadcasted_iota(jnp.int32, (128, 128), 1)
    rows_at = lax.broadcasted_iota(jnp.int32, (128, 128), 0)
    eye = lanes == rows_at
    lower = lanes <= rows_at
    last = jnp.zeros((128, 128), f32)
    for n, e in enumerate([ahead[1, 1], behind[1, 1], vec_f[0], vec_f[1], vec_b[0], vec_b[1]]):
        last = jnp.where(lanes == n, jnp.sum(jnp.where(eye, e, 0.0), axis=1, keepdims=True), last)
    return (
        (jnp.where(lower, ahead[0, 0], ahead[1, 1]), ahead[0, 1]),
        (jnp.where(lower, behind[0, 0], behind[1, 1]), behind[0, 1]),
        last,
    )


def block_kernel(at, design, own, forget, msg, infos, ahead, behind):
    stn = at[1]
    x = design[...]
    four = products(x, own)
    infos[...] = jnp.dot(own[16:32, :], x, precision=lax.Precision.HIGHEST, preferred_element_type=f32)
    all_row, all_col = None, None
    vec_f, vec_b = [None, None], [None, None]
    for t in range(16):
        if t % 4 == 0:
            all_same, all_cross = four(t // 4)
        same, cross = all_same[t % 4], all_cross[t % 4]
        row = [forget[t : t + 1, 128 * h : 128 * h + 128] for h in range(2)]
        col = [column(r) for r in row]
        all_row = row if t == 0 else [p * q for p, q in zip(all_row, row)]
        all_col = col if t == 0 else [p * q for p, q in zip(all_col, col)]
        for n, (i, j) in enumerate(BLOCKS):
            rs, cs = slice(128 * i, 128 * i + 128), slice(128 * j, 128 * j + 128)
            g = same[rs, cs] + (cross[rs, cs] + cross[cs, rs].T)
            past = (all_col[i] * all_row[j]) * g
            if t == 0:
                ahead[n] = g
                behind[n] = past
            else:
                ahead[n] = (col[i] * row[j]) * ahead[n] + g
                behind[n] += past
        for h in range(2):
            v = infos[t : t + 1, 128 * h : 128 * h + 128]
            vec_f[h] = v if t == 0 else row[h] * vec_f[h] + v
            vec_b[h] = all_row[h] * v if t == 0 else vec_b[h] + all_row[h] * v
    f, b, last = pack(
        {k: ahead[n] for n, k in enumerate(BLOCKS)}, {k: behind[n] for n, k in enumerate(BLOCKS)}, vec_f, vec_b
    )
    wide = [jnp.broadcast_to(r, (128, 128)) for r in all_row]
    share = jnp.where(stn == 1, wide[0], wide[1])
    turned_share = pltpu.roll(jnp.where(stn == 0, wide[0], wide[1]), 64, 1)
    share = jnp.where((stn == 0) | (stn == 2), turned_share, share)
    lanes = lax.broadcasted_iota(jnp.int32, (128, 128), 1)
    for n, part in enumerate((*f, *b, jnp.where(lanes < 64, last, share))):
        part_of(msg, n)[...] = part


def early_gram_kernel(at, design, own, gram, info, even, odd):
    stn = at[1]
    info[0:4, :] = jnp.zeros((4, 256), f32)
    rows = jnp.concatenate([quarter_rows(own[0:16, :], stn), quarter_rows(own[16:32, :], stn)], axis=0)
    add_block(design[...], rows, even, odd, info, True)
    for t in range(4):
        for n in range(3):
            gram[t, n] = gram_block(even, odd, t, n)


def gram_kernel(
    at, gram_in, info_in, got1, got2, got3, oth1, oth2, oth3, forget, gram, info, msg1, msg2, msg3, block, even, odd
):
    core, stn = at[0], at[1]
    info[...] = info_in[...]
    for n, (got, oth) in enumerate(((got1, oth1), (got3, oth3), (got2, oth2))):
        block[n, pl.ds(192 * core, 192), :] = got[0:192, :]
        block[n, pl.ds(192 * (1 - core), 192), :] = oth[0:192, :]
        rows = jnp.concatenate([got[192:200, :], got[200:208, 0:128]], axis=1)
        add_block(block[n], rows, even, odd, info, False, n == 0)
    for t in range(4):
        for n in range(3):
            gram[t, n] = gram_in[t, n] + gram_block(even, odd, t, n)
    row, col = decay(forget[...], stn)
    ahead, behind = {}, {}
    for n, (i, j) in enumerate(BLOCKS):
        g = [gram[t, n] for t in range(4)]
        f = [col[t][i] * row[t][j] for t in range(4)]
        acc = g[0]
        for t in range(1, 4):
            acc = f[t] * acc + g[t]
        ahead[i, j] = acc
        acc = f[3] * g[3]
        for t in (2, 1, 0):
            acc = f[t] * (acc + g[t])
        behind[i, j] = acc
    vec_f, vec_b = [], []
    for h in range(2):
        v = [info[4 + t : 5 + t, 128 * h : 128 * h + 128] for t in range(4)]
        f = [row[t][h] for t in range(4)]
        acc = v[0]
        for t in range(1, 4):
            acc = f[t] * acc + v[t]
        vec_f.append(acc)
        acc = f[3] * v[3]
        for t in (2, 1, 0):
            acc = f[t] * (acc + v[t])
        vec_b.append(acc)
    lanes = lax.broadcasted_iota(jnp.int32, (128, 128), 1)
    rows_at = lax.broadcasted_iota(jnp.int32, (128, 128), 0)
    edge = lax.broadcasted_iota(jnp.int32, (8, 128), 0)

    def rows_of(blocks, vec):
        diagonal = jnp.sum(jnp.where(lanes == rows_at, blocks[1, 1], 0.0), axis=0, keepdims=True)
        return (
            jnp.where(lanes <= rows_at, blocks[0, 0], blocks[1, 1]),
            blocks[0, 1],
            jnp.where(edge == 0, vec[0], jnp.where(edge == 1, diagonal, 0.0)),
            jnp.where(edge == 0, vec[1], 0.0),
        )

    f, b = rows_of(ahead, vec_f), rows_of(behind, vec_b)
    for o, msg in enumerate((msg1, msg2, msg3)):
        later = lax.rem(stn + (o + 1), 4) > stn
        for n in range(4):
            rows = slice(128, 136) if n >= 2 else slice(0, 128)
            msg[rows, 128 * (n % 2) : 128 * (n % 2) + 128] = jnp.where(later, f[n], b[n])


def shifted(x, n, fill, up):
    edge = jnp.full((n, x.shape[1]), fill, f32)
    if up:
        return jnp.concatenate([x[n:], edge], axis=0)
    return jnp.concatenate([edge, x[:-n]], axis=0)


def running(gain, value, up):
    n = 1
    while n < 32:
        value = value + gain * shifted(value, n, 0.0, up)
        if n < 16:
            gain = gain * shifted(gain, n, 1.0, up)
        n *= 2
    return shifted(value, 1, 0.0, up)


def carry_kernel(at, got, token, out):
    place = at[2]
    lanes = lax.broadcasted_iota(jnp.int32, (32, 128), 1)

    def rows(n, quarter):
        return pl.ds(5 * quarter + n, 32, stride=20)

    lasts = [got[rows(4, q), :] for q in range(4)]
    low = jnp.where(lanes < 64, pltpu.roll(lasts[0], 64, 1), lasts[1])
    high = jnp.where(lanes < 64, pltpu.roll(lasts[2], 64, 1), lasts[3])
    here = lanes == place
    at_low = jnp.sum(jnp.where(here, low, 0.0), axis=1, keepdims=True)
    at_high = jnp.sum(jnp.where(here, high, 0.0), axis=1, keepdims=True)
    extra = jnp.where(lanes < 2, at_high * at_high, jnp.where((lanes == 2) | (lanes == 4), at_low, at_high))
    gain = [jnp.where(lanes <= place, at_low * low, at_high * high), at_low * high, extra]

    def total(n):
        return (got[rows(n, 0), :] + got[rows(n, 1), :]) + (got[rows(n, 2), :] + got[rows(n, 3), :])

    last = jnp.where(lanes < 6, (lasts[0] + lasts[1]) + (lasts[2] + lasts[3]), 0.0)
    enter = [running(g, v, False) for g, v in zip(gain, (total(0), total(1), last))]
    leave = [running(g, v, True) for g, v in zip(gain, (total(2), total(3), last))]
    ahead_lane = (lanes == 0) | (lanes == 2) | (lanes == 3)
    parts = (enter[0], enter[1], leave[0], leave[1], jnp.where(ahead_lane, enter[2], leave[2]))
    for n, part in enumerate(parts):
        for q in range(4):
            out[rows(n, q), :] = part


def final_kernel(
    at, got, quarter1, quarter2, quarter3, gram, info, forget, filtered, smoothed, quarters,
    t_ref, b_ref, pan_ref, pn_ref, px_ref, bx_ref,
):
    stn = at[1]
    lanes = lax.broadcasted_iota(jnp.int32, (128, 128), 1)
    rows_at = lax.broadcasted_iota(jnp.int32, (128, 128), 0)
    eye = lanes == rows_at
    lower = lanes <= rows_at
    unit = jnp.where(eye, ridge, 0.0)
    for o, quarter in enumerate((quarter1, quarter2, quarter3)):
        quarters[lax.rem(stn + (3 - o), 4)] = quarter[...]
    got = [part_of(got, n)[...] for n in range(5)]
    last = got[4]

    def lane_row(n):
        col = jnp.sum(jnp.where(lanes == n, last, 0.0), axis=1, keepdims=True)
        return jnp.sum(jnp.where(eye, col, 0.0), axis=0, keepdims=True)

    first = [got[0], got[1], lane_row(2), lane_row(3), lane_row(0)]
    second = [got[2], got[3], lane_row(4), lane_row(5), lane_row(1)]

    def quarter_gains(q):
        gain = forget[4 * q : 4 * q + 1, :]
        for t in range(1, 4):
            gain = gain * forget[4 * q + t : 4 * q + t + 1, :]
        low, high = gain[:, 0:128], gain[:, 128:256]
        clow, chigh = column(low), column(high)
        return (jnp.where(lower, clow * low, chigh * high), clow * high, low, high, high * high)

    all_gains = [quarter_gains(q) for q in range(4)]

    def past_quarter(q, state, use):
        gains = all_gains[q]
        own = (
            quarters[q, 0:128, 0:128],
            quarters[q, 0:128, 128:256],
            quarters[q, 128:129, 0:128],
            quarters[q, 128:129, 128:256],
            quarters[q, 129:130, 0:128],
        )
        return [jnp.where(use, g * v + w, v) for g, v, w in zip(gains, state, own)]

    for q in (0, 1, 2):
        first = past_quarter(q, first, q < stn)
    for q in (3, 2, 1):
        second = past_quarter(q, second, q > stn)

    def unpack(state):
        packed = state[0]
        turned = packed.T
        one = jnp.where(lower, packed, turned)
        two = jnp.where(eye, state[4], jnp.where(lower, turned, packed))
        return {(0, 0): one, (0, 1): state[1], (1, 1): two}

    ahead = unpack(first)
    behind = unpack(second)
    row, col = decay(forget[...], stn)
    for n, (i, j) in enumerate(BLOCKS):
        f = [col[t][i] * row[t][j] for t in range(4)]
        acc = ahead[i, j]
        held = []
        for t in range(4):
            acc = f[t] * acc + gram[t, n]
            full = acc + unit if i == j else acc
            held.append(full)
            t_ref[j, 256 * t + 128 * i : 256 * t + 128 * i + 128, :] = full
        acc = behind[i, j]
        for t in (3, 2, 1, 0):
            at_row = 256 * (4 + t) + 128 * i
            t_ref[j, at_row : at_row + 128, :] = held[t] + acc
            if t:
                acc = f[t] * (acc + gram[t, n])
    for h in range(2):
        vec = first[2 + h]
        held = []
        for t in range(4):
            vec = row[t][h] * vec + info[4 + t : 5 + t, 128 * h : 128 * h + 128]
            held.append(vec)
        vec = second[2 + h]
        both = [None] * 4
        for t in (3, 2, 1, 0):
            both[t] = held[t] + vec
            if t:
                vec = row[t][h] * (vec + info[4 + t : 5 + t, 128 * h : 128 * h + 128])
        b_ref[h] = jnp.concatenate(held + both, axis=0)
    x = solve_in_place(t_ref, b_ref, pan_ref, pn_ref, px_ref, bx_ref)
    for h in range(2):
        filtered[:, 128 * h : 128 * h + 128] = x[h][0:4]
        smoothed[:, 128 * h : 128 * h + 128] = x[h][4:8]


def call(kernel, outs, scratch, operands, flops=1e6, away=()):
    return pl.pallas_call(
        kernel,
        out_shape=[jax.ShapeDtypeStruct(s, f32) for s in outs],
        in_specs=[pl.BlockSpec(memory_space=pltpu.SMEM)]
        + [pl.BlockSpec(memory_space=pl.ANY if n in away else pltpu.VMEM) for n in range(1, len(operands))],
        out_specs=[pl.BlockSpec(memory_space=pltpu.VMEM)] * len(outs),
        scratch_shapes=scratch,
        compiler_params=pltpu.CompilerParams(vmem_limit_bytes=VMEM),
        cost_estimate=pl.CostEstimate(flops=int(flops), bytes_accessed=1 << 20, transcendentals=0),
    )(*operands)


def ring(count, shift):
    return [(i, (i + shift) % count) for i in range(count)]


SWAP = [(i, i ^ 1) for i in range(32)]


def exchange(message):
    out = lax.all_to_all(message.reshape(128, 1, 640), ("tm", "stn"), 0, 0, tiled=True)
    return out.reshape(640, 128)


def body(readings, gap_mask, transfer, channel_weight, pole_site, forget):
    at = scalars()
    parts = [pltpu.VMEM((4, 256, 256), f32)] * 2
    with jax.named_scope("design"):
        design, own, *msgs = call(
            prepare_kernel,
            [(384, 256), (32, 384)] + [(208, 256)] * 3,
            [],
            (at, transfer, pole_site[None], channel_weight[None], gap_mask, readings),
        )
    with jax.named_scope("gather"):
        got = [lax.ppermute(m, "stn", ring(4, o + 1)) for o, m in enumerate(msgs)]
    with jax.named_scope("block"):
        (totals,) = call(
            block_kernel,
            [(640, 128)],
            [
                pltpu.VMEM((16, 256), f32),
                pltpu.VMEM((3, 128, 128), f32),
                pltpu.VMEM((3, 128, 128), f32),
            ],
            (at, design, own, forget),
            6e9,
        )
    with jax.named_scope("carry"):
        mine = exchange(totals)
    with jax.named_scope("swap"):
        other = [lax.ppermute(g, "tm", SWAP) for g in got]
    with jax.named_scope("early_gram"):
        gram, info = call(early_gram_kernel, [(4, 3, 128, 128), (8, 256)], parts, (at, design, own), 2e10)
    with jax.named_scope("gram"):
        gram, info, *totals = call(
            gram_kernel,
            [(4, 3, 128, 128), (8, 256)] + [(136, 256)] * 3,
            [pltpu.VMEM((3, 384, 256), f32)] + parts,
            (at, gram, info, *got, *other, forget),
            2e9,
        )
    with jax.named_scope("token"):
        token = lax.ppermute(info, "tm", SWAP)
    with jax.named_scope("quarters"):
        quarters = [lax.ppermute(m, "stn", ring(4, o + 1)) for o, m in enumerate(totals)]
    with jax.named_scope("carry"):
        (entering,) = call(carry_kernel, [(640, 128)], [], (at, mine, token), away=(2,))
        entering = exchange(entering)
    with jax.named_scope("solve"):
        filtered, smoothed = call(
            final_kernel,
            [(4, 256)] * 2,
            [pltpu.VMEM((4, 136, 256), f32)] + SOLVE_SCRATCH,
            (at, entering, *quarters, gram, info, forget),
        )
    return (filtered, smoothed)


def solution(mesh):
    in_specs = (P("tm", "stn"), P("tm", "stn"), P("stn", None), P("stn"), P("stn"), P("tm", None))
    out_specs = (P(("tm", "stn"), None), P(("tm", "stn"), None))
    return jax.shard_map(body, mesh=mesh, in_specs=in_specs, out_specs=out_specs, check_vma=False)
```
